32 devices in a mesh: fsdp: 4 (over y, x), ctx: 4 (over z), tp: 2 (over core).
Axes of the slice: x: 2, y: 2, z: 4, core: 2. Of those that a mesh axis runs over, the one named last changes fastest.
Arguments:
- hidden: bfloat16 [4, 2048, 1024], P('fsdp', 'ctx'), may hold values from -6 to 6
- teacher: bfloat16 [4, 2048, 1024], P('fsdp', 'ctx'), may hold values from -6 to 6
- positions: int32 [4, 2048], P('fsdp', 'ctx'), may hold values from 0 to 2047, as said below
- valid_mask: int32 [4, 2048], P('fsdp', 'ctx'), may hold values from 0 to 1, as said below
- norm_gain: bfloat16 [1024], P(('fsdp', 'ctx')), may hold values from 0.5 to 1.5
- w_query: bfloat16 [1024, 512], P(('fsdp', 'ctx'), 'tp'), may hold values from -0.1875 to 0.1875
- key_value_weight: bfloat16 [1024, 2, 128], P(('fsdp', 'ctx'), None, 'tp'), may hold values from -0.1875 to 0.1875
- w_gatein: bfloat16 [1024, 2, 1536], P(('fsdp', 'ctx'), None, 'tp'), may hold values from -0.1875 to 0.1875
- w_bc: bfloat16 [1024, 256], P(('fsdp', 'ctx')), may hold values from -0.1875 to 0.1875
- w_step: bfloat16 [1024, 24], P(('fsdp', 'ctx'), 'tp'), may hold values from -0.1875 to 0.1875
- ssm_gain: bfloat16 [1536], P(('tp', 'fsdp', 'ctx')), may hold values from 0.5 to 1.5
- mlp_gain: bfloat16 [1024], P(('fsdp', 'ctx')), may hold values from 0.5 to 1.5
- w_gateup: bfloat16 [1024, 2, 2048], P(('fsdp', 'ctx'), None, 'tp'), may hold values from -0.1875 to 0.1875
- w_out_attn: bfloat16 [512, 1024], P('tp', ('fsdp', 'ctx')), may hold values from -1 to 1
- w_out_ssm: bfloat16 [1536, 1024], P('tp', ('fsdp', 'ctx')), may hold values from -0.15625 to 0.15625
- w_down: bfloat16 [2048, 1024], P('tp', ('fsdp', 'ctx')), may hold values from -0.125 to 0.125
- conv_inner: bfloat16 [4, 1536], P(None, ('tp', 'fsdp', 'ctx')), may hold values from -3 to 3
- conv_bc: bfloat16 [4, 256], P(None, ('fsdp', 'ctx')), may hold values from -3 to 3
- head_params: float32 [3, 24], P(None, 'tp'), may hold values from -5.3 to 1.5, as said below
Outputs:
- out: bfloat16 [4, 2048, 1024], P('fsdp', 'ctx')
- loss: float32 [], replicated
- grad_hidden: float32 [4, 2048, 1024], P('fsdp', 'ctx')
- grad_norm_gain: float32 [1024], P(('fsdp', 'ctx'))
- grad_w_query: float32 [1024, 512], P(('fsdp', 'ctx'), 'tp')
- grad_w_keyval: float32 [1024, 2, 128], P(('fsdp', 'ctx'), None, 'tp')
- grad_w_gatein: float32 [1024, 2, 1536], P(('fsdp', 'ctx'), None, 'tp')
- grad_w_bc: float32 [1024, 256], P(('fsdp', 'ctx'))
- grad_w_step: float32 [1024, 24], P(('fsdp', 'ctx'), 'tp')
- grad_ssm_gain: float32 [1536], P(('tp', 'fsdp', 'ctx'))
- grad_mlp_gain: float32 [1024], P(('fsdp', 'ctx'))
- grad_w_gateup: float32 [1024, 2, 2048], P(('fsdp', 'ctx'), None, 'tp')
- grad_w_out_attn: float32 [512, 1024], P('tp', ('fsdp', 'ctx'))
- grad_w_out_ssm: float32 [1536, 1024], P('tp', ('fsdp', 'ctx'))
- grad_w_down: float32 [2048, 1024], P('tp', ('fsdp', 'ctx'))
- grad_conv_inner: float32 [4, 1536], P(None, ('tp', 'fsdp', 'ctx'))
- grad_conv_bc: float32 [4, 256], P(None, ('fsdp', 'ctx'))
- grad_head_params: float32 [3, 24], P(None, 'tp')
The draws below stay inside these ranges and needn't reach their ends.
Inputs may be any that keep to these rules, and one draw needn't show every extreme that they name: `positions`: each row is a run of documents, padding (if any) being its last one; a position is a token's offset in its document, 0 at a document's first token and one more than the token before elsewhere; row 0 is one document of 2048 tokens. `valid_mask`: 1 before a row's padding and 0 on it; row 0 has no padding, the last row has some. `head_params`: row 0 holds a head's step bias, row 1 the logarithm of its decay rate, row 2 its skip weight.
All inputs are finite; a program needn't handle non-finite values.
Results may differ from the reference program's by a relative error of at most 0.012.
Values may be sent and summed in bfloat16 or wider, within the bound.
No kernel may reach another device: no remote copies, remote signals or barrier semaphores. Data moves between devices by JAX's collectives and lax.ppermute only.
A program may use at most 192 MiB of HBM per device.

```python
import jax
import jax.numpy as jnp
from jax import lax

MODEL_WIDTH = 1024
QUERY_HEAD_COUNT = 8
KEY_VALUE_HEADS = 2
HEAD_SIZE = 64
HS = 24
DS = 128
KC = 4
FF = 2048
ROW_LENGTH = 2048
ROWS = 4


def layout_rows(key):
    base_key = jax.random.fold_in(key, 4242)
    rate_key, start_key, pad_key = jax.random.split(base_key, 3)
    offsets = jnp.arange(ROW_LENGTH, dtype=jnp.int32)
    row_ids = jnp.arange(ROWS, dtype=jnp.int32)
    rate_pick = jax.random.randint(rate_key, (ROWS,), 0, 4, dtype=jnp.int32)
    spacing = jnp.left_shift(jnp.full((ROWS,), 16, jnp.int32), 3 * rate_pick)
    raw_draws = jax.random.randint(start_key, (ROWS, ROW_LENGTH), 0, 1 << 20, dtype=jnp.int32)
    starts = raw_draws % spacing[:, None] == 0
    padding = jax.random.randint(pad_key, (ROWS,), 0, ROW_LENGTH // 8 + 1, dtype=jnp.int32)
    padding = jnp.where(row_ids == 0, 0, padding)
    padding = jnp.where(row_ids == ROWS - 1, jnp.maximum(padding, 1), padding)
    starts = jnp.where(row_ids[:, None] == 0, False, starts)
    boundary = ROW_LENGTH - padding
    starts = starts | (offsets[None, :] == 0) | (offsets[None, :] == boundary[:, None])
    last_start = lax.cummax(jnp.where(starts, offsets[None, :], 0), axis=1)
    token_placements = offsets[None, :] - last_start
    live_rows = (offsets[None, :] < boundary[:, None]).astype(jnp.int32)
    return (token_placements, live_rows)


def draw_positions(key, part):
    return layout_rows(key)[0]


def draw_valid_mask(key, part):
    return layout_rows(key)[1]


def draw_head_params(key, part):
    bias_key, rate_key, skip_key = jax.random.split(jax.random.fold_in(key, 77), 3)
    step_bias = jax.random.uniform(bias_key, (HS,), jnp.float32, -5.0, -3.0)
    log_rates = jax.random.uniform(rate_key, (HS,), jnp.float32, -3.9, 1.4)
    skip_weight = jax.random.uniform(skip_key, (HS,), jnp.float32, 0.5, 1.5)
    return jnp.stack([step_bias, log_rates, skip_weight])


def steps_of(own_key, extent, cuts, smallest, largest):
    factor_of = 1.0
    for axis_at, parts in cuts:
        draws = jax.random.uniform(jax.random.fold_in(jax.random.fold_in(own_key, 6), axis_at), (parts,), jnp.float32, smallest / len(cuts), largest / len(cuts))
        factor_of = factor_of * jnp.repeat(jnp.exp(draws), extent[axis_at] // parts).reshape((-1,) + (1,) * (len(extent) - 1 - axis_at))
    return factor_of


def scatter_about(stream_key, dims, deviation, bound, pieces=(), kind=jnp.bfloat16):
    level = steps_of(stream_key, dims, pieces, -0.22, 0.18) if pieces else 1.0
    drawn = jax.random.normal(stream_key, dims, jnp.float32) * deviation * level
    return jnp.minimum(jnp.maximum(drawn, -bound), bound).astype(kind)


def setup_inputs(seed: int = 0) -> dict:
    streams_of = jax.random.split(jax.random.key(seed), 20)
    return {
        "hidden": scatter_about(streams_of[0], (ROWS, ROW_LENGTH, MODEL_WIDTH), 1.0, 6.0, ((0, 4), (1, 4))),
        "teacher": scatter_about(streams_of[1], (ROWS, ROW_LENGTH, MODEL_WIDTH), 1.0, 6.0, ((0, 4), (1, 4))),
        "positions": draw_positions(jax.random.fold_in(streams_of[19], 71), 0),
        "valid_mask": draw_valid_mask(jax.random.fold_in(streams_of[19], 71), 0),
        "norm_gain": jnp.clip(1.0 + 0.1 * jax.random.normal(streams_of[4], (MODEL_WIDTH,), jnp.float32), 0.5, 1.5).astype(jnp.bfloat16),
        "w_query": scatter_about(streams_of[5], (MODEL_WIDTH, QUERY_HEAD_COUNT * HEAD_SIZE), MODEL_WIDTH ** -0.5, 0.1875, ((0, 16), (1, 2))),
        "key_value_weight": scatter_about(streams_of[6], (MODEL_WIDTH, 2, KEY_VALUE_HEADS * HEAD_SIZE), MODEL_WIDTH ** -0.5, 0.1875, ((0, 16), (2, 2))),
        "w_gatein": scatter_about(streams_of[7], (MODEL_WIDTH, 2, HS * HEAD_SIZE), MODEL_WIDTH ** -0.5, 0.1875, ((0, 16), (2, 2))),
        "w_bc": scatter_about(streams_of[8], (MODEL_WIDTH, 2 * DS), MODEL_WIDTH ** -0.5, 0.1875, ((0, 16),)),
        "w_step": scatter_about(streams_of[9], (MODEL_WIDTH, HS), MODEL_WIDTH ** -0.5, 0.1875, ((0, 16), (1, 2))),
        "ssm_gain": jnp.clip(1.0 + 0.1 * jax.random.normal(streams_of[10], (HS * HEAD_SIZE,), jnp.float32), 0.5, 1.5).astype(jnp.bfloat16),
        "mlp_gain": jnp.clip(1.0 + 0.1 * jax.random.normal(streams_of[11], (MODEL_WIDTH,), jnp.float32), 0.5, 1.5).astype(jnp.bfloat16),
        "w_gateup": scatter_about(streams_of[12], (MODEL_WIDTH, 2, FF), MODEL_WIDTH ** -0.5, 0.1875, ((0, 16), (2, 2))),
        "w_out_attn": scatter_about(streams_of[13], (QUERY_HEAD_COUNT * HEAD_SIZE, MODEL_WIDTH), (QUERY_HEAD_COUNT * HEAD_SIZE // 16) ** -0.5, 1.0, ((0, 2), (1, 16))),
        "w_out_ssm": scatter_about(streams_of[14], (HS * HEAD_SIZE, MODEL_WIDTH), (HS * HEAD_SIZE) ** -0.5, 0.15625, ((0, 2), (1, 16))),
        "w_down": scatter_about(streams_of[15], (FF, MODEL_WIDTH), FF ** -0.5, 0.125, ((0, 2), (1, 16))),
        "conv_inner": scatter_about(streams_of[16], (KC, HS * HEAD_SIZE), 0.5, 3.0, ((1, 32),)),
        "conv_bc": scatter_about(streams_of[17], (KC, 2 * DS), 0.5, 3.0, ((1, 16),)),
        "head_params": draw_head_params(jax.random.fold_in(streams_of[19], 71), 0),
    }


@jax.custom_vjp
def lower_precision(v):
    return lax.optimization_barrier(v.astype(jnp.bfloat16)).astype(jnp.float32)

@jax.custom_vjp
def lower_precision_backward(v):
    return v

def low_keep(v):
    return (lower_precision(v), None)

def low_pass(kept, grad):
    return (grad,)

def back_keep(v):
    return (v, None)

def back_low(kept, grad):
    return (lower_precision(grad),)
lower_precision.defvjp(low_keep, low_pass)
lower_precision_backward.defvjp(back_keep, back_low)
eps = 1e-05
rope_base = 100000000000.0
highest = lax.Precision.HIGHEST
masked_score = -1e+30

def product_full_precision(left_matrix, right_matrix):
    return jnp.dot(left_matrix, right_matrix, precision=highest)

def rms_scale(values):
    return lax.rsqrt(lax.optimization_barrier(jnp.mean(values * values, axis=-1, keepdims=True)) + eps)

def apply_rotary(values, token_placements, direction):
    half_width = values.shape[-1] // 2
    frequency = rope_base ** (-2.0 * jnp.arange(half_width, dtype=jnp.float32) / values.shape[-1])
    angle_table = token_placements.astype(jnp.float32)[..., None] * frequency
    cosine = jnp.cos(angle_table)[..., None, :]
    sine_table = direction * jnp.sin(angle_table)[..., None, :]
    first_half = values[..., :half_width]
    second_half = values[..., half_width:]
    return jnp.concatenate([first_half * cosine - second_half * sine_table, second_half * cosine + first_half * sine_table], axis=-1)

def convolve(extended, conv_taps, token_placements):
    kernel_width = conv_taps.shape[0]
    seq_length = token_placements.shape[1]
    summed = jnp.zeros((extended.shape[0], seq_length, extended.shape[2]), jnp.float32)
    for lag_index in range(kernel_width):
        distance = kernel_width - 1 - lag_index
        usable = (token_placements >= distance).astype(jnp.float32)[..., None]
        summed = summed + conv_taps[lag_index] * extended[:, lag_index:lag_index + seq_length, :] * usable
    return jax.nn.silu(summed)

def mixer_setup(step_raw, head_table, token_placements):
    step_size = jax.nn.softplus(step_raw + head_table[0])
    log_decay = step_size * -jnp.exp(head_table[1])
    cumulative = jnp.cumsum(log_decay, axis=1)
    offsets = jnp.arange(step_raw.shape[1], dtype=jnp.int32)
    doc_starts = offsets[None, :] - token_placements
    return (step_size, cumulative, offsets, doc_starts)

def mixer_output(inner_values, step_raw, input_basis, output_basis, head_table, state_in, token_placements):
    step_size, cumulative, offsets, doc_starts = mixer_setup(step_raw, head_table, token_placements)
    allowed = (offsets[None, None, :] <= offsets[None, :, None]) & (offsets[None, None, :] >= doc_starts[:, :, None])
    allowed = allowed[..., None]
    spread = cumulative[:, :, None, :] - cumulative[:, None, :, :]
    decay_table = jnp.where(allowed, jnp.exp(jnp.where(allowed, spread, 0.0)), 0.0)
    basis_match = jnp.einsum('rtn,rsn->rts', output_basis, input_basis, precision=highest)
    mixing = decay_table * basis_match[..., None] * step_size[:, None, :, :]
    result = jnp.einsum('rtsh,rshp->rthp', mixing, inner_values, precision=highest)
    carried = (token_placements > offsets[None, :]).astype(jnp.float32)
    entry_decay = jnp.exp(cumulative) * carried[..., None]
    result = result + jnp.einsum('rtn,rhpn->rthp', output_basis, state_in, precision=highest) * entry_decay[..., None]
    return result + head_table[2][None, None, :, None] * inner_values

def mixer_summary(inner_values, step_raw, input_basis, head_table, token_placements):
    step_size, cumulative, offsets, doc_starts = mixer_setup(step_raw, head_table, token_placements)
    last_index = step_raw.shape[1] - 1
    reaches_end = (offsets[None, :] >= doc_starts[:, -1:]).astype(jnp.float32)
    to_end = jnp.exp(cumulative[:, -1:, :] - cumulative) * reaches_end[..., None] * step_size
    summary = jnp.einsum('rsh,rshp,rsn->rhpn', to_end, inner_values, input_basis, precision=highest)
    passing = jnp.exp(cumulative[:, -1, :]) * (token_placements[:, -1:] > last_index).astype(jnp.float32)
    return (passing, summary)

def layer_row(params_in, inputs, targets, token_placements, live_rows):
    norm_gain, w_query, key_value_weight, w_gatein, w_bc, w_step, ssm_gain, mlp_gain, w_gateup, w_out_attn, w_out_ssm, w_down, conv_inner, conv_bc, head_params = params_in
    normalized_input = lower_precision(inputs * rms_scale(inputs) * norm_gain)
    query_lin = lower_precision_backward(product_full_precision(normalized_input, w_query))
    key_value_linear = lower_precision_backward(product_full_precision(normalized_input, key_value_weight.reshape(MODEL_WIDTH, 2 * KEY_VALUE_HEADS * HEAD_SIZE)))
    gatein_lin = lower_precision_backward(product_full_precision(normalized_input, w_gatein.reshape(MODEL_WIDTH, 2 * HS * HEAD_SIZE)))
    bc_lin = lower_precision_backward(product_full_precision(normalized_input, w_bc))
    step_lin = lower_precision_backward(product_full_precision(normalized_input, w_step))
    query_rotary = lower_precision(apply_rotary(query_lin.reshape(1, ROW_LENGTH, QUERY_HEAD_COUNT, HEAD_SIZE), token_placements, 1.0))
    every_key_row = lower_precision(apply_rotary(key_value_linear[:, :KEY_VALUE_HEADS * HEAD_SIZE].reshape(1, ROW_LENGTH, KEY_VALUE_HEADS, HEAD_SIZE), token_placements, 1.0))[0]
    every_value_row = lower_precision(key_value_linear[:, KEY_VALUE_HEADS * HEAD_SIZE:].reshape(ROW_LENGTH, KEY_VALUE_HEADS, HEAD_SIZE))
    rows_per_block = min(512, ROW_LENGTH)
    number_of_blocks = ROW_LENGTH // rows_per_block
    blocked_queries = query_rotary.reshape(number_of_blocks, rows_per_block, KEY_VALUE_HEADS, QUERY_HEAD_COUNT // KEY_VALUE_HEADS, HEAD_SIZE)
    index_blocks = jnp.arange(ROW_LENGTH, dtype=jnp.int32).reshape(number_of_blocks, rows_per_block)
    place_blocks = token_placements[0].reshape(number_of_blocks, rows_per_block)
    key_index = jnp.arange(ROW_LENGTH, dtype=jnp.int32)

    def attend(items):
        query_block, query_index, query_place = items
        allowed = (key_index[None, :] <= query_index[:, None]) & (key_index[None, :] >= (query_index - query_place)[:, None])
        scores = lower_precision_backward(jnp.einsum('qkgd,skd->kgqs', query_block, every_key_row, precision=highest) * HEAD_SIZE ** (-0.5))
        masked = jnp.where(allowed[None, None], scores, masked_score)
        top_score = lax.optimization_barrier(jnp.max(masked, axis=-1, keepdims=True))
        weights_exp = jnp.exp(masked - top_score)
        probs_low = lower_precision(weights_exp / lax.optimization_barrier(jnp.sum(weights_exp, axis=-1, keepdims=True)))
        return jnp.einsum('kgqs,skd->qkgd', probs_low, every_value_row, precision=highest).reshape(rows_per_block, QUERY_HEAD_COUNT * HEAD_SIZE)
    attn_out = lax.map(jax.checkpoint(attend), (blocked_queries, index_blocks, place_blocks)).reshape(ROW_LENGTH, QUERY_HEAD_COUNT * HEAD_SIZE)
    attn_low = lower_precision(lower_precision_backward(attn_out))
    conv_in = jnp.concatenate([gatein_lin[:, HS * HEAD_SIZE:], bc_lin], axis=-1)[None]
    extended = jnp.concatenate([jnp.zeros((1, KC - 1, HS * HEAD_SIZE + 2 * DS), jnp.float32), conv_in], axis=1)
    conv_out = convolve(extended, jnp.concatenate([conv_inner, conv_bc], axis=1), token_placements)
    span_rows = min(256, ROW_LENGTH)
    span_count = ROW_LENGTH // span_rows
    inner_blocks = conv_out[0, :, :HS * HEAD_SIZE].reshape(span_count, 1, span_rows, HS, HEAD_SIZE)
    in_blocks = conv_out[0, :, HS * HEAD_SIZE:HS * HEAD_SIZE + DS].reshape(span_count, 1, span_rows, DS)
    out_blocks = conv_out[0, :, HS * HEAD_SIZE + DS:].reshape(span_count, 1, span_rows, DS)
    step_blocks = step_lin.reshape(span_count, 1, span_rows, HS)
    place_spans = token_placements[0].reshape(span_count, 1, span_rows)

    def advance(carried_state, items):
        values_in, steps_in, basis_in, basis_out, places_in = items
        output = mixer_output(values_in, steps_in, basis_in, basis_out, head_params, carried_state, places_in)
        passing, summary = mixer_summary(values_in, steps_in, basis_in, head_params, places_in)
        return (passing[..., None, None] * carried_state + summary, output)
    start_state = jnp.zeros((1, HS, HEAD_SIZE, DS), jnp.float32)
    ssm_out = lax.scan(jax.checkpoint(advance), start_state, (inner_blocks, step_blocks, in_blocks, out_blocks, place_spans))[1].reshape(ROW_LENGTH, HS * HEAD_SIZE)
    gated_values = ssm_out * jax.nn.silu(gatein_lin[:, :HS * HEAD_SIZE])
    inv_ssm = lax.rsqrt(lax.optimization_barrier(jnp.mean(gated_values * gated_values, axis=-1, keepdims=True)) + eps)
    part_attn = lower_precision_backward(product_full_precision(attn_low, w_out_attn))
    part_ssm = lower_precision_backward(product_full_precision(lower_precision(gated_values * ssm_gain), w_out_ssm))
    residual = inputs + (part_attn + inv_ssm * part_ssm)
    normed_two = lower_precision(residual * rms_scale(residual) * mlp_gain)
    gateup = lower_precision_backward(product_full_precision(normed_two, w_gateup.reshape(MODEL_WIDTH, 2 * FF)))
    hidden_mlp = lower_precision(jax.nn.silu(gateup[:, :FF]) * gateup[:, FF:])
    final_rows = residual + lower_precision_backward(product_full_precision(hidden_mlp, w_down))
    difference = final_rows - targets
    return (final_rows, jnp.sum(live_rows * lax.optimization_barrier(jnp.sum(difference * difference, axis=-1))))

def reference(hidden, teacher, positions, valid_mask, norm_gain, w_query, key_value_weight, w_gatein, w_bc, w_step, ssm_gain, mlp_gain, w_gateup, w_out_attn, w_out_ssm, w_down, conv_inner, conv_bc, head_params):
    params = (norm_gain.astype(jnp.float32), w_query.astype(jnp.float32), key_value_weight.astype(jnp.float32), w_gatein.astype(jnp.float32), w_bc.astype(jnp.float32), w_step.astype(jnp.float32), ssm_gain.astype(jnp.float32), mlp_gain.astype(jnp.float32), w_gateup.astype(jnp.float32), w_out_attn.astype(jnp.float32), w_out_ssm.astype(jnp.float32), w_down.astype(jnp.float32), conv_inner.astype(jnp.float32), conv_bc.astype(jnp.float32), head_params.astype(jnp.float32))
    live_all = valid_mask.astype(jnp.float32)
    token_count = jnp.sum(live_all)
    factor = ROWS * ROW_LENGTH / (2.0 * token_count)

    def row_step(running, items):
        row_in, row_target, row_places, row_live = items

        def objective(params_row, inputs):
            return layer_row(params_row, inputs, row_target.astype(jnp.float32), row_places[None], row_live)
        primal, pullback = jax.vjp(objective, params, row_in.astype(jnp.float32))
        grads_row, grad_in = pullback((jnp.zeros_like(primal[0]), factor * jnp.ones_like(primal[1])))
        running = jax.tree.map(jnp.add, running, grads_row)
        return (running, (primal[0], primal[1], grad_in))
    zero_grads = jax.tree.map(jnp.zeros_like, params)
    totals, (finals, squares, grad_rows) = lax.scan(row_step, zero_grads, (hidden, teacher, positions, live_all))
    loss_value = jnp.sum(squares) / (token_count * MODEL_WIDTH)
    return (finals.astype(jnp.bfloat16), loss_value, grad_rows, totals[0], totals[1], totals[2], totals[3], totals[4], totals[5], totals[6], totals[7], totals[8], totals[9], totals[10], totals[11], totals[12], totals[13], totals[14])
```

```python
import functools

import jax
import jax.numpy as jnp
from jax import lax
from jax.experimental import pallas as pl
from jax.experimental.pallas import tpu as pltpu
from jax.sharding import PartitionSpec as P

MODEL_WIDTH = 1024
HEAD_SIZE = 64
HS = 24
DS = 128
KC = 4

eps = 1e-05
rope_base = 100000000000.0
masked_score = -1e30
f32 = jnp.float32
bf16 = jnp.bfloat16
CHUNK = 128
HALO = 128
VMEM_LIMIT = 44 * 2**20


def dot(left, right, left_dim, right_dim, precision=None):
    return lax.dot_general(
        left, right, (((left_dim,), (right_dim,)), ((), ())), precision=precision, preferred_element_type=f32
    )


def exact(left, right, left_dim, right_dim):
    return dot(left, right, left_dim, right_dim, lax.Precision.HIGHEST)


def low(value):
    return value.astype(bf16)


def factors():
    fsdp = lax.axis_size("fsdp")
    side = int(round(fsdp**0.5))
    if side * side != fsdp:
        side = 1
    return (
        ("fsdp", fsdp // side, side),
        ("fsdp", side, 1),
        ("ctx", lax.axis_size("ctx"), 1),
    )


def coordinate(dim):
    axis, size, stride = dim
    return lax.rem(lax.axis_index(axis) // stride, size)


def shifted(value, dim, step):
    axis, size, stride = dim
    pairs = []
    for source in range(lax.axis_size(axis)):
        at = source // stride % size
        pairs.append((source, source + ((at + step) % size - at) * stride))
    return lax.ppermute(value, axis, pairs)


def passed_along(value, axis, steps):
    count = lax.axis_size(axis)
    pairs = [(s, s + steps) for s in range(count) if 0 <= s + steps < count]
    return lax.ppermute(value, axis, pairs)


def swapped(value):
    return lax.ppermute(value, "tp", [(0, 1), (1, 0)])


def gathered_along(value, dim):
    size = dim[1]
    if size == 1:
        return value[None]
    at = coordinate(dim)
    if size == 2:
        other = shifted(value, dim, 1)
        return jnp.where(at == 0, jnp.stack([value, other]), jnp.stack([other, value]))
    pieces = [value] + [shifted(value, dim, s) for s in range(1, size)]
    ring = jnp.stack((pieces[::-1]) * 2)
    return lax.dynamic_slice_in_dim(ring, size - 1 - at, size, 0)


def gather_rows(shard):
    ydim, xdim, zdim = factors()
    rows, columns = shard.shape
    line = gathered_along(shard, zdim)
    half = columns // 256 * 128
    one = gathered_along(line[..., :half], ydim)
    two = gathered_along(line[..., half:], xdim)
    one = jnp.swapaxes(gathered_along(one, xdim), 0, 1)
    two = gathered_along(two, ydim)
    whole = jnp.concatenate([one, two], axis=-1)
    return whole.reshape(-1, columns)


def in_pair(value, kept):
    body, tail = value[..., :-128], value[..., -128:]
    whole = tail + jnp.roll(tail, 64, axis=-1)
    high = lax.reduce_precision(whole, 8, 7)
    rest = (whole - high).astype(bf16)
    high = high.astype(bf16)
    column = lax.broadcasted_iota(jnp.int32, tail.shape, tail.ndim - 1)
    tail = jnp.where(column < kept, tail.astype(bf16), jnp.where(column < 64, high, rest))
    return jnp.concatenate([body.astype(bf16), tail], axis=-1)


def reduced_along(value, dim, front, kept=None):
    size = dim[1]
    if size == 1:
        return lax.index_in_dim(value, 0, front, False)
    at = coordinate(dim)
    total = lax.dynamic_index_in_dim(value, at, front, False).astype(f32)
    for step in range(1, size):
        piece = lax.dynamic_index_in_dim(value, lax.rem(at + step, size), front, False)
        total = total + shifted(piece, dim, step).astype(f32)
    return total.astype(bf16) if kept is None else in_pair(total, kept)


def scatter_rows(partial, kept=None):
    ydim, xdim, zdim = factors()
    columns = partial.shape[1]
    blocks = partial.reshape(ydim[1], xdim[1], zdim[1], -1, columns)
    half = columns // 256 * 128
    one = reduced_along(reduced_along(blocks[..., :half], xdim, 1), ydim, 0)
    two = reduced_along(reduced_along(blocks[..., half:], ydim, 0, kept), xdim, 0, kept)
    size = zdim[1]
    blocks = jnp.concatenate([one, two], axis=-1)
    at = coordinate(zdim)
    total = lax.dynamic_index_in_dim(blocks, at, 0, False).astype(f32)
    for step in range(1, size):
        piece = lax.dynamic_index_in_dim(blocks, lax.rem(at + step, size), 0, False)
        total = total + shifted(piece, zdim, step).astype(f32)
    return total


def total_over_all(value):
    for dim in factors():
        parts = [value] + [shifted(value, dim, s) for s in range(1, dim[1])]
        value = functools.reduce(jnp.add, parts)
    return value


def call(body, outs, scratch, *args):
    return pl.pallas_call(
        body,
        out_shape=[jax.ShapeDtypeStruct(s, d) for s, d in outs],
        in_specs=[pl.BlockSpec(memory_space=pltpu.VMEM)] * len(args),
        out_specs=[pl.BlockSpec(memory_space=pltpu.VMEM)] * len(outs),
        scratch_shapes=[pltpu.VMEM(s, d) for s, d in scratch],
        compiler_params=pltpu.CompilerParams(vmem_limit_bytes=VMEM_LIMIT),
    )(*args)


def rotated(block, cosine, sine):
    half = block.shape[0] // 2
    one, two = block[:half], block[half:]
    return jnp.concatenate([one * cosine - two * sine, two * cosine + one * sine], axis=0)


def flipped(block):
    return jnp.transpose(block.astype(f32)).astype(block.dtype)


def block_scores(keys, query, low, at, back, width):
    scores = dot(keys, query, 1, 0)
    place = lax.broadcasted_iota(jnp.int32, scores.shape, 0) - back
    allowed = place >= low
    if back == 0:
        token = at + lax.broadcasted_iota(jnp.int32, scores.shape, 1)
        allowed = allowed & (place <= token)
    return jnp.where(allowed, scores, masked_score)


def attend_body(blocks, heads, q_ref, low_ref, *refs):
    kv = refs[:blocks]
    out_ref, log_ref, key_ref, score_ref = refs[blocks:]
    length = q_ref.shape[1]
    width = min(256, length)
    for j in range(blocks):
        key_ref[j] = flipped(kv[j][:HEAD_SIZE, :])

    @pl.loop(0, heads)
    def _(h):
        rows = pl.ds(pl.multiple_of(h * HEAD_SIZE, HEAD_SIZE), HEAD_SIZE)
        for at in range(0, length, width):
            lanes = slice(at, at + width)
            query = q_ref[rows, lanes]
            low = low_ref[0:1, lanes]
            top = jnp.full((1, width), masked_score, f32)
            for j in range(blocks):
                scores = block_scores(key_ref[j], query, low, at, j * length, width)
                score_ref[j] = scores
                top = jnp.maximum(top, jnp.max(scores, axis=0, keepdims=True))
            total = jnp.zeros((1, width), f32)
            mixed = jnp.zeros((HEAD_SIZE, width), f32)
            for j in range(blocks):
                weight = jnp.exp(score_ref[j] - top)
                total = total + jnp.sum(weight, axis=0, keepdims=True)
                mixed = mixed + dot(kv[j][HEAD_SIZE:, :], weight.astype(bf16), 1, 0)
            out_ref[rows, lanes] = (mixed / total).astype(bf16)
            log_ref[h, :, lanes] = jnp.broadcast_to(top + jnp.log(total), (8, width))


def attend(query, low, kv):
    heads, length = query.shape[0] // HEAD_SIZE, query.shape[1]
    width = min(256, length)
    return call(
        functools.partial(attend_body, len(kv), heads),
        [(query.shape, bf16), ((heads, 8, length), f32)],
        [((len(kv), length, HEAD_SIZE), bf16), ((len(kv), length, width), f32)],
        query, low, *kv,
    )


def attend_back_body(blocks, heads, q_ref, low_ref, out_ref, log_ref, g_ref, cos_ref, sin_ref, *refs):
    kv = refs[:blocks]
    gq_ref = refs[blocks]
    gkv = refs[blocks + 1 : 2 * blocks + 1]
    key_ref, value_ref, sum_ref = refs[2 * blocks + 1 :]
    length = q_ref.shape[1]
    width = min(256, length)
    for j in range(blocks):
        key_ref[j] = flipped(kv[j][:HEAD_SIZE, :])
        value_ref[j] = flipped(kv[j][HEAD_SIZE:, :])
    sum_ref[...] = jnp.zeros_like(sum_ref)

    @pl.loop(0, heads)
    def _(h):
        rows = pl.ds(pl.multiple_of(h * HEAD_SIZE, HEAD_SIZE), HEAD_SIZE)
        for at in range(0, length, width):
            lanes = slice(at, at + width)
            query = q_ref[rows, lanes]
            grad = g_ref[rows, lanes]
            low = low_ref[0:1, lanes]
            log_total = log_ref[h, 0:1, lanes]
            inner = jnp.sum(grad.astype(f32) * out_ref[rows, lanes].astype(f32), axis=0, keepdims=True)
            gq = jnp.zeros((HEAD_SIZE, width), f32)
            for j in range(blocks):
                scores = block_scores(key_ref[j], query, low, at, j * length, width)
                probs = jnp.exp(scores - log_total)
                grad_probs = dot(value_ref[j], grad, 1, 0)
                grad_scores = (probs * (grad_probs - inner)).astype(bf16)
                gq = gq + dot(kv[j][:HEAD_SIZE, :], grad_scores, 1, 0)
                sum_ref[j, :HEAD_SIZE, :] += dot(query, grad_scores, 1, 1)
                sum_ref[j, HEAD_SIZE:, :] += dot(grad, probs.astype(bf16), 1, 1)
            gq = rotated(gq * HEAD_SIZE**-0.5, cos_ref[:, lanes], -sin_ref[:, lanes])
            gq_ref[rows, lanes] = gq.astype(bf16)

    for j in range(blocks):
        gkv[j][...] = sum_ref[j].astype(gkv[j].dtype)


def attend_back(query, low, out, log_total, grad, cosine, sine, kv):
    heads, length = query.shape[0] // HEAD_SIZE, query.shape[1]
    blocks = len(kv)
    return call(
        functools.partial(attend_back_body, blocks, heads),
        [(query.shape, bf16)] + [((2 * HEAD_SIZE, length), bf16)] * blocks,
        [((blocks, length, HEAD_SIZE), bf16)] * 2 + [((blocks, 2 * HEAD_SIZE, length), f32)],
        query, low, out, log_total, grad, cosine, sine, *kv,
    )


def conv_pre(block, taps, places):
    total = None
    for lag in range(KC):
        back = KC - 1 - lag
        moved = pltpu.roll(block, back, 1) if back else block
        term = taps[:, lag : lag + 1] * moved[:, HALO:]
        if back:
            term = jnp.where(places >= back, term, 0.0)
        total = term if total is None else total + term
    return total


def sigmoid(value):
    return 1.0 / (1.0 + jnp.exp(-value))


def running_sum(value, reverse=False):
    width = value.shape[1]
    lane = lax.broadcasted_iota(jnp.int32, value.shape, 1)
    step = 1
    while step < width:
        if reverse:
            value = value + jnp.where(lane < width - step, pltpu.roll(value, width - step, 1), 0.0)
        else:
            value = value + jnp.where(lane >= step, pltpu.roll(value, step, 1), 0.0)
        step *= 2
    return value


def widened(rows):
    return jnp.transpose(jnp.concatenate([rows, jnp.zeros((112, rows.shape[1]), f32)], axis=0))


def pack_decay(ref, decay, first):
    wide = jnp.broadcast_to(decay, (16, DS))
    high = wide.astype(bf16)
    ref[first : first + 16, :] = high
    ref[first + 16 : first + 32, :] = (wide - high.astype(f32)).astype(bf16)


def chain(packs, heads, state_ref):
    width = heads * HEAD_SIZE
    for h in range(heads):
        rows = slice(h * HEAD_SIZE, (h + 1) * HEAD_SIZE)
        state = jnp.zeros((HEAD_SIZE, DS), f32)
        for pack in packs[::-1]:
            decay = pack[width : width + 16, :].astype(f32) + pack[width + 16 : width + 32, :].astype(f32)
            state = pack[rows, :].astype(f32) + decay[h : h + 1, :] * state
        state_ref[rows, :] = state


def conv_body(heads, u_ref, bc_ref, step_ref, taps_ref, hp_ref, place_ref, xs_ref, b_ref, c_ref, bt_ref, ct_ref, dt_ref, cum_ref, cumt_ref, pack_ref, end_ref):
    places = place_ref[0:1, :]
    length = places.shape[1]
    width = heads * HEAD_SIZE
    for at, flat, side in ((0, b_ref, bt_ref), (DS, c_ref, ct_ref)):
        pre = conv_pre(bc_ref[at : at + DS, :], taps_ref[width + at : width + at + DS, :], places)
        basis = pre * sigmoid(pre)
        side[...] = basis
        flat[...] = jnp.transpose(basis)
    raw = step_ref[...] + hp_ref[:, 0:1]
    dt = jnp.maximum(raw, 0.0) + jnp.log1p(jnp.exp(-jnp.abs(raw)))
    cum = running_sum(dt * -jnp.exp(hp_ref[:, 1:2]))
    dt_ref[...] = dt
    cum_ref[...] = cum
    cumt_ref[...] = widened(cum)
    last = cum[:, length - 1 :]
    lane = lax.broadcasted_iota(jnp.int32, (1, length), 1)
    last_place = places[:, length - 1 :]
    reach = lane >= length - 1 - last_place
    to_end = jnp.where(reach, jnp.exp(jnp.minimum(last - cum, 0.0)) * dt, 0.0)
    end_ref[...] = to_end

    def one(h, _):
        rows = pl.ds(pl.multiple_of(h * HEAD_SIZE, HEAD_SIZE), HEAD_SIZE)
        pre = conv_pre(u_ref[rows, :], taps_ref[rows, :], places)
        values = pre * sigmoid(pre)
        xs_ref[rows, :] = values
        summary = dot((values * end_ref[pl.ds(h, 1), :]).astype(bf16), low(b_ref[...]), 1, 0)
        pack_ref[rows, :] = summary.astype(bf16)
        return 0

    lax.fori_loop(0, heads, one, 0)
    keep = (last_place > length - 1).astype(f32)
    pack_decay(pack_ref, jnp.exp(last) * keep, width)


def conv_forward(heads, u, bc, step, taps, hp, places):
    length = places.shape[1]
    width = heads * HEAD_SIZE
    return call(
        functools.partial(conv_body, heads),
        [
            ((width, length), f32),
            ((length, DS), f32),
            ((length, DS), f32),
            ((DS, length), f32),
            ((DS, length), f32),
            ((16, length), f32),
            ((16, length), f32),
            ((length, 128), f32),
            ((width + 32, DS), bf16),
        ],
        [((16, length), f32)],
        u, bc, step, taps, hp, places,
    )


def chunk_rows(k, cum_ref, place_ref):
    lanes = slice(k * CHUNK, (k + 1) * CHUNK)
    cum = cum_ref[:, lanes]
    places = place_ref[0:1, lanes]
    base = cum_ref[:, k * CHUNK - 1 : k * CHUNK] if k else jnp.zeros((16, 1), f32)
    last = cum[:, CHUNK - 1 :]
    last_place = places[:, CHUNK - 1 :]
    lane = lax.broadcasted_iota(jnp.int32, (1, CHUNK), 1)
    entry = jnp.where(places > lane, jnp.exp(jnp.minimum(cum - base, 0.0)), 0.0)
    to_end = jnp.where(lane >= CHUNK - 1 - last_place, jnp.exp(jnp.minimum(last - cum, 0.0)), 0.0)
    over = jnp.where(last_place > CHUNK - 1, jnp.exp(jnp.minimum(last - base, 0.0)), 0.0)
    source = lax.broadcasted_iota(jnp.int32, (CHUNK, CHUNK), 0)
    target = lax.broadcasted_iota(jnp.int32, (CHUNK, CHUNK), 1)
    allowed = (source <= target) & (source >= target - places)
    return cum, entry, to_end, over, allowed


def mix_body(heads, packs, xs_ref, b_ref, ct_ref, dt_ref, cum_ref, cumt_ref, hp_ref, place_ref, z_ref, *refs):
    pack_refs = refs[:packs]
    y_ref, states_ref, squares_ref, state_ref, inter_ref, w_ref = refs[packs:]
    length = place_ref.shape[1]
    chain(pack_refs, heads, state_ref)
    for k in range(length // CHUNK):
        lanes = slice(k * CHUNK, (k + 1) * CHUNK)
        cum, entry, to_end, over, allowed = chunk_rows(k, cum_ref, place_ref)
        low_state = state_ref[...].astype(bf16)
        states_ref[k] = low_state
        side = ct_ref[:, lanes]
        match = jnp.where(allowed, exact(b_ref[lanes, :], side, 1, 0), 0.0)
        inter_ref[...] = dot(low_state, low(side), 1, 0)
        squares = jnp.zeros((1, CHUNK), f32)
        for h in range(heads):
            rows = slice(h * HEAD_SIZE, (h + 1) * HEAD_SIZE)
            spread = cum[h : h + 1, :] - cumt_ref[lanes, h : h + 1]
            mixing = (jnp.exp(jnp.minimum(spread, 0.0)) * match).astype(bf16)
            values = xs_ref[rows, lanes]
            stepped = values * dt_ref[h : h + 1, lanes]
            result = dot(stepped.astype(bf16), mixing, 1, 0)
            result = result + inter_ref[rows, :] * entry[h : h + 1, :] + hp_ref[h : h + 1, 2:3] * values
            y_ref[rows, lanes] = result
            w_ref[rows, :] = (stepped * to_end[h : h + 1, :]).astype(bf16)
            gate = z_ref[rows, lanes]
            gated = result * gate * sigmoid(gate)
            squares = squares + jnp.sum(gated * gated, axis=0, keepdims=True)
        squares_ref[:, lanes] = jnp.broadcast_to(squares, (8, CHUNK))
        if k + 1 < length // CHUNK:
            added = dot(w_ref[...], low(b_ref[lanes, :]), 1, 0)
            for h in range(heads):
                rows = slice(h * HEAD_SIZE, (h + 1) * HEAD_SIZE)
                state_ref[rows, :] = over[h : h + 1, :] * state_ref[rows, :] + added[rows, :]


def mix_forward(heads, xs, b, ct, dt, cum, cumt, hp, places, z, packs):
    length = places.shape[1]
    width = heads * HEAD_SIZE
    return call(
        functools.partial(mix_body, heads, len(packs)),
        [
            ((width, length), f32),
            ((length // CHUNK, width, DS), bf16),
            ((8, length), f32),
        ],
        [((width, DS), f32), ((width, CHUNK), f32), ((width, CHUNK), bf16)],
        xs, b, ct, dt, cum, cumt, hp, places, z, *packs,
    )


def gate_body(heads, g_ref, y_ref, z_ref, gain_ref, inv_ref, dot_ref, c_ref, cum_ref, place_ref, gy_ref, gz_ref, ggain_ref, pack_ref, entry_ref):
    length = place_ref.shape[1]
    width = heads * HEAD_SIZE
    first = g_ref.shape[0] - width
    places = place_ref[0:1, :]
    inv = inv_ref[0:1, :]
    shrink = inv * inv * inv * dot_ref[0:1, :] * (1.0 / (HS * HEAD_SIZE))
    lane = lax.broadcasted_iota(jnp.int32, (1, length), 1)
    entry_ref[...] = jnp.where(places > lane, jnp.exp(jnp.minimum(cum_ref[...], 0.0)), 0.0)

    def one(h, _):
        start = pl.multiple_of(h * HEAD_SIZE, HEAD_SIZE)
        rows = pl.ds(start, HEAD_SIZE)
        grad = g_ref[pl.ds(start + first, HEAD_SIZE), :] * inv
        values = y_ref[rows, :]
        gate = z_ref[rows, :]
        sig = sigmoid(gate)
        silu = gate * sig
        gated = values * silu
        ggain_ref[rows, :] = jnp.broadcast_to(jnp.sum(grad * gated, axis=1, keepdims=True), (HEAD_SIZE, 128))
        grad_gated = grad * gain_ref[rows, :][:, 0:1] - shrink * gated
        grad_values = grad_gated * silu
        gy_ref[rows, :] = grad_values
        gz_ref[rows, :] = (grad_gated * values * sig * (1.0 + gate * (1.0 - sig))).astype(bf16)
        entered = (grad_values * entry_ref[pl.ds(h, 1), :]).astype(bf16)
        pack_ref[rows, :] = dot(entered, low(c_ref[...]), 1, 0).astype(bf16)
        return 0

    lax.fori_loop(0, heads, one, 0)
    last = length - 1
    keep = (places[:, last:] > last).astype(f32)
    pack_decay(pack_ref, jnp.exp(cum_ref[:, last:]) * keep, width)


def gate_back(heads, grads, y, z, gain, inv, inner, c, cum, places):
    length = places.shape[1]
    width = heads * HEAD_SIZE
    return call(
        functools.partial(gate_body, heads),
        [
            ((width, length), f32),
            ((width, length), bf16),
            ((width, 128), f32),
            ((width + 32, DS), bf16),
        ],
        [((16, length), f32)],
        grads, y, z, gain, inv, inner, c, cum, places,
    )


def mix_back_body(heads, packs, gy_ref, xs_ref, b_ref, c_ref, bt_ref, ct_ref, dt_ref, cum_ref, cumt_ref, step_ref, hp_ref, place_ref, states_ref, *refs):
    pack_refs = refs[:packs]
    gxs_ref, gbc_ref, gstep_ref, ghead_ref, grad_ref, reach_ref, inter_ref, gye_ref, w_ref, col_ref, cumg_ref, dtg_ref = refs[packs:]
    length = place_ref.shape[1]
    chain(pack_refs, heads, grad_ref)
    col_ref[...] = jnp.zeros_like(col_ref)
    cumg_ref[...] = jnp.zeros_like(cumg_ref)
    dtg_ref[...] = jnp.zeros_like(dtg_ref)
    rate = -jnp.exp(hp_ref[:, 1:2])
    bias_sum = jnp.zeros((16, CHUNK), f32)
    rate_sum = jnp.zeros((16, CHUNK), f32)
    ghead_ref[...] = jnp.zeros_like(ghead_ref)
    at_last = lax.broadcasted_iota(jnp.int32, (1, CHUNK), 1) == CHUNK - 1
    for k in reversed(range(length // CHUNK)):
        lanes = slice(k * CHUNK, (k + 1) * CHUNK)
        cum, entry, to_end, over, allowed = chunk_rows(k, cum_ref, place_ref)
        b_side, c_side = bt_ref[:, lanes], ct_ref[:, lanes]
        b_flat, c_flat = b_ref[lanes, :], c_ref[lanes, :]
        match = jnp.where(allowed, exact(b_flat, c_side, 1, 0), 0.0)
        low_grad = grad_ref[...].astype(bf16)
        reach_ref[...] = dot(low_grad, low(b_side), 1, 0)
        inter_ref[...] = dot(states_ref[k], low(c_side), 1, 0)
        grad_match = jnp.zeros((CHUNK, CHUNK), f32)
        for h in range(heads):
            rows = slice(h * HEAD_SIZE, (h + 1) * HEAD_SIZE)
            head = slice(h, h + 1)
            grad = gy_ref[rows, lanes]
            values = xs_ref[rows, lanes]
            dt = dt_ref[head, lanes]
            stepped = values * dt
            decay = jnp.exp(jnp.minimum(cum[head, :] - cumt_ref[lanes, head], 0.0))
            mixing = decay * match
            low_y = grad.astype(bf16)
            grad_mixing = dot(stepped.astype(bf16), low_y, 0, 0)
            grad_match = grad_match + grad_mixing * decay
            spread = grad_mixing * mixing
            to = to_end[head, :]
            reached = reach_ref[rows, :] * to
            grad_stepped = dot(low_y, mixing.astype(bf16), 1, 1) + reached
            ended = jnp.sum(reached * stepped, axis=0, keepdims=True)
            entered = grad * entry[head, :]
            entry_sum = jnp.sum(entered * inter_ref[rows, :], axis=0, keepdims=True)
            kept = over[head, :] * jnp.sum(
                jnp.sum(grad_ref[rows, :] * states_ref[k, rows, :].astype(f32), axis=0, keepdims=True),
                axis=1, keepdims=True,
            )
            at_end = jnp.sum(ended, axis=1, keepdims=True) + kept
            cumg_ref[head, :] = (
                jnp.sum(spread, axis=0, keepdims=True) + entry_sum - ended + jnp.where(at_last, at_end, 0.0)
            )
            col_ref[:, head] = jnp.sum(spread, axis=1, keepdims=True)
            dtg_ref[head, :] = jnp.sum(grad_stepped * values, axis=0, keepdims=True)
            gxs_ref[rows, lanes] = grad_stepped * dt + hp_ref[head, 2:3] * grad
            ghead_ref[head, 2:3] += jnp.sum(
                jnp.sum(grad * values, axis=0, keepdims=True), axis=1, keepdims=True
            )
            gye_ref[rows, :] = entered.astype(bf16)
            w_ref[rows, :] = (stepped * to).astype(bf16)
        low_match = jnp.where(allowed, grad_match, 0.0)
        gbc_ref[:DS, lanes] = exact(c_side, low_match, 1, 1) + dot(low_grad, w_ref[...], 0, 0)
        gbc_ref[DS:, lanes] = exact(b_side, low_match, 1, 0) + dot(states_ref[k], gye_ref[...], 0, 0)
        if k:
            added = dot(gye_ref[...], low(c_flat), 1, 0)
            for h in range(heads):
                rows = slice(h * HEAD_SIZE, (h + 1) * HEAD_SIZE)
                grad_ref[rows, :] = over[h : h + 1, :] * grad_ref[rows, :] + added[rows, :]
        grad_log = running_sum(cumg_ref[...] - jnp.transpose(col_ref[...])[:16, :], reverse=True)
        dt = dt_ref[:, lanes]
        rate_sum = rate_sum + grad_log * dt
        grad_step = (dtg_ref[...] + grad_log * rate) * sigmoid(step_ref[:, lanes] + hp_ref[:, 0:1])
        gstep_ref[:, lanes] = grad_step
        bias_sum = bias_sum + grad_step
    ghead_ref[:, 0:1] = jnp.sum(bias_sum, axis=1, keepdims=True)
    ghead_ref[:, 1:2] = jnp.sum(rate_sum, axis=1, keepdims=True) * rate


def mix_back(heads, gy, xs, b, c, bt, ct, dt, cum, cumt, step, hp, places, states, packs):
    length = places.shape[1]
    width = heads * HEAD_SIZE
    return call(
        functools.partial(mix_back_body, heads, len(packs)),
        [
            ((width, length), f32),
            ((2 * DS, length), f32),
            ((16, length), f32),
            ((16, 128), f32),
        ],
        [
            ((width, DS), f32),
            ((width, CHUNK), f32),
            ((width, CHUNK), f32),
            ((width, CHUNK), bf16),
            ((width, CHUNK), bf16),
            ((CHUNK, 128), f32),
            ((16, CHUNK), f32),
            ((16, CHUNK), f32),
        ],
        gy, xs, b, c, bt, ct, dt, cum, cumt, step, hp, places, states, *packs,
    )


def conv_back_body(groups, u_ref, bc_ref, gxs_ref, gbc_ref, taps_ref, place_ref, g_ref, halo_ref, gtaps_ref):
    places = place_ref[0:1, :]
    length = places.shape[1]

    def one(source, grads, at, out_at):
        block = source[at, :]
        taps = taps_ref[out_at, :]
        pre = conv_pre(block, taps, places)
        sig = sigmoid(pre)
        grad_pre = grads[at, :] * sig * (1.0 + pre * (1.0 - sig))
        total = None
        for lag in range(KC):
            back = KC - 1 - lag
            counted = jnp.where(places >= back, grad_pre, 0.0) if back else grad_pre
            moved = pltpu.roll(block, back, 1) if back else block
            gtaps_ref[out_at, lag : lag + 1] = jnp.sum(counted * moved[:, HALO:], axis=1, keepdims=True)
            wide = jnp.concatenate([jnp.zeros((counted.shape[0], HALO), f32), counted * taps[:, lag : lag + 1]], axis=1)
            wide = pltpu.roll(wide, length + HALO - back, 1) if back else wide
            total = wide if total is None else total + wide
        g_ref[out_at, :] = total[:, HALO:]
        return jnp.transpose(total[:, :HALO])[HALO - 8 :, :]

    def inner(i, _):
        start = pl.multiple_of(i * 128, 128)
        rows = pl.ds(start, 128)
        halo_ref[:, pl.ds(start, 128)] = one(u_ref, gxs_ref, rows, rows)
        return 0

    gtaps_ref[...] = jnp.zeros_like(gtaps_ref)
    lax.fori_loop(0, groups, inner, 0)
    for i in range(2):
        out_at = slice((groups + i) * 128, (groups + i + 1) * 128)
        halo_ref[:, out_at] = one(bc_ref, gbc_ref, slice(i * 128, (i + 1) * 128), out_at)


def conv_back(u, bc, gxs, gbc, taps, places):
    length = places.shape[1]
    width = u.shape[0]
    return call(
        functools.partial(conv_back_body, width // 128),
        [((width + 2 * DS, length), f32), ((8, width + 2 * DS), f32), ((width + 2 * DS, 128), f32)],
        [],
        u, bc, gxs, gbc, taps, places,
    )


def rms_scale(values):
    return lax.rsqrt(jnp.mean(values * values, axis=-1, keepdims=True) + eps)


def norm_back(inputs, inv_rms, grad_normed):
    inner_mean = jnp.mean(grad_normed * inputs, axis=-1, keepdims=True)
    return inv_rms * grad_normed - inv_rms * inv_rms * inv_rms * inputs * inner_mean


def padded_rows(block, rows):
    return jnp.pad(block, ((0, rows - block.shape[0]), (0, 0)))


def shards(
    hidden,
    teacher,
    positions,
    valid_mask,
    norm_gain,
    w_query,
    key_value_weight,
    w_gatein,
    w_bc,
    w_step,
    ssm_gain,
    mlp_gain,
    w_gateup,
    w_out_attn,
    w_out_ssm,
    w_down,
    conv_inner,
    conv_bc,
    head_params,
):
    ways = lax.axis_size(("fsdp", "ctx"))
    blocks = lax.axis_size("ctx")
    rows = norm_gain.shape[0]
    length = hidden.shape[1]
    heads = w_step.shape[1]
    width = heads * HEAD_SIZE
    attn_width = w_query.shape[1]
    kv_width = key_value_weight.shape[2]
    ff_local = w_down.shape[0]
    inner_rows = ssm_gain.shape[0]
    bc_rows = conv_bc.shape[1]
    qkv_width = attn_width + 2 * kv_width
    step_at = qkv_width + 2 * DS

    small = jnp.concatenate(
        [
            w_step,
            norm_gain[:, None],
            mlp_gain[:, None],
            padded_rows(ssm_gain[:, None], rows),
            padded_rows(conv_inner.T, rows),
            padded_rows(conv_bc.T, rows),
        ],
        axis=1,
    )
    small_width = small.shape[1]
    first_shard = jnp.concatenate(
        [w_query, key_value_weight.reshape(rows, 2 * kv_width), w_bc, jnp.pad(small, ((0, 0), (0, 128 - small_width)))],
        axis=1,
    )
    mixer_shard = jnp.concatenate([w_gatein[:, 1], w_gatein[:, 0]], axis=1)
    out_shard = jnp.concatenate([w_out_attn, w_out_ssm], axis=0).T
    mlp_shard = jnp.concatenate([w_gateup.reshape(rows, 2 * ff_local), w_down.T], axis=1)

    mlp_w = lax.all_gather(mlp_shard, ("fsdp", "ctx"), axis=0, tiled=True)
    first_w = gather_rows(first_shard)
    first_w, mixer_shard = lax.optimization_barrier((first_w, mixer_shard))
    mixer_w = gather_rows(mixer_shard)
    mixer_w, out_shard = lax.optimization_barrier((mixer_w, out_shard))
    out_w = gather_rows(out_shard)
    gateup_w, down_w = mlp_w[:, : 2 * ff_local], mlp_w[:, 2 * ff_local :]

    live_rows = valid_mask.reshape(length, 1).astype(f32)
    total_count = total_over_all(jnp.full((8, 128), jnp.sum(live_rows), f32))[0, 0]

    flat_in = hidden.reshape(length, MODEL_WIDTH).astype(f32)
    before = passed_along(hidden.reshape(length, MODEL_WIDTH)[length - 16 :], "ctx", 1).astype(f32)
    extended = jnp.concatenate([jnp.zeros((HALO - 16, MODEL_WIDTH), f32), before, flat_in], axis=0)
    places = positions.reshape(1, length)
    place_rows = jnp.broadcast_to(places, (8, length))
    low_rows = jnp.broadcast_to(jnp.arange(length, dtype=jnp.int32)[None] - places, (8, length))
    half = HEAD_SIZE // 2
    frequency = rope_base ** (-2.0 * jnp.arange(half, dtype=f32) / HEAD_SIZE)
    angle = frequency[:, None] * places.astype(f32)
    cosine, sine = jnp.cos(angle), jnp.sin(angle)
    hp = jnp.pad(head_params.T, ((0, 16 - heads), (0, 125)))

    tail = first_w[:, step_at:]
    at = heads
    gain_one = tail[:, at].astype(f32)[None]
    gain_two = tail[:, at + 1].astype(f32)[None]
    by_shard = tail.astype(f32).reshape(ways, rows, 128)
    gain_ssm = by_shard[:, :inner_rows, at + 2 : at + 3].reshape(width, 1)
    taps = jnp.concatenate(
        [
            by_shard[:, :inner_rows, at + 3 : at + 3 + KC].reshape(width, KC),
            by_shard[:, :bc_rows, at + 3 + KC : at + 3 + 2 * KC].reshape(2 * DS, KC),
        ],
        axis=0,
    )
    taps = jnp.pad(taps, ((0, 0), (0, 128 - KC)))
    gain_wide = jnp.pad(gain_ssm, ((0, 0), (0, 127)))

    scale_ext = rms_scale(extended)
    normed_ext = (extended * scale_ext * gain_one).astype(bf16)
    normed = normed_ext[HALO:]
    scale_one = scale_ext[HALO:]

    first_lin = dot(first_w, normed_ext, 0, 1)
    qkv = first_lin[:qkv_width, HALO:]
    query = jnp.concatenate(
        [rotated(qkv[a : a + HEAD_SIZE], cosine, sine) for a in range(0, attn_width, HEAD_SIZE)], axis=0
    ).astype(bf16) * bf16(HEAD_SIZE**-0.5)
    kv_own = jnp.concatenate(
        [rotated(qkv[attn_width : attn_width + HEAD_SIZE], cosine, sine), qkv[attn_width + kv_width :]], axis=0
    ).astype(bf16)
    kv = [kv_own] + [passed_along(kv_own, "ctx", s) for s in range(1, blocks)]
    bc_in = first_lin[qkv_width:step_at]
    step = first_lin[step_at : step_at + 16, HALO:]

    mixer_lin = dot(mixer_w, normed_ext, 0, 1)
    u_in = mixer_lin[:width]
    gate_z = mixer_lin[width:, HALO:]
    xs, b_flat, c_flat, b_side, c_side, dt, cum, cumt, pack = conv_forward(heads, u_in, bc_in, step, taps, hp, place_rows)
    packs = [passed_along(pack, "ctx", s) for s in range(1, blocks)]
    attn, log_total = attend(query, low_rows, kv)
    ssm, states, squares = mix_forward(heads, xs, b_flat, c_side, dt, cum, cumt, hp, place_rows, gate_z, packs)
    inv_ssm = lax.rsqrt((squares + swapped(squares)) / (HS * HEAD_SIZE) + eps)
    gated = ssm * jax.nn.silu(gate_z)
    branches = jnp.concatenate([attn, (gated * gain_ssm * inv_ssm[0:1]).astype(bf16)], axis=0)
    part = dot(branches, out_w, 0, 1)
    residual = flat_in + (part + swapped(part.astype(bf16)).astype(f32))

    scale_two = rms_scale(residual)
    normed_two = (residual * scale_two * gain_two).astype(bf16)
    gateup = dot(normed_two, gateup_w, 1, 0)
    gate_part, up_part = gateup[:, :ff_local], gateup[:, ff_local:]
    hidden_mlp = (jax.nn.silu(gate_part) * up_part).astype(bf16)
    part = dot(hidden_mlp, down_w, 1, 1)
    final_rows = residual + (part + swapped(part.astype(bf16)).astype(f32))
    difference = (final_rows - teacher.reshape(length, MODEL_WIDTH).astype(f32)) * live_rows
    local_sq = jnp.sum(difference * difference)

    all_tokens = length * ways
    grad_final = difference * (all_tokens / total_count)
    grad_low = grad_final.astype(bf16)
    grad_hidden_mlp = dot(grad_low, down_w, 1, 0)
    sigma = jax.nn.sigmoid(gate_part)
    grad_gate = grad_hidden_mlp * up_part * sigma * (1.0 + gate_part * (1.0 - sigma))
    grad_up = grad_hidden_mlp * gate_part * sigma
    grad_gateup = jnp.concatenate([grad_gate, grad_up], axis=-1).astype(bf16)
    part = dot(grad_gateup, gateup_w, 1, 1)
    grad_normed_two = part + swapped(part.astype(bf16)).astype(f32)
    mlp_grads = jnp.concatenate(
        [dot(normed_two, grad_gateup, 0, 0).astype(bf16), dot(grad_low, hidden_mlp, 0, 0).astype(bf16)], axis=1
    )
    mlp_out = lax.psum_scatter(mlp_grads, ("fsdp", "ctx"), scatter_dimension=0, tiled=True)
    grad_gain_two = jnp.sum(grad_normed_two * residual * scale_two, axis=0)
    grad_residual = grad_final + norm_back(residual, scale_two, grad_normed_two * gain_two)
    grad_out = grad_residual.astype(bf16)

    grad_branches = dot(out_w, grad_out, 0, 1)
    grad_attn = grad_branches[:attn_width].astype(bf16)
    inner = jnp.sum(grad_branches[attn_width:] * gated * gain_ssm, axis=0, keepdims=True)
    inner = jnp.broadcast_to(inner, (8, length))
    inner = inner + swapped(inner)
    gy, grad_z, grad_gain_ssm, back_pack = gate_back(
        heads, grad_branches, ssm, gate_z, gain_wide, inv_ssm, inner, c_flat, cum, place_rows
    )
    back_packs = [passed_along(back_pack, "ctx", -s) for s in range(1, blocks)]
    grad_out_w = scatter_rows(dot(grad_out, branches, 0, 1).astype(bf16))
    grad_query, *grad_kv = attend_back(query, low_rows, attn, log_total, grad_attn, cosine, sine, kv)
    grad_kv_own = grad_kv[0].astype(f32)
    for s in range(1, blocks):
        grad_kv_own = grad_kv_own + passed_along(grad_kv[s], "ctx", -s).astype(f32)
    grad_kv_low = jnp.concatenate(
        [rotated(grad_kv_own[:HEAD_SIZE], cosine, -sine), grad_kv_own[HEAD_SIZE:]], axis=0
    ).astype(bf16)
    grad_xs, grad_basis, grad_step, grad_head = mix_back(
        heads, gy, xs, b_flat, c_flat, b_side, c_side, dt, cum, cumt, step, hp, place_rows, states, back_packs
    )
    grad_conv, halo, grad_taps = conv_back(u_in, bc_in, grad_xs, grad_basis, taps, place_rows)
    behind = passed_along(halo, "ctx", -1)
    grad_conv = grad_conv + jnp.pad(behind.T, ((0, 0), (length - 8, 0)))
    grad_conv_low = grad_conv.astype(bf16)

    grad_first = jnp.concatenate(
        [grad_query, grad_kv_low, grad_conv_low[width:], jnp.pad(grad_step[:heads].astype(bf16), ((0, 128 - heads), (0, 0)))],
        axis=0,
    )
    grad_mixer = jnp.concatenate([grad_conv_low[:width], grad_z], axis=0)
    part = dot(grad_first, first_w, 0, 1) + dot(grad_mixer, mixer_w, 0, 1)
    grad_normed = part + swapped(part.astype(bf16)).astype(f32)
    grad_gain_one = jnp.sum(grad_normed * flat_in * scale_one, axis=0)
    grad_input = grad_residual + norm_back(flat_in, scale_one, grad_normed * gain_one)

    def by_rows(block):
        blocked = block.reshape(ways, -1, block.shape[-1])
        return jnp.pad(blocked, ((0, 0), (0, rows - blocked.shape[1]), (0, 0))).reshape(MODEL_WIDTH, -1)

    scalars = jnp.concatenate([grad_head[:heads, :3].reshape(1, 3 * heads), local_sq.reshape(1, 1)], axis=1)
    scalars = by_rows(jnp.broadcast_to(scalars[None], (ways, 1, 3 * heads + 1)))
    small_grads = jnp.concatenate(
        [
            grad_gain_one[:, None],
            grad_gain_two[:, None],
            by_rows(grad_gain_ssm[:, :1]),
            by_rows(grad_taps[:width, :KC]),
            by_rows(grad_taps[width:, :KC]),
            scalars,
        ],
        axis=1,
    )
    spare = 64 - heads - small_grads.shape[1]
    grad_first_w = dot(normed, grad_first, 0, 1)
    grad_tail = grad_first_w[:, step_at:] + jnp.pad(small_grads, ((0, 0), (heads, spare + 64)))
    grad_first_w = in_pair(jnp.concatenate([grad_first_w[:, :step_at], grad_tail], axis=1), heads)
    mixer_out = scatter_rows(dot(normed, grad_mixer, 0, 1).astype(bf16))
    first_out = scatter_rows(grad_first_w, heads)
    first_tail = first_out[:, step_at:]
    small_out = jnp.concatenate([first_tail[:, :heads], first_tail[:, heads:64] + first_tail[:, 64 + heads :]], axis=1)
    shared = jnp.concatenate([first_out[:, qkv_width:step_at], small_out[:, heads + 3 + KC :][:, :KC]], axis=1)
    shared = shared + swapped(shared)

    at = heads
    scalar_at = at + 3 + 2 * KC
    head_out = small_out[0, scalar_at : scalar_at + 3 * heads].reshape(heads, 3).T
    loss_value = small_out[0, scalar_at + 3 * heads] / (total_count * MODEL_WIDTH)
    return (
        final_rows.astype(bf16).reshape(1, length, MODEL_WIDTH),
        loss_value,
        grad_input.reshape(1, length, MODEL_WIDTH),
        small_out[:, at],
        first_out[:, :attn_width],
        first_out[:, attn_width:qkv_width].reshape(rows, 2, kv_width),
        jnp.stack([mixer_out[:, width:], mixer_out[:, :width]], axis=1),
        shared[:, : 2 * DS],
        small_out[:, :heads],
        small_out[:inner_rows, at + 2],
        small_out[:, at + 1],
        mlp_out[:, : 2 * ff_local].astype(f32).reshape(rows, 2, ff_local),
        grad_out_w[:, :attn_width].T,
        grad_out_w[:, attn_width:].T,
        mlp_out[:, 2 * ff_local :].astype(f32).T,
        small_out[:inner_rows, at + 3 : at + 3 + KC].T,
        shared[:bc_rows, 2 * DS :].T,
        head_out,
    )


def solution(mesh):
    placed = (
        P("fsdp", "ctx", None),
        P("fsdp", "ctx", None),
        P("fsdp", "ctx"),
        P("fsdp", "ctx"),
        P(("fsdp", "ctx")),
        P(("fsdp", "ctx"), "tp"),
        P(("fsdp", "ctx"), None, "tp"),
        P(("fsdp", "ctx"), None, "tp"),
        P(("fsdp", "ctx"), None),
        P(("fsdp", "ctx"), "tp"),
        P(("tp", "fsdp", "ctx")),
        P(("fsdp", "ctx")),
        P(("fsdp", "ctx"), None, "tp"),
        P("tp", ("fsdp", "ctx")),
        P("tp", ("fsdp", "ctx")),
        P("tp", ("fsdp", "ctx")),
        P(None, ("tp", "fsdp", "ctx")),
        P(None, ("fsdp", "ctx")),
        P(None, "tp"),
    )
    return jax.shard_map(
        shards,
        mesh=mesh,
        in_specs=placed,
        out_specs=(
            P("fsdp", "ctx", None),
            P(),
            P("fsdp", "ctx", None),
            P(("fsdp", "ctx")),
            P(("fsdp", "ctx"), "tp"),
            P(("fsdp", "ctx"), None, "tp"),
            P(("fsdp", "ctx"), None, "tp"),
            P(("fsdp", "ctx"), None),
            P(("fsdp", "ctx"), "tp"),
            P(("tp", "fsdp", "ctx")),
            P(("fsdp", "ctx")),
            P(("fsdp", "ctx"), None, "tp"),
            P("tp", ("fsdp", "ctx")),
            P("tp", ("fsdp", "ctx")),
            P("tp", ("fsdp", "ctx")),
            P(None, ("tp", "fsdp", "ctx")),
            P(None, ("fsdp", "ctx")),
            P(None, "tp"),
        ),
        check_vma=False,
    )
```

```python
import functools

import jax
import jax.numpy as jnp
from jax import lax
from jax.experimental import pallas as pl
from jax.experimental.pallas import tpu as pltpu
from jax.sharding import PartitionSpec as P

MODEL_WIDTH = 1024
HEAD_SIZE = 64
HS = 24
DS = 128
KC = 4

eps = 1e-05
rope_base = 100000000000.0
masked_score = -1e30
f32 = jnp.float32
bf16 = jnp.bfloat16
CHUNK = 128
HALO = 128
VMEM_LIMIT = 40 * 2**20


def dot(left, right, left_dim, right_dim, precision=None):
    return lax.dot_general(
        left, right, (((left_dim,), (right_dim,)), ((), ())), precision=precision, preferred_element_type=f32
    )


def exact(left, right, left_dim, right_dim):
    return dot(left, right, left_dim, right_dim, lax.Precision.HIGHEST)


def low(value):
    return value.astype(bf16)


def factors():
    fsdp = lax.axis_size("fsdp")
    side = int(round(fsdp**0.5))
    if side * side != fsdp:
        side = 1
    return (
        ("fsdp", fsdp // side, side),
        ("fsdp", side, 1),
        ("ctx", lax.axis_size("ctx"), 1),
    )


def coordinate(dim):
    axis, size, stride = dim
    return lax.rem(lax.axis_index(axis) // stride, size)


def shifted(value, dim, step):
    axis, size, stride = dim
    pairs = []
    for source in range(lax.axis_size(axis)):
        at = source // stride % size
        pairs.append((source, source + ((at + step) % size - at) * stride))
    return lax.ppermute(value, axis, pairs)


def passed_along(value, axis, steps):
    count = lax.axis_size(axis)
    pairs = [(s, s + steps) for s in range(count) if 0 <= s + steps < count]
    return lax.ppermute(value, axis, pairs)


def swapped(value):
    return lax.ppermute(value, "tp", [(0, 1), (1, 0)])


def gathered_along(value, dim):
    size = dim[1]
    if size == 1:
        return value[None]
    at = coordinate(dim)
    if size == 2:
        other = shifted(value, dim, 1)
        return jnp.where(at == 0, jnp.stack([value, other]), jnp.stack([other, value]))
    pieces = [value] + [shifted(value, dim, s) for s in range(1, size)]
    ring = jnp.stack((pieces[::-1]) * 2)
    return lax.dynamic_slice_in_dim(ring, size - 1 - at, size, 0)


def tied(*values):
    return lax.optimization_barrier(values)


def gathered_line(shard, doubling=True):
    zdim = factors()[2]
    size = zdim[1]
    if not doubling or size & (size - 1):
        return gathered_along(shard, zdim)
    at = coordinate(zdim)
    value = shard[None]
    step = 1
    while step < size:
        other = lax.ppermute(value, zdim[0], [(i, i ^ step) for i in range(size)])
        pair = (jnp.concatenate([value, other]), jnp.concatenate([other, value]))
        value = jnp.where(at // step % 2 == 0, *pair)
        step *= 2
    return value


def gathered_plane(line):
    ydim, xdim, _ = factors()
    columns = line.shape[-1]
    half = columns // 256 * 128
    one = gathered_along(line[..., :half], ydim)
    two = gathered_along(line[..., half:], xdim)
    one = jnp.swapaxes(gathered_along(one, xdim), 0, 1)
    two = gathered_along(two, ydim)
    return jnp.concatenate([one, two], axis=-1).reshape(-1, columns)


def in_pair(value, kept):
    body, tail = value[..., :-128], value[..., -128:]
    whole = tail + jnp.roll(tail, 64, axis=-1)
    high = lax.reduce_precision(whole, 8, 7)
    rest = (whole - high).astype(bf16)
    high = high.astype(bf16)
    column = lax.broadcasted_iota(jnp.int32, tail.shape, tail.ndim - 1)
    tail = jnp.where(column < kept, tail.astype(bf16), jnp.where(column < 64, high, rest))
    return jnp.concatenate([body.astype(bf16), tail], axis=-1)


def reduced_along(value, dim, front, kept=None):
    size = dim[1]
    if size == 1:
        return lax.index_in_dim(value, 0, front, False)
    at = coordinate(dim)
    total = lax.dynamic_index_in_dim(value, at, front, False).astype(f32)
    for step in range(1, size):
        piece = lax.dynamic_index_in_dim(value, lax.rem(at + step, size), front, False)
        total = total + shifted(piece, dim, step).astype(f32)
    return total.astype(bf16) if kept is None else in_pair(total, kept)


def scatter_first(partial, kept=None):
    ydim, xdim, zdim = factors()
    columns = partial.shape[1]
    blocks = partial.reshape(ydim[1], xdim[1], zdim[1], -1, columns)
    half = columns // 256 * 128
    return reduced_along(blocks[..., :half], xdim, 1), reduced_along(blocks[..., half:], ydim, 0, kept)


def scatter_second(parts, kept=None):
    ydim, xdim, _ = factors()
    return reduced_along(parts[0], ydim, 0), reduced_along(parts[1], xdim, 0, kept)


def exchanged(blocks, step):
    zdim = factors()[2]
    upper = coordinate(zdim) // step % 2 == 1
    halves = blocks.reshape(2, step, *blocks.shape[1:])
    kept = jnp.where(upper, halves[1], halves[0])
    sent = jnp.where(upper, halves[0], halves[1])
    return kept, lax.ppermute(sent, zdim[0], [(i, i ^ step) for i in range(zdim[1])])


def halved(parts):
    blocks = jnp.concatenate(parts, axis=-1)
    return exchanged(blocks, blocks.shape[0] // 2)


def halved_on(kept, other):
    while True:
        total = kept.astype(f32) + other.astype(f32)
        if total.shape[0] == 1:
            return total[0]
        kept, other = exchanged(total.astype(bf16), total.shape[0] // 2)


def scatter_third(parts):
    zdim = factors()[2]
    blocks = jnp.concatenate(parts, axis=-1)
    at = coordinate(zdim)
    total = lax.dynamic_index_in_dim(blocks, at, 0, False).astype(f32)
    for step in range(1, zdim[1]):
        piece = lax.dynamic_index_in_dim(blocks, lax.rem(at + step, zdim[1]), 0, False)
        total = total + shifted(piece, zdim, step).astype(f32)
    return total


def call(body, outs, scratch, *args):
    return pl.pallas_call(
        body,
        out_shape=[jax.ShapeDtypeStruct(s, d) for s, d in outs],
        in_specs=[pl.BlockSpec(memory_space=pltpu.VMEM)] * len(args),
        out_specs=[pl.BlockSpec(memory_space=pltpu.VMEM)] * len(outs),
        scratch_shapes=[pltpu.VMEM(s, d) for s, d in scratch],
        compiler_params=pltpu.CompilerParams(vmem_limit_bytes=VMEM_LIMIT),
        cost_estimate=pl.CostEstimate(flops=1000, bytes_accessed=1000, transcendentals=0),
    )(*args)


def rotated(block, cosine, sine):
    half = block.shape[0] // 2
    one, two = block[:half], block[half:]
    return jnp.concatenate([one * cosine - two * sine, two * cosine + one * sine], axis=0)


def flipped(block):
    return jnp.transpose(block.astype(f32)).astype(block.dtype)


def block_scores(keys, query, low, at, back, width):
    scores = dot(keys, query, 1, 0)
    place = lax.broadcasted_iota(jnp.int32, scores.shape, 0) - back
    allowed = place >= low
    if back == 0:
        token = at + lax.broadcasted_iota(jnp.int32, scores.shape, 1)
        allowed = allowed & (place <= token)
    return jnp.where(allowed, scores, masked_score)


def attend_body(blocks, heads, q_ref, low_ref, *refs):
    kv = refs[:blocks]
    out_ref, log_ref, key_ref, score_ref = refs[blocks:]
    length = q_ref.shape[1]
    width = min(256, length)
    for j in range(blocks):
        key_ref[j] = flipped(kv[j][:HEAD_SIZE, :])

    @pl.loop(0, heads)
    def _(h):
        rows = pl.ds(pl.multiple_of(h * HEAD_SIZE, HEAD_SIZE), HEAD_SIZE)
        for at in range(0, length, width):
            lanes = slice(at, at + width)
            query = q_ref[rows, lanes]
            low = low_ref[0:1, lanes]
            top = jnp.full((1, width), masked_score, f32)
            for j in range(blocks):
                scores = block_scores(key_ref[j], query, low, at, j * length, width)
                score_ref[j] = scores
                top = jnp.maximum(top, jnp.max(scores, axis=0, keepdims=True))
            total = jnp.zeros((1, width), f32)
            mixed = jnp.zeros((HEAD_SIZE, width), f32)
            for j in range(blocks):
                weight = jnp.exp(score_ref[j] - top)
                total = total + jnp.sum(weight, axis=0, keepdims=True)
                mixed = mixed + dot(kv[j][HEAD_SIZE:, :], weight.astype(bf16), 1, 0)
            out_ref[rows, lanes] = (mixed / total).astype(bf16)
            log_ref[h, :, lanes] = jnp.broadcast_to(top + jnp.log(total), (8, width))


def attend(query, low, kv):
    heads, length = query.shape[0] // HEAD_SIZE, query.shape[1]
    width = min(256, length)
    return call(
        functools.partial(attend_body, len(kv), heads),
        [(query.shape, bf16), ((heads, 8, length), f32)],
        [((len(kv), length, HEAD_SIZE), bf16), ((len(kv), length, width), f32)],
        query, low, *kv,
    )


def attend_back_body(blocks, heads, q_ref, low_ref, out_ref, log_ref, g_ref, cos_ref, sin_ref, *refs):
    kv = refs[:blocks]
    gq_ref = refs[blocks]
    gkv = refs[blocks + 1 : 2 * blocks + 1]
    key_ref, value_ref, sum_ref = refs[2 * blocks + 1 :]
    length = q_ref.shape[1]
    width = min(256, length)
    for j in range(blocks):
        key_ref[j] = flipped(kv[j][:HEAD_SIZE, :])
        value_ref[j] = flipped(kv[j][HEAD_SIZE:, :])
    sum_ref[...] = jnp.zeros_like(sum_ref)

    @pl.loop(0, heads)
    def _(h):
        rows = pl.ds(pl.multiple_of(h * HEAD_SIZE, HEAD_SIZE), HEAD_SIZE)
        for at in range(0, length, width):
            lanes = slice(at, at + width)
            query = q_ref[rows, lanes]
            grad = g_ref[rows, lanes]
            low = low_ref[0:1, lanes]
            log_total = log_ref[h, 0:1, lanes]
            inner = jnp.sum(grad.astype(f32) * out_ref[rows, lanes].astype(f32), axis=0, keepdims=True)
            gq = jnp.zeros((HEAD_SIZE, width), f32)
            for j in range(blocks):
                scores = block_scores(key_ref[j], query, low, at, j * length, width)
                probs = jnp.exp(scores - log_total)
                grad_probs = dot(value_ref[j], grad, 1, 0)
                grad_scores = (probs * (grad_probs - inner)).astype(bf16)
                gq = gq + dot(kv[j][:HEAD_SIZE, :], grad_scores, 1, 0)
                sum_ref[j, :HEAD_SIZE, :] += dot(query, grad_scores, 1, 1)
                sum_ref[j, HEAD_SIZE:, :] += dot(grad, probs.astype(bf16), 1, 1)
            gq = rotated(gq * HEAD_SIZE**-0.5, cos_ref[:, lanes], -sin_ref[:, lanes])
            gq_ref[rows, lanes] = gq.astype(bf16)

    for j in range(blocks):
        gkv[j][...] = sum_ref[j].astype(gkv[j].dtype)


def attend_back(query, low, out, log_total, grad, cosine, sine, kv):
    heads, length = query.shape[0] // HEAD_SIZE, query.shape[1]
    blocks = len(kv)
    return call(
        functools.partial(attend_back_body, blocks, heads),
        [(query.shape, bf16)] + [((2 * HEAD_SIZE, length), bf16)] * blocks,
        [((blocks, length, HEAD_SIZE), bf16)] * 2 + [((blocks, 2 * HEAD_SIZE, length), f32)],
        query, low, out, log_total, grad, cosine, sine, *kv,
    )


def pack_body(q_ref, kv_ref, bc_ref, step_ref, gains_ref, ssm_ref, inner_ref, basis_ref, valid_ref, out_ref, small_ref):
    rows, heads = step_ref.shape
    small_ref[...] = jnp.zeros_like(small_ref)
    small_ref[heads : heads + 2, :rows] = gains_ref[...].astype(f32)
    small_ref[heads + 2 : heads + 3, : ssm_ref.shape[1]] = ssm_ref[...].astype(f32)
    small_ref[heads + 3 : heads + 3 + KC, : inner_ref.shape[1]] = inner_ref[...].astype(f32)
    small_ref[heads + 3 + KC : heads + 3 + 2 * KC, : basis_ref.shape[1]] = basis_ref[...].astype(f32)
    count = jnp.sum(valid_ref[...].astype(f32), axis=1, keepdims=True)
    high = jnp.floor(count * (1.0 / 16.0))
    small_ref[heads + 3 + 2 * KC : heads + 4 + 2 * KC, 0:1] = high
    small_ref[heads + 4 + 2 * KC : heads + 5 + 2 * KC, 0:1] = count - 16.0 * high
    tail = jnp.transpose(small_ref[...])[:rows, :]
    step = jnp.concatenate([step_ref[...].astype(f32), jnp.zeros((rows, 128 - heads), f32)], axis=1)
    at = 0
    for ref in (q_ref, kv_ref, bc_ref):
        out_ref[:, at : at + ref.shape[1]] = ref[...]
        at += ref.shape[1]
    out_ref[:, at:] = (tail + step).astype(bf16)


def packed(*args):
    columns = sum(a.shape[1] for a in args[:3]) + 128
    return call(pack_body, [((args[0].shape[0], columns), bf16)], [((128, 128), f32)], *args)[0]


def prep_body(x_ref, before_ref, xt_ref, scale_ref):
    length = x_ref.shape[0]
    for at in range(-HALO, length, HALO):
        if at < 0:
            first = HALO - before_ref.shape[0]
            block = jnp.concatenate([jnp.zeros((first, x_ref.shape[1]), f32), before_ref[...].astype(f32)], axis=0)
        else:
            block = x_ref[at : at + HALO, :].astype(f32)
        block = jnp.transpose(block)
        lanes = slice(at + HALO, at + 2 * HALO)
        xt_ref[:, lanes] = block.astype(bf16)
        mean = jnp.mean(block * block, axis=0, keepdims=True)
        scale_ref[:, lanes] = jnp.broadcast_to(lax.rsqrt(mean + eps), (8, HALO))


def prepared(x, before):
    length, features = x.shape
    return call(prep_body, [((features, length + HALO), bf16), ((8, length + HALO), f32)], [], x, before)


def params_body(shape, w_ref, xt_ref, scale_ref, inner_ref, basis_ref, gains_ref, n1_ref):
    ways, rows, inner_rows, bc_rows, heads, step_at = shape
    tail = w_ref[:, step_at:].astype(f32)
    for s in range(ways):
        inner_ref[s * inner_rows : (s + 1) * inner_rows, :] = tail[s * rows : s * rows + inner_rows, :]
        basis_ref[s * bc_rows : (s + 1) * bc_rows, :] = tail[s * rows : s * rows + bc_rows, :]
    gains_ref[...] = jnp.transpose(tail)
    for at in range(0, xt_ref.shape[1], HALO):
        lanes = slice(at, at + HALO)
        normed = xt_ref[:, lanes].astype(f32) * scale_ref[0:1, lanes] * tail[:, heads : heads + 1]
        n1_ref[:, lanes] = normed.astype(bf16)


def unpacked(shape, first_w, xt, scale):
    ways, rows, inner_rows, bc_rows, heads, step_at = shape
    return call(
        functools.partial(params_body, shape),
        [((ways * inner_rows, 128), f32), ((ways * bc_rows, 128), f32), ((128, ways * rows), f32), (xt.shape, bf16)],
        [],
        first_w, xt, scale,
    )


def rope_body(attn_width, lin_ref, cos_ref, sin_ref, q_ref, kv_ref):
    cosine, sine = cos_ref[...], sin_ref[...]
    for at in range(0, attn_width, HEAD_SIZE):
        query = rotated(lin_ref[at : at + HEAD_SIZE, HALO:], cosine, sine)
        q_ref[at : at + HEAD_SIZE, :] = query.astype(bf16) * bf16(HEAD_SIZE**-0.5)
    keys = lin_ref[attn_width : attn_width + HEAD_SIZE, HALO:]
    kv_ref[:HEAD_SIZE, :] = rotated(keys, cosine, sine).astype(bf16)
    kv_ref[HEAD_SIZE:, :] = lin_ref[attn_width + HEAD_SIZE : attn_width + 2 * HEAD_SIZE, HALO:].astype(bf16)


def roped(attn_width, first_lin, cosine, sine):
    length = cosine.shape[1]
    return call(
        functools.partial(rope_body, attn_width),
        [((attn_width, length), bf16), ((2 * HEAD_SIZE, length), bf16)],
        [],
        first_lin, cosine, sine,
    )


def conv_pre(block, taps, places):
    total = None
    for lag in range(KC):
        back = KC - 1 - lag
        moved = pltpu.roll(block, back, 1) if back else block
        term = taps[:, lag : lag + 1] * moved[:, HALO:]
        if back:
            term = jnp.where(places >= back, term, 0.0)
        total = term if total is None else total + term
    return total


def sigmoid(value):
    return 1.0 / (1.0 + jnp.exp(-value))


def running_sum(value, reverse=False):
    width = value.shape[1]
    lane = lax.broadcasted_iota(jnp.int32, value.shape, 1)
    step = 1
    while step < width:
        if reverse:
            value = value + jnp.where(lane < width - step, pltpu.roll(value, width - step, 1), 0.0)
        else:
            value = value + jnp.where(lane >= step, pltpu.roll(value, step, 1), 0.0)
        step *= 2
    return value


def widened(rows):
    return jnp.transpose(jnp.concatenate([rows, jnp.zeros((112, rows.shape[1]), f32)], axis=0))


def pack_decay(ref, decay, first):
    wide = jnp.broadcast_to(decay, (16, DS))
    high = wide.astype(bf16)
    ref[first : first + 16, :] = high
    ref[first + 16 : first + 32, :] = (wide - high.astype(f32)).astype(bf16)


def chain(packs, heads, state_ref):
    width = heads * HEAD_SIZE
    for h in range(heads):
        rows = slice(h * HEAD_SIZE, (h + 1) * HEAD_SIZE)
        state = jnp.zeros((HEAD_SIZE, DS), f32)
        for pack in packs[::-1]:
            decay = pack[width : width + 16, :].astype(f32) + pack[width + 16 : width + 32, :].astype(f32)
            state = pack[rows, :].astype(f32) + decay[h : h + 1, :] * state
        state_ref[rows, :] = state


def conv_body(heads, bc_at, u_ref, lin_ref, inner_ref, basis_ref, hp_ref, place_ref, xs_ref, b_ref, c_ref, bt_ref, ct_ref, dt_ref, cum_ref, cumt_ref, pack_ref, end_ref):
    places = place_ref[0:1, :]
    length = places.shape[1]
    width = heads * HEAD_SIZE
    for at, flat, side in ((0, b_ref, bt_ref), (DS, c_ref, ct_ref)):
        taps = basis_ref[at : at + DS, heads + 3 + KC : heads + 3 + 2 * KC]
        pre = conv_pre(lin_ref[bc_at + at : bc_at + at + DS, :], taps, places)
        basis = pre * sigmoid(pre)
        side[...] = basis
        flat[...] = jnp.transpose(basis)
    raw = lin_ref[bc_at + 2 * DS : bc_at + 2 * DS + 16, HALO:] + hp_ref[:, 0:1]
    dt = jnp.maximum(raw, 0.0) + jnp.log1p(jnp.exp(-jnp.abs(raw)))
    cum = running_sum(dt * -jnp.exp(hp_ref[:, 1:2]))
    dt_ref[...] = dt
    cum_ref[...] = cum
    cumt_ref[...] = widened(cum)
    last = cum[:, length - 1 :]
    lane = lax.broadcasted_iota(jnp.int32, (1, length), 1)
    last_place = places[:, length - 1 :]
    reach = lane >= length - 1 - last_place
    to_end = jnp.where(reach, jnp.exp(jnp.minimum(last - cum, 0.0)) * dt, 0.0)
    end_ref[...] = to_end

    def one(h, _):
        rows = pl.ds(pl.multiple_of(h * HEAD_SIZE, HEAD_SIZE), HEAD_SIZE)
        pre = conv_pre(u_ref[rows, :], inner_ref[rows, :][:, heads + 3 : heads + 3 + KC], places)
        values = pre * sigmoid(pre)
        xs_ref[rows, :] = values
        summary = dot((values * end_ref[pl.ds(h, 1), :]).astype(bf16), low(b_ref[...]), 1, 0)
        pack_ref[rows, :] = summary.astype(bf16)
        return 0

    lax.fori_loop(0, heads, one, 0)
    keep = (last_place > length - 1).astype(f32)
    pack_decay(pack_ref, jnp.exp(last) * keep, width)


def conv_forward(heads, bc_at, u, lin, inner, basis, hp, places):
    length = places.shape[1]
    width = heads * HEAD_SIZE
    return call(
        functools.partial(conv_body, heads, bc_at),
        [
            ((width, length), f32),
            ((length, DS), f32),
            ((length, DS), f32),
            ((DS, length), f32),
            ((DS, length), f32),
            ((16, length), f32),
            ((16, length), f32),
            ((length, 128), f32),
            ((width + 32, DS), bf16),
        ],
        [((16, length), f32)],
        u, lin, inner, basis, hp, places,
    )


def chunk_rows(k, cum_ref, place_ref):
    lanes = slice(k * CHUNK, (k + 1) * CHUNK)
    cum = cum_ref[:, lanes]
    places = place_ref[0:1, lanes]
    base = cum_ref[:, k * CHUNK - 1 : k * CHUNK] if k else jnp.zeros((16, 1), f32)
    last = cum[:, CHUNK - 1 :]
    last_place = places[:, CHUNK - 1 :]
    lane = lax.broadcasted_iota(jnp.int32, (1, CHUNK), 1)
    entry = jnp.where(places > lane, jnp.exp(jnp.minimum(cum - base, 0.0)), 0.0)
    to_end = jnp.where(lane >= CHUNK - 1 - last_place, jnp.exp(jnp.minimum(last - cum, 0.0)), 0.0)
    over = jnp.where(last_place > CHUNK - 1, jnp.exp(jnp.minimum(last - base, 0.0)), 0.0)
    source = lax.broadcasted_iota(jnp.int32, (CHUNK, CHUNK), 0)
    target = lax.broadcasted_iota(jnp.int32, (CHUNK, CHUNK), 1)
    allowed = (source <= target) & (source >= target - places)
    return cum, entry, to_end, over, allowed


def mix_body(heads, packs, xs_ref, b_ref, ct_ref, dt_ref, cum_ref, cumt_ref, hp_ref, place_ref, z_ref, *refs):
    pack_refs = refs[:packs]
    y_ref, states_ref, squares_ref, state_ref, inter_ref, w_ref = refs[packs:]
    length = place_ref.shape[1]
    chain(pack_refs, heads, state_ref)
    for k in range(length // CHUNK):
        lanes = slice(k * CHUNK, (k + 1) * CHUNK)
        cum, entry, to_end, over, allowed = chunk_rows(k, cum_ref, place_ref)
        low_state = state_ref[...].astype(bf16)
        states_ref[k] = low_state
        side = ct_ref[:, lanes]
        match = jnp.where(allowed, exact(b_ref[lanes, :], side, 1, 0), 0.0)
        inter_ref[...] = dot(low_state, low(side), 1, 0)
        squares = jnp.zeros((1, CHUNK), f32)
        for h in range(heads):
            rows = slice(h * HEAD_SIZE, (h + 1) * HEAD_SIZE)
            spread = cum[h : h + 1, :] - cumt_ref[lanes, h : h + 1]
            mixing = (jnp.exp(jnp.minimum(spread, 0.0)) * match).astype(bf16)
            values = xs_ref[rows, lanes]
            stepped = values * dt_ref[h : h + 1, lanes]
            result = dot(stepped.astype(bf16), mixing, 1, 0)
            result = result + inter_ref[rows, :] * entry[h : h + 1, :] + hp_ref[h : h + 1, 2:3] * values
            y_ref[rows, lanes] = result
            w_ref[rows, :] = (stepped * to_end[h : h + 1, :]).astype(bf16)
            gate = z_ref[rows, lanes]
            gated = result * gate * sigmoid(gate)
            squares = squares + jnp.sum(gated * gated, axis=0, keepdims=True)
        squares_ref[:, lanes] = jnp.broadcast_to(squares, (8, CHUNK))
        if k + 1 < length // CHUNK:
            added = dot(w_ref[...], low(b_ref[lanes, :]), 1, 0)
            for h in range(heads):
                rows = slice(h * HEAD_SIZE, (h + 1) * HEAD_SIZE)
                state_ref[rows, :] = over[h : h + 1, :] * state_ref[rows, :] + added[rows, :]


def mix_forward(heads, xs, b, ct, dt, cum, cumt, hp, places, z, packs):
    length = places.shape[1]
    width = heads * HEAD_SIZE
    return call(
        functools.partial(mix_body, heads, len(packs)),
        [
            ((width, length), f32),
            ((length // CHUNK, width, DS), bf16),
            ((8, length), f32),
        ],
        [((width, DS), f32), ((width, CHUNK), f32), ((width, CHUNK), bf16)],
        xs, b, ct, dt, cum, cumt, hp, places, z, *packs,
    )


def gate_body(heads, g_ref, y_ref, z_ref, gain_ref, inv_ref, dot_ref, c_ref, cum_ref, place_ref, gy_ref, gz_ref, ggain_ref, pack_ref, entry_ref):
    length = place_ref.shape[1]
    width = heads * HEAD_SIZE
    first = g_ref.shape[0] - width
    places = place_ref[0:1, :]
    inv = inv_ref[0:1, :]
    shrink = inv * inv * inv * dot_ref[0:1, :] * (1.0 / (HS * HEAD_SIZE))
    lane = lax.broadcasted_iota(jnp.int32, (1, length), 1)
    entry_ref[...] = jnp.where(places > lane, jnp.exp(jnp.minimum(cum_ref[...], 0.0)), 0.0)

    def one(h, _):
        start = pl.multiple_of(h * HEAD_SIZE, HEAD_SIZE)
        rows = pl.ds(start, HEAD_SIZE)
        grad = g_ref[pl.ds(start + first, HEAD_SIZE), :] * inv
        values = y_ref[rows, :]
        gate = z_ref[rows, :]
        sig = sigmoid(gate)
        silu = gate * sig
        gated = values * silu
        column = lax.broadcasted_iota(jnp.int32, (HEAD_SIZE, 128), 1)
        ggain_ref[rows, :] = jnp.where(column == heads + 2, jnp.sum(grad * gated, axis=1, keepdims=True), 0.0)
        grad_gated = grad * gain_ref[rows, :][:, heads + 2 : heads + 3] - shrink * gated
        grad_values = grad_gated * silu
        gy_ref[rows, :] = grad_values
        gz_ref[rows, :] = (grad_gated * values * sig * (1.0 + gate * (1.0 - sig))).astype(bf16)
        entered = (grad_values * entry_ref[pl.ds(h, 1), :]).astype(bf16)
        pack_ref[rows, :] = dot(entered, low(c_ref[...]), 1, 0).astype(bf16)
        return 0

    lax.fori_loop(0, heads, one, 0)
    last = length - 1
    keep = (places[:, last:] > last).astype(f32)
    pack_decay(pack_ref, jnp.exp(cum_ref[:, last:]) * keep, width)


def gate_back(heads, grads, y, z, gain, inv, inner, c, cum, places):
    length = places.shape[1]
    width = heads * HEAD_SIZE
    return call(
        functools.partial(gate_body, heads),
        [
            ((width, length), f32),
            ((width, length), bf16),
            ((width, 128), f32),
            ((width + 32, DS), bf16),
        ],
        [((16, length), f32)],
        grads, y, z, gain, inv, inner, c, cum, places,
    )


def mix_back_body(heads, packs, step_at, gy_ref, xs_ref, b_ref, c_ref, bt_ref, ct_ref, dt_ref, cum_ref, cumt_ref, lin_ref, hp_ref, place_ref, states_ref, *refs):
    pack_refs = refs[:packs]
    gxs_ref, gbc_ref, gstep_ref, grow_ref, ghead_ref, grad_ref, reach_ref, inter_ref, gye_ref, w_ref, col_ref, cumg_ref, dtg_ref = refs[packs:]
    length = place_ref.shape[1]
    chain(pack_refs, heads, grad_ref)
    col_ref[...] = jnp.zeros_like(col_ref)
    cumg_ref[...] = jnp.zeros_like(cumg_ref)
    dtg_ref[...] = jnp.zeros_like(dtg_ref)
    rate = -jnp.exp(hp_ref[:, 1:2])
    bias_sum = jnp.zeros((16, CHUNK), f32)
    rate_sum = jnp.zeros((16, CHUNK), f32)
    ghead_ref[...] = jnp.zeros_like(ghead_ref)
    at_last = lax.broadcasted_iota(jnp.int32, (1, CHUNK), 1) == CHUNK - 1
    for k in reversed(range(length // CHUNK)):
        lanes = slice(k * CHUNK, (k + 1) * CHUNK)
        cum, entry, to_end, over, allowed = chunk_rows(k, cum_ref, place_ref)
        b_side, c_side = bt_ref[:, lanes], ct_ref[:, lanes]
        b_flat, c_flat = b_ref[lanes, :], c_ref[lanes, :]
        match = jnp.where(allowed, exact(b_flat, c_side, 1, 0), 0.0)
        low_grad = grad_ref[...].astype(bf16)
        reach_ref[...] = dot(low_grad, low(b_side), 1, 0)
        inter_ref[...] = dot(states_ref[k], low(c_side), 1, 0)
        grad_match = jnp.zeros((CHUNK, CHUNK), f32)
        for h in range(heads):
            rows = slice(h * HEAD_SIZE, (h + 1) * HEAD_SIZE)
            head = slice(h, h + 1)
            grad = gy_ref[rows, lanes]
            values = xs_ref[rows, lanes]
            dt = dt_ref[head, lanes]
            stepped = values * dt
            decay = jnp.exp(jnp.minimum(cum[head, :] - cumt_ref[lanes, head], 0.0))
            mixing = decay * match
            low_y = grad.astype(bf16)
            grad_mixing = dot(stepped.astype(bf16), low_y, 0, 0)
            grad_match = grad_match + grad_mixing * decay
            spread = grad_mixing * mixing
            to = to_end[head, :]
            reached = reach_ref[rows, :] * to
            grad_stepped = dot(low_y, mixing.astype(bf16), 1, 1) + reached
            ended = jnp.sum(reached * stepped, axis=0, keepdims=True)
            entered = grad * entry[head, :]
            entry_sum = jnp.sum(entered * inter_ref[rows, :], axis=0, keepdims=True)
            kept = over[head, :] * jnp.sum(
                jnp.sum(grad_ref[rows, :] * states_ref[k, rows, :].astype(f32), axis=0, keepdims=True),
                axis=1, keepdims=True,
            )
            at_end = jnp.sum(ended, axis=1, keepdims=True) + kept
            cumg_ref[head, :] = (
                jnp.sum(spread, axis=0, keepdims=True) + entry_sum - ended + jnp.where(at_last, at_end, 0.0)
            )
            col_ref[:, head] = jnp.sum(spread, axis=1, keepdims=True)
            dtg_ref[head, :] = jnp.sum(grad_stepped * values, axis=0, keepdims=True)
            gxs_ref[rows, lanes] = grad_stepped * dt + hp_ref[head, 2:3] * grad
            ghead_ref[head, 2:3] += jnp.sum(
                jnp.sum(grad * values, axis=0, keepdims=True), axis=1, keepdims=True
            )
            gye_ref[rows, :] = entered.astype(bf16)
            w_ref[rows, :] = (stepped * to).astype(bf16)
        low_match = jnp.where(allowed, grad_match, 0.0)
        gbc_ref[:DS, lanes] = exact(c_side, low_match, 1, 1) + dot(low_grad, w_ref[...], 0, 0)
        gbc_ref[DS:, lanes] = exact(b_side, low_match, 1, 0) + dot(states_ref[k], gye_ref[...], 0, 0)
        if k:
            added = dot(gye_ref[...], low(c_flat), 1, 0)
            for h in range(heads):
                rows = slice(h * HEAD_SIZE, (h + 1) * HEAD_SIZE)
                grad_ref[rows, :] = over[h : h + 1, :] * grad_ref[rows, :] + added[rows, :]
        grad_log = running_sum(cumg_ref[...] - jnp.transpose(col_ref[...])[:16, :], reverse=True)
        dt = dt_ref[:, lanes]
        rate_sum = rate_sum + grad_log * dt
        grad_step = (dtg_ref[...] + grad_log * rate) * sigmoid(lin_ref[step_at : step_at + 16, HALO:][:, lanes] + hp_ref[:, 0:1])
        gstep_ref[:, lanes] = grad_step
        bias_sum = bias_sum + grad_step
    ghead_ref[:, 0:1] = jnp.sum(bias_sum, axis=1, keepdims=True)
    ghead_ref[:, 1:2] = jnp.sum(rate_sum, axis=1, keepdims=True) * rate
    side = jnp.transpose(jnp.concatenate([ghead_ref[...], jnp.zeros((112, 128), f32)], axis=0))
    lane = lax.broadcasted_iota(jnp.int32, (8, 128), 1)
    row = jnp.zeros((8, 128), f32)
    for j in range(3):
        own = jnp.where(lane < heads, jnp.broadcast_to(side[j : j + 1, :], (8, 128)), 0.0)
        row = row + pltpu.roll(own, heads + 3 + 2 * KC + j * heads, 1)
    grow_ref[...] = row


def mix_back(heads, step_at, gy, xs, b, c, bt, ct, dt, cum, cumt, lin, hp, places, states, packs):
    length = places.shape[1]
    width = heads * HEAD_SIZE
    return call(
        functools.partial(mix_back_body, heads, len(packs), step_at),
        [
            ((width, length), f32),
            ((2 * DS, length), f32),
            ((16, length), f32),
            ((8, 128), f32),
        ],
        [
            ((16, 128), f32),
            ((width, DS), f32),
            ((width, CHUNK), f32),
            ((width, CHUNK), f32),
            ((width, CHUNK), bf16),
            ((width, CHUNK), bf16),
            ((CHUNK, 128), f32),
            ((16, CHUNK), f32),
            ((16, CHUNK), f32),
        ],
        gy, xs, b, c, bt, ct, dt, cum, cumt, lin, hp, places, states, *packs,
    )


def conv_back_body(heads, bc_at, u_ref, lin_ref, gxs_ref, gbc_ref, inner_ref, basis_ref, place_ref, g_ref, halo_ref, ginner_ref, gbasis_ref):
    places = place_ref[0:1, :]
    length = places.shape[1]
    width = u_ref.shape[0]

    def one(block, grads, taps, first, sums_ref, at):
        pre = conv_pre(block, taps, places)
        sig = sigmoid(pre)
        grad_pre = grads * sig * (1.0 + pre * (1.0 - sig))
        total = None
        for lag in range(KC):
            back = KC - 1 - lag
            counted = jnp.where(places >= back, grad_pre, 0.0) if back else grad_pre
            moved = pltpu.roll(block, back, 1) if back else block
            sums_ref[at, first + lag : first + lag + 1] = jnp.sum(counted * moved[:, HALO:], axis=1, keepdims=True)
            wide = jnp.concatenate([jnp.zeros((counted.shape[0], HALO), f32), counted * taps[:, lag : lag + 1]], axis=1)
            wide = pltpu.roll(wide, length + HALO - back, 1) if back else wide
            total = wide if total is None else total + wide
        return total[:, HALO:], jnp.transpose(total[:, :HALO])[HALO - 8 :, :]

    ginner_ref[...] = jnp.zeros_like(ginner_ref)
    gbasis_ref[...] = jnp.zeros_like(gbasis_ref)

    def inner(i, _):
        start = pl.multiple_of(i * 128, 128)
        rows = pl.ds(start, 128)
        taps = inner_ref[rows, :][:, heads + 3 : heads + 3 + KC]
        own, halo = one(u_ref[rows, :], gxs_ref[rows, :], taps, heads + 3, ginner_ref, rows)
        g_ref[rows, :] = own
        halo_ref[:, pl.ds(start, 128)] = halo
        return 0

    lax.fori_loop(0, width // 128, inner, 0)
    for i in range(0, 2 * DS, 128):
        rows = slice(i, i + 128)
        first = heads + 3 + KC
        block = lin_ref[bc_at + i : bc_at + i + 128, :]
        own, halo = one(block, gbc_ref[rows, :], basis_ref[rows, first : first + KC], first, gbasis_ref, rows)
        g_ref[width + i : width + i + 128, :] = own
        halo_ref[:, width + i : width + i + 128] = halo


def conv_back(heads, bc_at, u, lin, gxs, gbc, inner, basis, places):
    length = places.shape[1]
    width = u.shape[0]
    return call(
        functools.partial(conv_back_body, heads, bc_at),
        [((width + 2 * DS, length), f32), ((8, width + 2 * DS), f32), ((width, 128), f32), ((2 * DS, 128), f32)],
        [],
        u, lin, gxs, gbc, inner, basis, places,
    )


def early_body(pieces, n1_ref, gq_ref, gz_ref, cos_ref, sin_ref, first_ref, z_ref, *refs):
    kv_refs = refs[:pieces]
    gw_ref, gn_ref = refs[pieces:]
    n1 = n1_ref[:, HALO:]
    gkv = kv_refs[0][...].astype(f32)
    for ref in kv_refs[1:]:
        gkv = gkv + ref[...].astype(f32)
    gkv = jnp.concatenate([rotated(gkv[:HEAD_SIZE], cos_ref[...], -sin_ref[...]), gkv[HEAD_SIZE:]], axis=0).astype(bf16)
    at = 0
    total = None
    for grad, weights in ((gz_ref[...], z_ref[...]), (gq_ref[...], first_ref), (gkv, first_ref)):
        rows = grad.shape[0]
        gw_ref[:, at : at + rows] = dot(n1, grad, 1, 1).astype(bf16)
        if weights is first_ref:
            first = at - gz_ref.shape[0]
            weights = first_ref[:, first : first + rows]
        term = dot(weights, grad, 1, 0)
        total = term if total is None else total + term
        at += rows
    gn_ref[...] = total


def rows_call(body, outs, cuts, *args):
    blocks = 4

    def spec(shape, cut=0):
        if cut is None:
            return pl.BlockSpec(shape, lambda i: (0,) * len(shape))
        if cut == 1:
            return pl.BlockSpec((shape[0], shape[1] // blocks), lambda i: (0, i))
        return pl.BlockSpec((shape[0] // blocks, cut or shape[1]), lambda i: (i, 0))

    return pl.pallas_call(
        body,
        grid=(blocks,),
        out_shape=[jax.ShapeDtypeStruct(s, d) for s, d in outs],
        in_specs=[spec(a.shape, cut) for a, cut in zip(args, cuts, strict=True)],
        out_specs=[spec(s) for s, _ in outs],
        compiler_params=pltpu.CompilerParams(vmem_limit_bytes=VMEM_LIMIT),
        cost_estimate=pl.CostEstimate(flops=1000, bytes_accessed=1000, transcendentals=0),
    )(*args)


def early_products(n1, gq, gz, cosine, sine, first_w, last_w, gkv):
    features, length = n1.shape[0], gq.shape[1]
    columns = gq.shape[0] + gkv[0].shape[0] + gz.shape[0]
    return rows_call(
        functools.partial(early_body, len(gkv)),
        [((features, columns), bf16), ((features, length), f32)],
        (0, None, None, None, None, 0, gz.shape[0]) + (None,) * len(gkv),
        n1, gq, gz, cosine, sine, first_w, last_w, *gkv,
    )


def join_body(width, heads, g_ref, behind_ref, step_ref, low_ref):
    length = g_ref.shape[1]
    if length > 128:
        low_ref[: g_ref.shape[0], : length - 128] = g_ref[:, : length - 128].astype(bf16)
    behind = jnp.concatenate([jnp.zeros((120, behind_ref.shape[1]), f32), behind_ref[...]], axis=0)
    low_ref[: g_ref.shape[0], length - 128 :] = (g_ref[:, length - 128 :] + jnp.transpose(behind)).astype(bf16)
    row = lax.broadcasted_iota(jnp.int32, (16, length), 0)
    step = jnp.where(row < heads, step_ref[...], 0.0)
    low_ref[g_ref.shape[0] :, :] = jnp.concatenate([step, jnp.zeros((112, length), f32)], axis=0).astype(bf16)


def joined(heads, grads, behind, step):
    rows, length = grads.shape
    return call(functools.partial(join_body, rows, heads), [((rows + 128, length), bf16)], [], grads, behind, step)[0]


def late_body(shape, width, rest_at, n1_ref, xt_ref, scale_ref, g_ref, first_ref, u_ref, gn_ref, two_ref, inner_a_ref, inner_b_ref, basis_ref, head_ref, loss_ref, gw_ref, total_ref, low_ref, tail_ref):
    rows, inner_rows, bc_rows, heads = shape
    grad = g_ref[...]
    columns = grad.shape[0]
    made = dot(n1_ref[:, HALO:], grad, 1, 1)
    gw_ref[:, : columns - 128] = made[:, : columns - 128].astype(bf16)
    total = gn_ref[...] + dot(u_ref[...], grad[:width], 1, 0) + dot(first_ref[:, rest_at:], grad[width:], 1, 0)
    total_ref[...] = total
    low_ref[...] = total.astype(bf16)
    scaled = xt_ref[:, HALO:].astype(f32) * scale_ref[0:1, HALO:]
    column = lax.broadcasted_iota(jnp.int32, tail_ref.shape, 1)
    one = jnp.sum(total * scaled, axis=1, keepdims=True)
    two = jnp.concatenate([two_ref[...], jnp.zeros((120, two_ref.shape[1]), f32)], axis=0)
    two = jnp.transpose(two)[:, 0:1]
    tail_ref[...] = made[:, columns - 128 :] + jnp.where(column == heads, one, jnp.where(column == heads + 1, two, 0.0))
    for s in range(tail_ref.shape[0] // rows):
        inner = slice(s * inner_rows, (s + 1) * inner_rows)
        tail_ref[s * rows : s * rows + inner_rows, :] += inner_a_ref[inner, :] + inner_b_ref[inner, :]
        tail_ref[s * rows : s * rows + bc_rows, :] += basis_ref[s * bc_rows : (s + 1) * bc_rows, :]
        tail_ref[s * rows : s * rows + 1, :] += head_ref[0:1, :] + loss_ref[0:1, :]
    value = tail_ref[...]
    high = value.astype(bf16).astype(f32)
    rest = pltpu.roll(value - high, 64, 1)
    gw_ref[:, columns - 128 :] = jnp.where(column < 64, high, jnp.where(column < 64 + heads, 0.0, rest)).astype(bf16)


def late_products(shape, width, rest_at, n1, xt, scale, grads, first_w, u_w, gn, two, inner_a, inner_b, basis, head, loss):
    features, length = gn.shape
    return rows_call(
        functools.partial(late_body, shape, width, rest_at),
        [((features, grads.shape[0]), bf16), ((features, length), f32), ((features, length), bf16), ((features, 128), f32)],
        (0, 0, None, None, 0, 0, 0, 1, 0, 0, 0, None, None),
        n1, xt, scale, grads, first_w, u_w, gn, two, inner_a, inner_b, basis, head, loss,
    )[:3]


def finish_body(shape, total_ref, other_ref, count_ref, bc_ref, norm_ref, step_ref, ssm_ref, two_ref, inner_ref, basis_ref, head_ref, loss_ref):
    rows, inner_rows, bc_rows, heads, bc_at = shape
    bc_width = bc_ref.shape[1]
    bc_ref[...] = total_ref[:, bc_at : bc_at + bc_width] + other_ref[:, :bc_width]
    tail = total_ref[:, bc_at + bc_width :]
    own = jnp.where(lax.broadcasted_iota(jnp.int32, tail.shape, 1) < heads, tail, tail + pltpu.roll(tail, 64, 1))
    step_ref[...] = own[:, :heads]
    other = other_ref[:, bc_width:]
    both = own + other + pltpu.roll(other, 64, 1)
    own = jnp.concatenate([own, jnp.zeros((128 - rows, 128), f32)], axis=0) if rows < 128 else own
    both = jnp.concatenate([both, jnp.zeros((128 - rows, 128), f32)], axis=0) if rows < 128 else both
    side, side_both = jnp.transpose(own), jnp.transpose(both)
    norm_ref[...] = side_both[heads : heads + 1, :rows]
    two_ref[...] = side[heads + 1 : heads + 2, :rows]
    ssm_ref[...] = side[heads + 2 : heads + 3, :inner_rows]
    inner_ref[...] = side[heads + 3 : heads + 3 + KC, :inner_rows]
    basis_ref[...] = side_both[heads + 3 + KC : heads + 3 + 2 * KC, :bc_rows]
    at = heads + 3 + 2 * KC
    for j in range(3):
        head_ref[j : j + 1, :] = own[0:1, at + j * heads : at + (j + 1) * heads]
    loss_ref[...] = own[0:1, at + 3 * heads : at + 3 * heads + 1] / (count_ref[0:1, 0:1] * MODEL_WIDTH)


def finished(shape, total, other, count):
    rows, inner_rows, bc_rows, heads, _ = shape
    return call(
        functools.partial(finish_body, shape),
        [
            ((rows, 2 * DS), f32),
            ((1, rows), f32),
            ((rows, heads), f32),
            ((1, inner_rows), f32),
            ((1, rows), f32),
            ((KC, inner_rows), f32),
            ((KC, bc_rows), f32),
            ((3, heads), f32),
            ((1, 1), f32),
        ],
        [],
        total, other, count,
    )


def input_body(own_ref, low_ref, x_ref, res_ref, gain_ref, out_ref):
    length = x_ref.shape[0]
    for at in range(0, length, HALO):
        rows = slice(at, at + HALO)
        grad = jnp.transpose(own_ref[:, rows] + low_ref[:, rows].astype(f32)) * gain_ref[0:1, :]
        x = x_ref[rows, :].astype(f32)
        scale = lax.rsqrt(jnp.mean(x * x, axis=1, keepdims=True) + eps)
        inner = jnp.mean(grad * x, axis=1, keepdims=True)
        out_ref[rows, :] = res_ref[rows, :] + scale * grad - scale * scale * scale * x * inner


def input_grad(own, low, x, res, gain):
    return call(input_body, [(x.shape, f32)], [], own, low, x, res, gain)[0]


def mlp_grads_body(n2_ref, e_ref, ggu_ref, m_ref, out_ref):
    both = ggu_ref.shape[1]
    out_ref[:, :both] = dot(n2_ref[...], ggu_ref[...], 0, 0).astype(bf16)
    out_ref[:, both:] = dot(e_ref[...], m_ref[...], 0, 0).astype(bf16)


def mlp_weight_grads(n2, e, ggu, m):
    length, features = n2.shape
    blocks = 4
    columns = ggu.shape[1] + m.shape[1]
    cut = pl.BlockSpec((length, features // blocks), lambda i: (0, i))
    return pl.pallas_call(
        mlp_grads_body,
        grid=(blocks,),
        out_shape=jax.ShapeDtypeStruct((features, columns), bf16),
        in_specs=[cut, cut, pl.BlockSpec(ggu.shape, lambda i: (0, 0)), pl.BlockSpec(m.shape, lambda i: (0, 0))],
        out_specs=pl.BlockSpec((features // blocks, columns), lambda i: (i, 0)),
        compiler_params=pltpu.CompilerParams(vmem_limit_bytes=VMEM_LIMIT),
        cost_estimate=pl.CostEstimate(flops=1000, bytes_accessed=1000, transcendentals=0),
    )(n2, e, ggu, m)


def residual_body(own_ref, low_ref, res_ref, gf_ref, gain_ref, out_ref, ea_ref, ggain_ref):
    total = jnp.zeros((1, res_ref.shape[1]), f32)
    for at in range(0, res_ref.shape[0], HALO):
        rows = slice(at, at + HALO)
        grad = own_ref[rows, :] + low_ref[rows, :].astype(f32)
        res = res_ref[rows, :]
        scale = lax.rsqrt(jnp.mean(res * res, axis=1, keepdims=True) + eps)
        total = total + jnp.sum(grad * (res * scale), axis=0, keepdims=True)
        grad = grad * gain_ref[0:1, :]
        inner = jnp.mean(grad * res, axis=1, keepdims=True)
        grad = gf_ref[rows, :] + scale * grad - scale * scale * scale * res * inner
        out_ref[rows, :] = grad
        ea_ref[rows, :] = grad.astype(bf16)
    ggain_ref[...] = jnp.broadcast_to(total, ggain_ref.shape)


def residual_back(own, low, res, gf, gain):
    return call(
        residual_body, [(res.shape, f32), (res.shape, bf16), ((8, res.shape[1]), f32)], [], own, low, res, gf, gain
    )


def rms_scale(values):
    return lax.rsqrt(jnp.mean(values * values, axis=-1, keepdims=True) + eps)


def norm_back(inputs, inv_rms, grad_normed):
    inner_mean = jnp.mean(grad_normed * inputs, axis=-1, keepdims=True)
    return inv_rms * grad_normed - inv_rms * inv_rms * inv_rms * inputs * inner_mean


def padded_rows(block, rows):
    return jnp.pad(block, ((0, rows - block.shape[0]), (0, 0)))


def shards(
    hidden,
    teacher,
    positions,
    valid_mask,
    norm_gain,
    w_query,
    key_value_weight,
    w_gatein,
    w_bc,
    w_step,
    ssm_gain,
    mlp_gain,
    w_gateup,
    w_out_attn,
    w_out_ssm,
    w_down,
    conv_inner,
    conv_bc,
    head_params,
):
    ways = lax.axis_size(("fsdp", "ctx"))
    blocks = lax.axis_size("ctx")
    rows = norm_gain.shape[0]
    length = hidden.shape[1]
    heads = w_step.shape[1]
    width = heads * HEAD_SIZE
    attn_width = w_query.shape[1]
    kv_width = key_value_weight.shape[2]
    ff_local = w_down.shape[0]
    inner_rows = ssm_gain.shape[0]
    bc_rows = conv_bc.shape[1]
    qkv_width = attn_width + 2 * kv_width
    step_at = qkv_width + 2 * DS

    live_rows = valid_mask.reshape(length, 1).astype(f32)
    count_at = heads + 3 + 2 * KC
    first_shard = packed(
        w_query,
        key_value_weight.reshape(rows, 2 * kv_width),
        w_bc,
        w_step,
        jnp.stack([norm_gain, mlp_gain]),
        ssm_gain[None],
        conv_inner,
        conv_bc,
        valid_mask,
    )
    mlp_shard = jnp.concatenate([w_gateup.reshape(rows, 2 * ff_local), w_down.T], axis=1)
    u_shard = w_gatein[:, 1]
    last_shard = jnp.concatenate([w_gatein[:, 0], jnp.concatenate([w_out_attn, w_out_ssm], axis=0).T], axis=1)

    flat_in = hidden.reshape(length, MODEL_WIDTH)
    first_line = gathered_line(first_shard, False)
    before = passed_along(flat_in[length - 16 :], "ctx", 1)
    u_shard, first_line = tied(u_shard, first_line)
    u_line = gathered_line(u_shard)
    first_w = gathered_plane(first_line)
    mlp_w = lax.all_gather(mlp_shard, ("fsdp", "ctx"), axis=0, tiled=True)

    places = positions.reshape(1, length)
    place_rows = jnp.broadcast_to(places, (8, length))
    low_rows = jnp.broadcast_to(jnp.arange(length, dtype=jnp.int32)[None] - places, (8, length))
    half = HEAD_SIZE // 2
    frequency = rope_base ** (-2.0 * jnp.arange(half, dtype=f32) / HEAD_SIZE)
    angle = frequency[:, None] * places.astype(f32)
    cosine, sine = jnp.cos(angle), jnp.sin(angle)
    hp = jnp.pad(head_params.T, ((0, 16 - heads), (0, 125)))
    xt, scale_one = prepared(flat_in, before)
    xt, scale_one, cosine, sine, hp, first_w = lax.optimization_barrier((xt, scale_one, cosine, sine, hp, first_w))

    shape = (ways, rows, inner_rows, bc_rows, heads, step_at)
    par_inner, par_basis, param_rows, n1 = unpacked(shape, first_w, xt, scale_one)
    total_count = jnp.sum(param_rows[count_at]) * 16.0 + jnp.sum(param_rows[count_at + 1])
    gain_ssm = par_inner[:, heads + 2 : heads + 3]
    gain_two = param_rows[heads + 1 : heads + 2]
    gain_two_rows = jnp.broadcast_to(gain_two, (8, MODEL_WIDTH))

    first_lin = dot(first_w, n1, 0, 0)
    query, kv_own = roped(attn_width, first_lin, cosine, sine)
    last_shard, kv_own = tied(last_shard, kv_own)
    last_line = gathered_line(last_shard)
    kv = [kv_own] + [passed_along(kv_own, "ctx", s) for s in range(1, blocks)]
    u_w = gathered_plane(u_line)
    attn, log_total = attend(query, low_rows, kv)
    u_w, attn = tied(u_w, attn)
    u_in = dot(u_w, n1, 0, 0)

    xs, b_flat, c_flat, b_side, c_side, dt, cum, cumt, pack = conv_forward(
        heads, qkv_width, u_in, first_lin, par_inner, par_basis, hp, place_rows
    )
    packs = [passed_along(pack, "ctx", s) for s in range(1, blocks)]
    last_w = gathered_plane(last_line)
    last_w, packs = tied(last_w, packs)
    z_w, out_w = last_w[:, :width], last_w[:, width:]
    gateup_w, down_w = mlp_w[:, : 2 * ff_local], mlp_w[:, 2 * ff_local :]
    gate_z = dot(z_w, n1[:, HALO:], 0, 0)
    ssm, states, squares = mix_forward(heads, xs, b_flat, c_side, dt, cum, cumt, hp, place_rows, gate_z, packs)
    inv_ssm = lax.rsqrt((squares + swapped(squares)) / (HS * HEAD_SIZE) + eps)
    gated = ssm * jax.nn.silu(gate_z)
    branches = jnp.concatenate([attn, (gated * gain_ssm * inv_ssm[0:1]).astype(bf16)], axis=0)
    part = dot(branches, out_w, 0, 1)
    residual = flat_in.astype(f32) + (part + swapped(part.astype(bf16)).astype(f32))

    scale_two = rms_scale(residual)
    normed_two = (residual * scale_two * gain_two).astype(bf16)
    gateup = dot(normed_two, gateup_w, 1, 0)
    gate_part, up_part = gateup[:, :ff_local], gateup[:, ff_local:]
    hidden_mlp = (jax.nn.silu(gate_part) * up_part).astype(bf16)
    part = dot(hidden_mlp, down_w, 1, 1)
    final_rows = residual + (part + swapped(part.astype(bf16)).astype(f32))
    difference = (final_rows - teacher.reshape(length, MODEL_WIDTH).astype(f32)) * live_rows
    local_sq = jnp.sum(difference * difference)

    all_tokens = length * ways
    grad_final = difference * (all_tokens / total_count)
    grad_low = grad_final.astype(bf16)
    grad_hidden_mlp = dot(grad_low, down_w, 1, 0)
    sigma = jax.nn.sigmoid(gate_part)
    grad_gate = grad_hidden_mlp * up_part * sigma * (1.0 + gate_part * (1.0 - sigma))
    grad_up = grad_hidden_mlp * gate_part * sigma
    grad_gateup = jnp.concatenate([grad_gate, grad_up], axis=-1).astype(bf16)
    part = dot(grad_gateup, gateup_w, 1, 1)
    low_part, grad_gateup = tied(part.astype(bf16), grad_gateup)
    loss_lane = heads + 3 + 2 * KC + 3 * heads
    loss_row = jnp.where(lax.broadcasted_iota(jnp.int32, (8, 128), 1) == loss_lane, local_sq, 0.0)
    mlp_grads = mlp_weight_grads(normed_two, grad_low, grad_gateup, hidden_mlp)
    mlp_out = lax.psum_scatter(mlp_grads, "fsdp", scatter_dimension=0, tiled=True)
    grad_residual, grad_out, grad_gain_two = residual_back(part, swapped(low_part), residual, grad_final, gain_two_rows)

    grad_branches = dot(out_w, grad_out, 0, 1)
    grad_attn = grad_branches[:attn_width].astype(bf16)
    inner = jnp.sum(grad_branches[attn_width:] * gated * gain_ssm, axis=0, keepdims=True)
    inner = jnp.broadcast_to(inner, (8, length))
    inner = inner + swapped(inner)
    gy, grad_z, grad_gain_ssm, back_pack = gate_back(
        heads, grad_branches, ssm, gate_z, par_inner, inv_ssm, inner, c_flat, cum, place_rows
    )
    out_partial = dot(grad_out, branches, 0, 1).astype(bf16)
    grad_attn, out_partial, back_pack = tied(grad_attn, out_partial, back_pack)
    back_packs = [passed_along(back_pack, "ctx", -s) for s in range(1, blocks)]
    out_parts = scatter_first(out_partial)
    grad_query, *grad_kv = attend_back(query, low_rows, attn, log_total, grad_attn, cosine, sine, kv)
    back_packs, out_parts, grad_kv = lax.optimization_barrier((back_packs, out_parts, grad_kv))
    returned = [passed_along(grad_kv[s], "ctx", -s) for s in range(1, blocks)]
    out_parts = scatter_second(out_parts)
    grad_xs, grad_basis, grad_step, grad_head = mix_back(
        heads, step_at, gy, xs, b_flat, c_flat, b_side, c_side, dt, cum, cumt, first_lin, hp, place_rows, states, back_packs
    )
    *grad_kv, grad_xs = tied(grad_kv[0], *returned, grad_xs)
    early_w, grad_first = early_products(n1, grad_query, grad_z, cosine, sine, first_w, last_w, grad_kv)
    grad_xs, early_w = tied(grad_xs, early_w)
    early_parts = scatter_first(early_w)
    grad_conv, halo, grad_inner, grad_bc_taps = conv_back(
        heads, qkv_width, u_in, first_lin, grad_xs, grad_basis, par_inner, par_basis, place_rows
    )
    halo, mlp_out = tied(halo, mlp_out)
    mlp_out = lax.psum_scatter(mlp_out, "ctx", scatter_dimension=0, tiled=True)
    behind = passed_along(halo, "ctx", -1)
    behind, early_parts, out_parts = tied(behind, early_parts, out_parts)
    early_parts = scatter_second(early_parts)
    grad_late = joined(heads, grad_conv, behind, grad_step)
    late_w, grad_normed, low_normed = late_products(
        shape[1:-1], width, qkv_width, n1, xt, scale_one, grad_late, first_w, u_w, grad_first,
        grad_gain_two, grad_gain_ssm, grad_inner, grad_bc_taps, grad_head, loss_row,
    )
    gain_one = jnp.broadcast_to(param_rows[heads : heads + 1], (8, MODEL_WIDTH))
    late_w, low_normed, early_parts, out_parts = tied(late_w, low_normed, early_parts, out_parts)
    late_parts = scatter_first(late_w, heads)
    inner_kept, inner_other = halved([*early_parts, *out_parts])
    grad_input = input_grad(grad_normed, swapped(low_normed), flat_in, grad_residual, gain_one)
    gateup_out = mlp_out[:, : 2 * ff_local].astype(f32).reshape(rows, 2, ff_local)
    down_out = mlp_out[:, 2 * ff_local :].astype(f32).T
    late_parts, grad_input, gateup_out, down_out = tied(late_parts, grad_input, gateup_out, down_out)
    late_parts = scatter_second(late_parts, heads)
    late_parts, inner_other = tied(late_parts, inner_other)
    inner_parts = halved_on(inner_kept, inner_other)
    out_at = width + attn_width + 2 * kv_width
    query_out = inner_parts[:, width : width + attn_width]
    kv_out = inner_parts[:, width + attn_width : out_at].reshape(rows, 2, kv_width)
    attn_out = inner_parts[:, out_at : out_at + attn_width].T
    ssm_out = inner_parts[:, out_at + attn_width :].T
    late_out = scatter_third(late_parts)
    count_row = jnp.full((8, 128), total_count, f32)
    bc_out, norm_out, step_out, ssm_gain_out, mlp_gain_out, inner_out, basis_out, head_out, loss_value = finished(
        (rows, inner_rows, bc_rows, heads, width), late_out, swapped(late_out[:, width:]), count_row
    )
    return (
        final_rows.astype(bf16).reshape(1, length, MODEL_WIDTH),
        loss_value.reshape(()),
        grad_input.reshape(1, length, MODEL_WIDTH),
        norm_out.reshape(rows),
        query_out,
        kv_out,
        jnp.stack([inner_parts[:, :width], late_out[:, :width]], axis=1),
        bc_out,
        step_out,
        ssm_gain_out.reshape(inner_rows),
        mlp_gain_out.reshape(rows),
        gateup_out,
        attn_out,
        ssm_out,
        down_out,
        inner_out,
        basis_out,
        head_out,
    )


def solution(mesh):
    placed = (
        P("fsdp", "ctx", None),
        P("fsdp", "ctx", None),
        P("fsdp", "ctx"),
        P("fsdp", "ctx"),
        P(("fsdp", "ctx")),
        P(("fsdp", "ctx"), "tp"),
        P(("fsdp", "ctx"), None, "tp"),
        P(("fsdp", "ctx"), None, "tp"),
        P(("fsdp", "ctx"), None),
        P(("fsdp", "ctx"), "tp"),
        P(("tp", "fsdp", "ctx")),
        P(("fsdp", "ctx")),
        P(("fsdp", "ctx"), None, "tp"),
        P("tp", ("fsdp", "ctx")),
        P("tp", ("fsdp", "ctx")),
        P("tp", ("fsdp", "ctx")),
        P(None, ("tp", "fsdp", "ctx")),
        P(None, ("fsdp", "ctx")),
        P(None, "tp"),
    )
    return jax.shard_map(
        shards,
        mesh=mesh,
        in_specs=placed,
        out_specs=(
            P("fsdp", "ctx", None),
            P(),
            P("fsdp", "ctx", None),
            P(("fsdp", "ctx")),
            P(("fsdp", "ctx"), "tp"),
            P(("fsdp", "ctx"), None, "tp"),
            P(("fsdp", "ctx"), None, "tp"),
            P(("fsdp", "ctx"), None),
            P(("fsdp", "ctx"), "tp"),
            P(("tp", "fsdp", "ctx")),
            P(("fsdp", "ctx")),
            P(("fsdp", "ctx"), None, "tp"),
            P("tp", ("fsdp", "ctx")),
            P("tp", ("fsdp", "ctx")),
            P("tp", ("fsdp", "ctx")),
            P(None, ("tp", "fsdp", "ctx")),
            P(None, ("fsdp", "ctx")),
            P(None, "tp"),
        ),
        check_vma=False,
    )
```

```python
import functools

import jax
import jax.numpy as jnp
from jax import lax
from jax.experimental import pallas as pl
from jax.experimental.pallas import tpu as pltpu
from jax.sharding import PartitionSpec as P

MODEL_WIDTH = 1024
HEAD_SIZE = 64
HS = 24
DS = 128
KC = 4

eps = 1e-05
rope_base = 100000000000.0
masked_score = -1e30
f32 = jnp.float32
bf16 = jnp.bfloat16
CHUNK = 128
HALO = 128
VMEM_LIMIT = 40 * 2**20


def dot(left, right, left_dim, right_dim, precision=None):
    return lax.dot_general(
        left, right, (((left_dim,), (right_dim,)), ((), ())), precision=precision, preferred_element_type=f32
    )


def exact(left, right, left_dim, right_dim):
    return dot(left, right, left_dim, right_dim, lax.Precision.HIGHEST)


def low(value):
    return value.astype(bf16)


def factors():
    fsdp = lax.axis_size("fsdp")
    side = int(round(fsdp**0.5))
    if side * side != fsdp:
        side = 1
    return (
        ("fsdp", fsdp // side, side),
        ("fsdp", side, 1),
        ("ctx", lax.axis_size("ctx"), 1),
    )


def coordinate(dim):
    axis, size, stride = dim
    return lax.rem(lax.axis_index(axis) // stride, size)


def shifted(value, dim, step):
    axis, size, stride = dim
    pairs = []
    for source in range(lax.axis_size(axis)):
        at = source // stride % size
        pairs.append((source, source + ((at + step) % size - at) * stride))
    return lax.ppermute(value, axis, pairs)


def passed_along(value, axis, steps):
    count = lax.axis_size(axis)
    pairs = [(s, s + steps) for s in range(count) if 0 <= s + steps < count]
    return lax.ppermute(value, axis, pairs)


def swapped(value):
    return lax.ppermute(value, "tp", [(0, 1), (1, 0)])


def gathered_along(value, dim):
    size = dim[1]
    if size == 1:
        return value[None]
    at = coordinate(dim)
    if size == 2:
        other = shifted(value, dim, 1)
        return jnp.where(at == 0, jnp.stack([value, other]), jnp.stack([other, value]))
    pieces = [value] + [shifted(value, dim, s) for s in range(1, size)]
    ring = jnp.stack((pieces[::-1]) * 2)
    return lax.dynamic_slice_in_dim(ring, size - 1 - at, size, 0)


def tied(*values):
    return lax.optimization_barrier(values)


def gathered_line(shard, doubling=True):
    zdim = factors()[2]
    size = zdim[1]
    if not doubling or size & (size - 1):
        return gathered_along(shard, zdim)
    at = coordinate(zdim)
    value = shard[None]
    step = 1
    while step < size:
        other = lax.ppermute(value, zdim[0], [(i, i ^ step) for i in range(size)])
        pair = (jnp.concatenate([value, other]), jnp.concatenate([other, value]))
        value = jnp.where(at // step % 2 == 0, *pair)
        step *= 2
    return value


def plane_first(line):
    ydim, xdim, _ = factors()
    half = line.shape[-1] // 256 * 128
    return gathered_along(line[..., :half], ydim), gathered_along(line[..., half:], xdim)


def plane_second(one, two):
    ydim, xdim, _ = factors()
    one = jnp.swapaxes(gathered_along(one, xdim), 0, 1)
    two = gathered_along(two, ydim)
    whole = jnp.concatenate([one, two], axis=-1)
    return whole.reshape(-1, whole.shape[-1])


def gathered_plane(line):
    return plane_second(*plane_first(line))


def in_pair(value, kept):
    body, tail = value[..., :-128], value[..., -128:]
    whole = tail + jnp.roll(tail, 64, axis=-1)
    high = lax.reduce_precision(whole, 8, 7)
    rest = (whole - high).astype(bf16)
    high = high.astype(bf16)
    column = lax.broadcasted_iota(jnp.int32, tail.shape, tail.ndim - 1)
    tail = jnp.where(column < kept, tail.astype(bf16), jnp.where(column < 64, high, rest))
    return jnp.concatenate([body.astype(bf16), tail], axis=-1)


def reduced_along(value, dim, front, kept=None):
    size = dim[1]
    if size == 1:
        return lax.index_in_dim(value, 0, front, False)
    at = coordinate(dim)
    total = lax.dynamic_index_in_dim(value, at, front, False).astype(f32)
    for step in range(1, size):
        piece = lax.dynamic_index_in_dim(value, lax.rem(at + step, size), front, False)
        total = total + shifted(piece, dim, step).astype(f32)
    return total.astype(bf16) if kept is None else in_pair(total, kept)


def scatter_first(partial, kept=None):
    ydim, xdim, zdim = factors()
    columns = partial.shape[1]
    blocks = partial.reshape(ydim[1], xdim[1], zdim[1], -1, columns)
    half = columns // 256 * 128
    return reduced_along(blocks[..., :half], xdim, 1), reduced_along(blocks[..., half:], ydim, 0, kept)


def scatter_second(parts, kept=None):
    ydim, xdim, _ = factors()
    return reduced_along(parts[0], ydim, 0), reduced_along(parts[1], xdim, 0, kept)


def exchanged(blocks, step):
    zdim = factors()[2]
    upper = coordinate(zdim) // step % 2 == 1
    halves = blocks.reshape(2, step, *blocks.shape[1:])
    kept = jnp.where(upper, halves[1], halves[0])
    sent = jnp.where(upper, halves[0], halves[1])
    return kept, lax.ppermute(sent, zdim[0], [(i, i ^ step) for i in range(zdim[1])])


def halved(parts):
    blocks = jnp.concatenate(parts, axis=-1)
    return exchanged(blocks, blocks.shape[0] // 2)


def halved_on(kept, other):
    while True:
        total = kept.astype(f32) + other.astype(f32)
        if total.shape[0] == 1:
            return total[0]
        kept, other = exchanged(total.astype(bf16), total.shape[0] // 2)


def scatter_third(parts):
    zdim = factors()[2]
    blocks = jnp.concatenate(parts, axis=-1)
    at = coordinate(zdim)
    total = lax.dynamic_index_in_dim(blocks, at, 0, False).astype(f32)
    for step in range(1, zdim[1]):
        piece = lax.dynamic_index_in_dim(blocks, lax.rem(at + step, zdim[1]), 0, False)
        total = total + shifted(piece, zdim, step).astype(f32)
    return total


COSTS = {"prep_body": 1, "params_body": 1, "rope_body": 1, "attend_body": 9, "attend_back_body": 14, "conv_body": 7, "mix_body": 3,
    "gate_body": 3, "mix_back_body": 13, "conv_back_body": 8, "residual_body": 2, "input_body": 2}


def call(body, outs, scratch, *args):
    name = getattr(body, "func", body).__name__
    return pl.pallas_call(
        body,
        out_shape=[jax.ShapeDtypeStruct(s, d) for s, d in outs],
        in_specs=[pl.BlockSpec(memory_space=pltpu.VMEM)] * len(args),
        out_specs=[pl.BlockSpec(memory_space=pltpu.VMEM)] * len(outs),
        scratch_shapes=[pltpu.VMEM(s, d) for s, d in scratch],
        compiler_params=pltpu.CompilerParams(vmem_limit_bytes=VMEM_LIMIT),
        cost_estimate=pl.CostEstimate(flops=COSTS.get(name, 1) * 10**9, bytes_accessed=1000, transcendentals=0),
    )(*args)


def rotated(block, cosine, sine):
    half = block.shape[0] // 2
    one, two = block[:half], block[half:]
    return jnp.concatenate([one * cosine - two * sine, two * cosine + one * sine], axis=0)


def flipped(block):
    return jnp.transpose(block.astype(f32)).astype(block.dtype)


def block_scores(keys, query, low, at, back, width):
    scores = dot(keys, query, 1, 0)
    place = lax.broadcasted_iota(jnp.int32, scores.shape, 0) - back
    allowed = place >= low
    if back == 0:
        token = at + lax.broadcasted_iota(jnp.int32, scores.shape, 1)
        allowed = allowed & (place <= token)
    return jnp.where(allowed, scores, masked_score)


def attend_body(blocks, heads, q_ref, low_ref, *refs):
    kv = refs[:blocks]
    out_ref, log_ref, key_ref, score_ref = refs[blocks:]
    length = q_ref.shape[1]
    width = min(256, length)
    for j in range(blocks):
        key_ref[j] = flipped(kv[j][:HEAD_SIZE, :])

    @pl.loop(0, heads)
    def _(h):
        rows = pl.ds(pl.multiple_of(h * HEAD_SIZE, HEAD_SIZE), HEAD_SIZE)
        for at in range(0, length, width):
            lanes = slice(at, at + width)
            query = q_ref[rows, lanes]
            low = low_ref[0:1, lanes]
            top = jnp.full((1, width), masked_score, f32)
            for j in range(blocks):
                scores = block_scores(key_ref[j], query, low, at, j * length, width)
                score_ref[j] = scores
                top = jnp.maximum(top, jnp.max(scores, axis=0, keepdims=True))
            total = jnp.zeros((1, width), f32)
            mixed = jnp.zeros((HEAD_SIZE, width), f32)
            for j in range(blocks):
                weight = jnp.exp(score_ref[j] - top)
                total = total + jnp.sum(weight, axis=0, keepdims=True)
                mixed = mixed + dot(kv[j][HEAD_SIZE:, :], weight.astype(bf16), 1, 0)
            out_ref[rows, lanes] = (mixed / total).astype(bf16)
            log_ref[h, :, lanes] = jnp.broadcast_to(top + jnp.log(total), (8, width))


def attend(query, low, kv):
    heads, length = query.shape[0] // HEAD_SIZE, query.shape[1]
    width = min(256, length)
    return call(
        functools.partial(attend_body, len(kv), heads),
        [(query.shape, bf16), ((heads, 8, length), f32)],
        [((len(kv), length, HEAD_SIZE), bf16), ((len(kv), length, width), f32)],
        query, low, *kv,
    )


def attend_back_body(blocks, heads, q_ref, low_ref, out_ref, log_ref, g_ref, cos_ref, sin_ref, *refs):
    kv = refs[:blocks]
    gq_ref = refs[blocks]
    gkv = refs[blocks + 1 : 2 * blocks + 1]
    key_ref, value_ref, sum_ref = refs[2 * blocks + 1 :]
    length = q_ref.shape[1]
    width = min(256, length)
    for j in range(blocks):
        key_ref[j] = flipped(kv[j][:HEAD_SIZE, :])
        value_ref[j] = flipped(kv[j][HEAD_SIZE:, :])
    sum_ref[...] = jnp.zeros_like(sum_ref)

    @pl.loop(0, heads)
    def _(h):
        rows = pl.ds(pl.multiple_of(h * HEAD_SIZE, HEAD_SIZE), HEAD_SIZE)
        for at in range(0, length, width):
            lanes = slice(at, at + width)
            query = q_ref[rows, lanes]
            grad = g_ref[rows, lanes]
            low = low_ref[0:1, lanes]
            log_total = log_ref[h, 0:1, lanes]
            inner = jnp.sum(grad.astype(f32) * out_ref[rows, lanes].astype(f32), axis=0, keepdims=True)
            gq = jnp.zeros((HEAD_SIZE, width), f32)
            for j in range(blocks):
                scores = block_scores(key_ref[j], query, low, at, j * length, width)
                probs = jnp.exp(scores - log_total)
                grad_probs = dot(value_ref[j], grad, 1, 0)
                grad_scores = (probs * (grad_probs - inner)).astype(bf16)
                gq = gq + dot(kv[j][:HEAD_SIZE, :], grad_scores, 1, 0)
                sum_ref[j, :HEAD_SIZE, :] += dot(query, grad_scores, 1, 1)
                sum_ref[j, HEAD_SIZE:, :] += dot(grad, probs.astype(bf16), 1, 1)
            gq = rotated(gq * HEAD_SIZE**-0.5, cos_ref[:, lanes], -sin_ref[:, lanes])
            gq_ref[rows, lanes] = gq.astype(bf16)

    for j in range(blocks):
        gkv[j][...] = sum_ref[j].astype(gkv[j].dtype)


def attend_back(query, low, out, log_total, grad, cosine, sine, kv):
    heads, length = query.shape[0] // HEAD_SIZE, query.shape[1]
    blocks = len(kv)
    return call(
        functools.partial(attend_back_body, blocks, heads),
        [(query.shape, bf16)] + [((2 * HEAD_SIZE, length), bf16)] * blocks,
        [((blocks, length, HEAD_SIZE), bf16)] * 2 + [((blocks, 2 * HEAD_SIZE, length), f32)],
        query, low, out, log_total, grad, cosine, sine, *kv,
    )


def pack_body(q_ref, kv_ref, bc_ref, step_ref, gains_ref, ssm_ref, inner_ref, basis_ref, valid_ref, out_ref, small_ref):
    rows, heads = step_ref.shape
    small_ref[...] = jnp.zeros_like(small_ref)
    small_ref[heads : heads + 2, :rows] = gains_ref[...].astype(f32)
    small_ref[heads + 2 : heads + 3, : ssm_ref.shape[1]] = ssm_ref[...].astype(f32)
    small_ref[heads + 3 : heads + 3 + KC, : inner_ref.shape[1]] = inner_ref[...].astype(f32)
    small_ref[heads + 3 + KC : heads + 3 + 2 * KC, : basis_ref.shape[1]] = basis_ref[...].astype(f32)
    count = jnp.sum(valid_ref[...].astype(f32), axis=1, keepdims=True)
    high = jnp.floor(count * (1.0 / 16.0))
    small_ref[heads + 3 + 2 * KC : heads + 4 + 2 * KC, 0:1] = high
    small_ref[heads + 4 + 2 * KC : heads + 5 + 2 * KC, 0:1] = count - 16.0 * high
    tail = jnp.transpose(small_ref[...])[:rows, :]
    step = jnp.concatenate([step_ref[...].astype(f32), jnp.zeros((rows, 128 - heads), f32)], axis=1)
    at = 0
    for ref in (q_ref, kv_ref, bc_ref):
        out_ref[:, at : at + ref.shape[1]] = ref[...]
        at += ref.shape[1]
    out_ref[:, at:] = (tail + step).astype(bf16)


def packed(*args):
    columns = sum(a.shape[1] for a in args[:3]) + 128
    return call(pack_body, [((args[0].shape[0], columns), bf16)], [((128, 128), f32)], *args)[0]


def prep_body(x_ref, before_ref, xt_ref, scale_ref):
    length = x_ref.shape[0]
    for at in range(-HALO, length, HALO):
        if at < 0:
            first = HALO - before_ref.shape[0]
            block = jnp.concatenate([jnp.zeros((first, x_ref.shape[1]), f32), before_ref[...].astype(f32)], axis=0)
        else:
            block = x_ref[at : at + HALO, :].astype(f32)
        block = jnp.transpose(block)
        lanes = slice(at + HALO, at + 2 * HALO)
        xt_ref[:, lanes] = block.astype(bf16)
        mean = jnp.mean(block * block, axis=0, keepdims=True)
        scale_ref[:, lanes] = jnp.broadcast_to(lax.rsqrt(mean + eps), (8, HALO))


def prepared(x, before):
    length, features = x.shape
    return call(prep_body, [((features, length + HALO), bf16), ((8, length + HALO), f32)], [], x, before)


def params_body(shape, w_ref, xt_ref, scale_ref, inner_ref, basis_ref, gains_ref, n1_ref):
    ways, rows, inner_rows, bc_rows, heads, step_at = shape
    tail = w_ref[:, step_at:].astype(f32)
    for s in range(ways):
        inner_ref[s * inner_rows : (s + 1) * inner_rows, :] = tail[s * rows : s * rows + inner_rows, :]
        basis_ref[s * bc_rows : (s + 1) * bc_rows, :] = tail[s * rows : s * rows + bc_rows, :]
    gains_ref[...] = jnp.transpose(tail)
    for at in range(0, xt_ref.shape[1], HALO):
        lanes = slice(at, at + HALO)
        normed = xt_ref[:, lanes].astype(f32) * scale_ref[0:1, lanes] * tail[:, heads : heads + 1]
        n1_ref[:, lanes] = normed.astype(bf16)


def unpacked(shape, first_w, xt, scale):
    ways, rows, inner_rows, bc_rows, heads, step_at = shape
    return call(
        functools.partial(params_body, shape),
        [((ways * inner_rows, 128), f32), ((ways * bc_rows, 128), f32), ((128, ways * rows), f32), (xt.shape, bf16)],
        [],
        first_w, xt, scale,
    )


def rope_body(attn_width, lin_ref, cos_ref, sin_ref, q_ref, kv_ref):
    cosine, sine = cos_ref[...], sin_ref[...]
    for at in range(0, attn_width, HEAD_SIZE):
        query = rotated(lin_ref[at : at + HEAD_SIZE, HALO:], cosine, sine)
        q_ref[at : at + HEAD_SIZE, :] = query.astype(bf16) * bf16(HEAD_SIZE**-0.5)
    keys = lin_ref[attn_width : attn_width + HEAD_SIZE, HALO:]
    kv_ref[:HEAD_SIZE, :] = rotated(keys, cosine, sine).astype(bf16)
    kv_ref[HEAD_SIZE:, :] = lin_ref[attn_width + HEAD_SIZE : attn_width + 2 * HEAD_SIZE, HALO:].astype(bf16)


def roped(attn_width, first_lin, cosine, sine):
    length = cosine.shape[1]
    return call(
        functools.partial(rope_body, attn_width),
        [((attn_width, length), bf16), ((2 * HEAD_SIZE, length), bf16)],
        [],
        first_lin, cosine, sine,
    )


def conv_pre(block, taps, places):
    total = None
    for lag in range(KC):
        back = KC - 1 - lag
        moved = pltpu.roll(block, back, 1) if back else block
        term = taps[:, lag : lag + 1] * moved[:, HALO:]
        if back:
            term = jnp.where(places >= back, term, 0.0)
        total = term if total is None else total + term
    return total


def sigmoid(value):
    return 1.0 / (1.0 + jnp.exp(-value))


def running_sum(value, reverse=False):
    width = value.shape[1]
    lane = lax.broadcasted_iota(jnp.int32, value.shape, 1)
    step = 1
    while step < width:
        if reverse:
            value = value + jnp.where(lane < width - step, pltpu.roll(value, width - step, 1), 0.0)
        else:
            value = value + jnp.where(lane >= step, pltpu.roll(value, step, 1), 0.0)
        step *= 2
    return value


def widened(rows):
    return jnp.transpose(jnp.concatenate([rows, jnp.zeros((112, rows.shape[1]), f32)], axis=0))


def pack_decay(ref, decay, first):
    wide = jnp.broadcast_to(decay, (16, DS))
    high = wide.astype(bf16)
    ref[first : first + 16, :] = high
    ref[first + 16 : first + 32, :] = (wide - high.astype(f32)).astype(bf16)


def chain(packs, heads, state_ref):
    width = heads * HEAD_SIZE
    for h in range(heads):
        rows = slice(h * HEAD_SIZE, (h + 1) * HEAD_SIZE)
        state = jnp.zeros((HEAD_SIZE, DS), f32)
        for pack in packs[::-1]:
            decay = pack[width : width + 16, :].astype(f32) + pack[width + 16 : width + 32, :].astype(f32)
            state = pack[rows, :].astype(f32) + decay[h : h + 1, :] * state
        state_ref[rows, :] = state


def conv_body(heads, bc_at, u_ref, lin_ref, inner_ref, basis_ref, hp_ref, place_ref, xs_ref, b_ref, c_ref, bt_ref, ct_ref, dt_ref, cum_ref, cumt_ref, pack_ref, end_ref):
    places = place_ref[0:1, :]
    length = places.shape[1]
    width = heads * HEAD_SIZE
    for at, flat, side in ((0, b_ref, bt_ref), (DS, c_ref, ct_ref)):
        taps = basis_ref[at : at + DS, heads + 3 + KC : heads + 3 + 2 * KC]
        pre = conv_pre(lin_ref[bc_at + at : bc_at + at + DS, :], taps, places)
        basis = pre * sigmoid(pre)
        side[...] = basis
        flat[...] = jnp.transpose(basis)
    raw = lin_ref[bc_at + 2 * DS : bc_at + 2 * DS + 16, HALO:] + hp_ref[:, 0:1]
    dt = jnp.maximum(raw, 0.0) + jnp.log1p(jnp.exp(-jnp.abs(raw)))
    cum = running_sum(dt * -jnp.exp(hp_ref[:, 1:2]))
    dt_ref[...] = dt
    cum_ref[...] = cum
    cumt_ref[...] = widened(cum)
    last = cum[:, length - 1 :]
    lane = lax.broadcasted_iota(jnp.int32, (1, length), 1)
    last_place = places[:, length - 1 :]
    reach = lane >= length - 1 - last_place
    to_end = jnp.where(reach, jnp.exp(jnp.minimum(last - cum, 0.0)) * dt, 0.0)
    end_ref[...] = to_end

    def one(h, _):
        rows = pl.ds(pl.multiple_of(h * HEAD_SIZE, HEAD_SIZE), HEAD_SIZE)
        pre = conv_pre(u_ref[rows, :], inner_ref[rows, :][:, heads + 3 : heads + 3 + KC], places)
        values = pre * sigmoid(pre)
        xs_ref[rows, :] = values
        summary = dot((values * end_ref[pl.ds(h, 1), :]).astype(bf16), low(b_ref[...]), 1, 0)
        pack_ref[rows, :] = summary.astype(bf16)
        return 0

    lax.fori_loop(0, heads, one, 0)
    keep = (last_place > length - 1).astype(f32)
    pack_decay(pack_ref, jnp.exp(last) * keep, width)


def conv_forward(heads, bc_at, u, lin, inner, basis, hp, places):
    length = places.shape[1]
    width = heads * HEAD_SIZE
    return call(
        functools.partial(conv_body, heads, bc_at),
        [
            ((width, length), f32),
            ((length, DS), f32),
            ((length, DS), f32),
            ((DS, length), f32),
            ((DS, length), f32),
            ((16, length), f32),
            ((16, length), f32),
            ((length, 128), f32),
            ((width + 32, DS), bf16),
        ],
        [((16, length), f32)],
        u, lin, inner, basis, hp, places,
    )


def chunk_rows(k, cum_ref, place_ref):
    lanes = slice(k * CHUNK, (k + 1) * CHUNK)
    cum = cum_ref[:, lanes]
    places = place_ref[0:1, lanes]
    base = cum_ref[:, k * CHUNK - 1 : k * CHUNK] if k else jnp.zeros((16, 1), f32)
    last = cum[:, CHUNK - 1 :]
    last_place = places[:, CHUNK - 1 :]
    lane = lax.broadcasted_iota(jnp.int32, (1, CHUNK), 1)
    entry = jnp.where(places > lane, jnp.exp(jnp.minimum(cum - base, 0.0)), 0.0)
    to_end = jnp.where(lane >= CHUNK - 1 - last_place, jnp.exp(jnp.minimum(last - cum, 0.0)), 0.0)
    over = jnp.where(last_place > CHUNK - 1, jnp.exp(jnp.minimum(last - base, 0.0)), 0.0)
    source = lax.broadcasted_iota(jnp.int32, (CHUNK, CHUNK), 0)
    target = lax.broadcasted_iota(jnp.int32, (CHUNK, CHUNK), 1)
    allowed = (source <= target) & (source >= target - places)
    return cum, entry, to_end, over, allowed


def mix_body(heads, packs, xs_ref, b_ref, ct_ref, dt_ref, cum_ref, cumt_ref, hp_ref, place_ref, z_ref, *refs):
    pack_refs = refs[:packs]
    y_ref, states_ref, squares_ref, state_ref, inter_ref, w_ref = refs[packs:]
    length = place_ref.shape[1]
    chain(pack_refs, heads, state_ref)
    for k in range(length // CHUNK):
        lanes = slice(k * CHUNK, (k + 1) * CHUNK)
        cum, entry, to_end, over, allowed = chunk_rows(k, cum_ref, place_ref)
        low_state = state_ref[...].astype(bf16)
        states_ref[k] = low_state
        side = ct_ref[:, lanes]
        match = jnp.where(allowed, exact(b_ref[lanes, :], side, 1, 0), 0.0)
        inter_ref[...] = dot(low_state, low(side), 1, 0)
        squares = jnp.zeros((1, CHUNK), f32)
        for h in range(heads):
            rows = slice(h * HEAD_SIZE, (h + 1) * HEAD_SIZE)
            spread = cum[h : h + 1, :] - cumt_ref[lanes, h : h + 1]
            mixing = (jnp.exp(jnp.minimum(spread, 0.0)) * match).astype(bf16)
            values = xs_ref[rows, lanes]
            stepped = values * dt_ref[h : h + 1, lanes]
            result = dot(stepped.astype(bf16), mixing, 1, 0)
            result = result + inter_ref[rows, :] * entry[h : h + 1, :] + hp_ref[h : h + 1, 2:3] * values
            y_ref[rows, lanes] = result
            w_ref[rows, :] = (stepped * to_end[h : h + 1, :]).astype(bf16)
            gate = z_ref[rows, lanes]
            gated = result * gate * sigmoid(gate)
            squares = squares + jnp.sum(gated * gated, axis=0, keepdims=True)
        squares_ref[:, lanes] = jnp.broadcast_to(squares, (8, CHUNK))
        if k + 1 < length // CHUNK:
            added = dot(w_ref[...], low(b_ref[lanes, :]), 1, 0)
            for h in range(heads):
                rows = slice(h * HEAD_SIZE, (h + 1) * HEAD_SIZE)
                state_ref[rows, :] = over[h : h + 1, :] * state_ref[rows, :] + added[rows, :]


def mix_forward(heads, xs, b, ct, dt, cum, cumt, hp, places, z, packs):
    length = places.shape[1]
    width = heads * HEAD_SIZE
    return call(
        functools.partial(mix_body, heads, len(packs)),
        [
            ((width, length), f32),
            ((length // CHUNK, width, DS), bf16),
            ((8, length), f32),
        ],
        [((width, DS), f32), ((width, CHUNK), f32), ((width, CHUNK), bf16)],
        xs, b, ct, dt, cum, cumt, hp, places, z, *packs,
    )


def gate_body(heads, g_ref, y_ref, z_ref, gain_ref, inv_ref, dot_ref, c_ref, cum_ref, place_ref, gy_ref, gz_ref, ggain_ref, pack_ref, entry_ref):
    length = place_ref.shape[1]
    width = heads * HEAD_SIZE
    first = g_ref.shape[0] - width
    places = place_ref[0:1, :]
    inv = inv_ref[0:1, :]
    shrink = inv * inv * inv * dot_ref[0:1, :] * (1.0 / (HS * HEAD_SIZE))
    lane = lax.broadcasted_iota(jnp.int32, (1, length), 1)
    entry_ref[...] = jnp.where(places > lane, jnp.exp(jnp.minimum(cum_ref[...], 0.0)), 0.0)

    def one(h, _):
        start = pl.multiple_of(h * HEAD_SIZE, HEAD_SIZE)
        rows = pl.ds(start, HEAD_SIZE)
        grad = g_ref[pl.ds(start + first, HEAD_SIZE), :] * inv
        values = y_ref[rows, :]
        gate = z_ref[rows, :]
        sig = sigmoid(gate)
        silu = gate * sig
        gated = values * silu
        column = lax.broadcasted_iota(jnp.int32, (HEAD_SIZE, 128), 1)
        ggain_ref[rows, :] = jnp.where(column == heads + 2, jnp.sum(grad * gated, axis=1, keepdims=True), 0.0)
        grad_gated = grad * gain_ref[rows, :][:, heads + 2 : heads + 3] - shrink * gated
        grad_values = grad_gated * silu
        gy_ref[rows, :] = grad_values
        gz_ref[rows, :] = (grad_gated * values * sig * (1.0 + gate * (1.0 - sig))).astype(bf16)
        entered = (grad_values * entry_ref[pl.ds(h, 1), :]).astype(bf16)
        pack_ref[rows, :] = dot(entered, low(c_ref[...]), 1, 0).astype(bf16)
        return 0

    lax.fori_loop(0, heads, one, 0)
    last = length - 1
    keep = (places[:, last:] > last).astype(f32)
    pack_decay(pack_ref, jnp.exp(cum_ref[:, last:]) * keep, width)


def gate_back(heads, grads, y, z, gain, inv, inner, c, cum, places):
    length = places.shape[1]
    width = heads * HEAD_SIZE
    return call(
        functools.partial(gate_body, heads),
        [
            ((width, length), f32),
            ((width, length), bf16),
            ((width, 128), f32),
            ((width + 32, DS), bf16),
        ],
        [((16, length), f32)],
        grads, y, z, gain, inv, inner, c, cum, places,
    )


def mix_back_body(heads, packs, step_at, gy_ref, xs_ref, b_ref, c_ref, bt_ref, ct_ref, dt_ref, cum_ref, cumt_ref, lin_ref, hp_ref, place_ref, states_ref, *refs):
    pack_refs = refs[:packs]
    gxs_ref, gbc_ref, gstep_ref, grow_ref, ghead_ref, grad_ref, reach_ref, inter_ref, gye_ref, w_ref, col_ref, cumg_ref, dtg_ref = refs[packs:]
    length = place_ref.shape[1]
    chain(pack_refs, heads, grad_ref)
    col_ref[...] = jnp.zeros_like(col_ref)
    cumg_ref[...] = jnp.zeros_like(cumg_ref)
    dtg_ref[...] = jnp.zeros_like(dtg_ref)
    rate = -jnp.exp(hp_ref[:, 1:2])
    bias_sum = jnp.zeros((16, CHUNK), f32)
    rate_sum = jnp.zeros((16, CHUNK), f32)
    ghead_ref[...] = jnp.zeros_like(ghead_ref)
    at_last = lax.broadcasted_iota(jnp.int32, (1, CHUNK), 1) == CHUNK - 1
    for k in reversed(range(length // CHUNK)):
        lanes = slice(k * CHUNK, (k + 1) * CHUNK)
        cum, entry, to_end, over, allowed = chunk_rows(k, cum_ref, place_ref)
        b_side, c_side = bt_ref[:, lanes], ct_ref[:, lanes]
        b_flat, c_flat = b_ref[lanes, :], c_ref[lanes, :]
        match = jnp.where(allowed, exact(b_flat, c_side, 1, 0), 0.0)
        low_grad = grad_ref[...].astype(bf16)
        reach_ref[...] = dot(low_grad, low(b_side), 1, 0)
        inter_ref[...] = dot(states_ref[k], low(c_side), 1, 0)
        grad_match = jnp.zeros((CHUNK, CHUNK), f32)
        for h in range(heads):
            rows = slice(h * HEAD_SIZE, (h + 1) * HEAD_SIZE)
            head = slice(h, h + 1)
            grad = gy_ref[rows, lanes]
            values = xs_ref[rows, lanes]
            dt = dt_ref[head, lanes]
            stepped = values * dt
            decay = jnp.exp(jnp.minimum(cum[head, :] - cumt_ref[lanes, head], 0.0))
            mixing = decay * match
            low_y = grad.astype(bf16)
            grad_mixing = dot(stepped.astype(bf16), low_y, 0, 0)
            grad_match = grad_match + grad_mixing * decay
            spread = grad_mixing * mixing
            to = to_end[head, :]
            reached = reach_ref[rows, :] * to
            grad_stepped = dot(low_y, mixing.astype(bf16), 1, 1) + reached
            ended = jnp.sum(reached * stepped, axis=0, keepdims=True)
            entered = grad * entry[head, :]
            entry_sum = jnp.sum(entered * inter_ref[rows, :], axis=0, keepdims=True)
            kept = over[head, :] * jnp.sum(
                jnp.sum(grad_ref[rows, :] * states_ref[k, rows, :].astype(f32), axis=0, keepdims=True),
                axis=1, keepdims=True,
            )
            at_end = jnp.sum(ended, axis=1, keepdims=True) + kept
            cumg_ref[head, :] = (
                jnp.sum(spread, axis=0, keepdims=True) + entry_sum - ended + jnp.where(at_last, at_end, 0.0)
            )
            col_ref[:, head] = jnp.sum(spread, axis=1, keepdims=True)
            dtg_ref[head, :] = jnp.sum(grad_stepped * values, axis=0, keepdims=True)
            gxs_ref[rows, lanes] = grad_stepped * dt + hp_ref[head, 2:3] * grad
            ghead_ref[head, 2:3] += jnp.sum(
                jnp.sum(grad * values, axis=0, keepdims=True), axis=1, keepdims=True
            )
            gye_ref[rows, :] = entered.astype(bf16)
            w_ref[rows, :] = (stepped * to).astype(bf16)
        low_match = jnp.where(allowed, grad_match, 0.0)
        gbc_ref[:DS, lanes] = exact(c_side, low_match, 1, 1) + dot(low_grad, w_ref[...], 0, 0)
        gbc_ref[DS:, lanes] = exact(b_side, low_match, 1, 0) + dot(states_ref[k], gye_ref[...], 0, 0)
        if k:
            added = dot(gye_ref[...], low(c_flat), 1, 0)
            for h in range(heads):
                rows = slice(h * HEAD_SIZE, (h + 1) * HEAD_SIZE)
                grad_ref[rows, :] = over[h : h + 1, :] * grad_ref[rows, :] + added[rows, :]
        grad_log = running_sum(cumg_ref[...] - jnp.transpose(col_ref[...])[:16, :], reverse=True)
        dt = dt_ref[:, lanes]
        rate_sum = rate_sum + grad_log * dt
        grad_step = (dtg_ref[...] + grad_log * rate) * sigmoid(lin_ref[step_at : step_at + 16, HALO:][:, lanes] + hp_ref[:, 0:1])
        gstep_ref[:, lanes] = grad_step
        bias_sum = bias_sum + grad_step
    ghead_ref[:, 0:1] = jnp.sum(bias_sum, axis=1, keepdims=True)
    ghead_ref[:, 1:2] = jnp.sum(rate_sum, axis=1, keepdims=True) * rate
    side = jnp.transpose(jnp.concatenate([ghead_ref[...], jnp.zeros((112, 128), f32)], axis=0))
    lane = lax.broadcasted_iota(jnp.int32, (8, 128), 1)
    row = jnp.zeros((8, 128), f32)
    for j in range(3):
        own = jnp.where(lane < heads, jnp.broadcast_to(side[j : j + 1, :], (8, 128)), 0.0)
        row = row + pltpu.roll(own, heads + 3 + 2 * KC + j * heads, 1)
    grow_ref[...] = row


def mix_back(heads, step_at, gy, xs, b, c, bt, ct, dt, cum, cumt, lin, hp, places, states, packs):
    length = places.shape[1]
    width = heads * HEAD_SIZE
    return call(
        functools.partial(mix_back_body, heads, len(packs), step_at),
        [
            ((width, length), f32),
            ((2 * DS, length), f32),
            ((16, length), f32),
            ((8, 128), f32),
        ],
        [
            ((16, 128), f32),
            ((width, DS), f32),
            ((width, CHUNK), f32),
            ((width, CHUNK), f32),
            ((width, CHUNK), bf16),
            ((width, CHUNK), bf16),
            ((CHUNK, 128), f32),
            ((16, CHUNK), f32),
            ((16, CHUNK), f32),
        ],
        gy, xs, b, c, bt, ct, dt, cum, cumt, lin, hp, places, states, *packs,
    )


def conv_back_body(heads, bc_at, u_ref, lin_ref, gxs_ref, gbc_ref, inner_ref, basis_ref, place_ref, g_ref, halo_ref, ginner_ref, gbasis_ref):
    places = place_ref[0:1, :]
    length = places.shape[1]
    width = u_ref.shape[0]

    def one(block, grads, taps, first, sums_ref, at):
        pre = conv_pre(block, taps, places)
        sig = sigmoid(pre)
        grad_pre = grads * sig * (1.0 + pre * (1.0 - sig))
        total = None
        for lag in range(KC):
            back = KC - 1 - lag
            counted = jnp.where(places >= back, grad_pre, 0.0) if back else grad_pre
            moved = pltpu.roll(block, back, 1) if back else block
            sums_ref[at, first + lag : first + lag + 1] = jnp.sum(counted * moved[:, HALO:], axis=1, keepdims=True)
            wide = jnp.concatenate([jnp.zeros((counted.shape[0], HALO), f32), counted * taps[:, lag : lag + 1]], axis=1)
            wide = pltpu.roll(wide, length + HALO - back, 1) if back else wide
            total = wide if total is None else total + wide
        return total[:, HALO:], jnp.transpose(total[:, :HALO])[HALO - 8 :, :]

    ginner_ref[...] = jnp.zeros_like(ginner_ref)
    gbasis_ref[...] = jnp.zeros_like(gbasis_ref)

    def inner(i, _):
        start = pl.multiple_of(i * 128, 128)
        rows = pl.ds(start, 128)
        taps = inner_ref[rows, :][:, heads + 3 : heads + 3 + KC]
        own, halo = one(u_ref[rows, :], gxs_ref[rows, :], taps, heads + 3, ginner_ref, rows)
        g_ref[rows, :] = own
        halo_ref[:, pl.ds(start, 128)] = halo
        return 0

    lax.fori_loop(0, width // 128, inner, 0)
    for i in range(0, 2 * DS, 128):
        rows = slice(i, i + 128)
        first = heads + 3 + KC
        block = lin_ref[bc_at + i : bc_at + i + 128, :]
        own, halo = one(block, gbc_ref[rows, :], basis_ref[rows, first : first + KC], first, gbasis_ref, rows)
        g_ref[width + i : width + i + 128, :] = own
        halo_ref[:, width + i : width + i + 128] = halo


def conv_back(heads, bc_at, u, lin, gxs, gbc, inner, basis, places):
    length = places.shape[1]
    width = u.shape[0]
    return call(
        functools.partial(conv_back_body, heads, bc_at),
        [((width + 2 * DS, length), f32), ((8, width + 2 * DS), f32), ((width, 128), f32), ((2 * DS, 128), f32)],
        [],
        u, lin, gxs, gbc, inner, basis, places,
    )


def early_body(pieces, n1_ref, gq_ref, gz_ref, cos_ref, sin_ref, first_ref, z_ref, *refs):
    kv_refs = refs[:pieces]
    gw_ref, gn_ref = refs[pieces:]
    n1 = n1_ref[:, HALO:]
    gkv = kv_refs[0][...].astype(f32)
    for ref in kv_refs[1:]:
        gkv = gkv + ref[...].astype(f32)
    gkv = jnp.concatenate([rotated(gkv[:HEAD_SIZE], cos_ref[...], -sin_ref[...]), gkv[HEAD_SIZE:]], axis=0).astype(bf16)
    at = 0
    total = None
    for grad, weights in ((gz_ref[...], z_ref[...]), (gq_ref[...], first_ref), (gkv, first_ref)):
        rows = grad.shape[0]
        gw_ref[:, at : at + rows] = dot(n1, grad, 1, 1).astype(bf16)
        if weights is first_ref:
            first = at - gz_ref.shape[0]
            weights = first_ref[:, first : first + rows]
        term = dot(weights, grad, 1, 0)
        total = term if total is None else total + term
        at += rows
    gn_ref[...] = total


def rows_call(body, outs, cuts, *args):
    blocks = 4

    def spec(shape, cut=0):
        if cut is None:
            return pl.BlockSpec(shape, lambda i: (0,) * len(shape))
        if cut == 1:
            return pl.BlockSpec((shape[0], shape[1] // blocks), lambda i: (0, i))
        return pl.BlockSpec((shape[0] // blocks, cut or shape[1]), lambda i: (i, 0))

    return pl.pallas_call(
        body,
        grid=(blocks,),
        out_shape=[jax.ShapeDtypeStruct(s, d) for s, d in outs],
        in_specs=[spec(a.shape, cut) for a, cut in zip(args, cuts, strict=True)],
        out_specs=[spec(s) for s, _ in outs],
        compiler_params=pltpu.CompilerParams(vmem_limit_bytes=VMEM_LIMIT),
        cost_estimate=pl.CostEstimate(flops=1000, bytes_accessed=1000, transcendentals=0),
    )(*args)


def early_products(n1, gq, gz, cosine, sine, first_w, last_w, gkv):
    features, length = n1.shape[0], gq.shape[1]
    columns = gq.shape[0] + gkv[0].shape[0] + gz.shape[0]
    return rows_call(
        functools.partial(early_body, len(gkv)),
        [((features, columns), bf16), ((features, length), f32)],
        (0, None, None, None, None, 0, gz.shape[0]) + (None,) * len(gkv),
        n1, gq, gz, cosine, sine, first_w, last_w, *gkv,
    )


def join_body(width, heads, g_ref, behind_ref, step_ref, low_ref):
    length = g_ref.shape[1]
    if length > 128:
        low_ref[: g_ref.shape[0], : length - 128] = g_ref[:, : length - 128].astype(bf16)
    behind = jnp.concatenate([jnp.zeros((120, behind_ref.shape[1]), f32), behind_ref[...]], axis=0)
    low_ref[: g_ref.shape[0], length - 128 :] = (g_ref[:, length - 128 :] + jnp.transpose(behind)).astype(bf16)
    row = lax.broadcasted_iota(jnp.int32, (16, length), 0)
    step = jnp.where(row < heads, step_ref[...], 0.0)
    low_ref[g_ref.shape[0] :, :] = jnp.concatenate([step, jnp.zeros((112, length), f32)], axis=0).astype(bf16)


def joined(heads, grads, behind, step):
    rows, length = grads.shape
    return call(functools.partial(join_body, rows, heads), [((rows + 128, length), bf16)], [], grads, behind, step)[0]


def late_body(shape, width, rest_at, n1_ref, xt_ref, scale_ref, g_ref, first_ref, u_ref, gn_ref, two_ref, inner_a_ref, inner_b_ref, basis_ref, head_ref, loss_ref, gw_ref, total_ref, low_ref, tail_ref):
    rows, inner_rows, bc_rows, heads = shape
    grad = g_ref[...]
    columns = grad.shape[0]
    made = dot(n1_ref[:, HALO:], grad, 1, 1)
    gw_ref[:, : columns - 128] = made[:, : columns - 128].astype(bf16)
    total = gn_ref[...] + dot(u_ref[:, width:], grad[:width], 1, 0) + dot(first_ref[:, rest_at:], grad[width:], 1, 0)
    total_ref[...] = total
    low_ref[...] = total.astype(bf16)
    scaled = xt_ref[:, HALO:].astype(f32) * scale_ref[0:1, HALO:]
    column = lax.broadcasted_iota(jnp.int32, tail_ref.shape, 1)
    one = jnp.sum(total * scaled, axis=1, keepdims=True)
    two = jnp.concatenate([two_ref[...], jnp.zeros((120, two_ref.shape[1]), f32)], axis=0)
    two = jnp.transpose(two)[:, 0:1]
    tail_ref[...] = made[:, columns - 128 :] + jnp.where(column == heads, one, jnp.where(column == heads + 1, two, 0.0))
    for s in range(tail_ref.shape[0] // rows):
        inner = slice(s * inner_rows, (s + 1) * inner_rows)
        tail_ref[s * rows : s * rows + inner_rows, :] += inner_a_ref[inner, :] + inner_b_ref[inner, :]
        tail_ref[s * rows : s * rows + bc_rows, :] += basis_ref[s * bc_rows : (s + 1) * bc_rows, :]
        tail_ref[s * rows : s * rows + 1, :] += head_ref[0:1, :] + loss_ref[0:1, :]
    value = tail_ref[...]
    high = value.astype(bf16).astype(f32)
    rest = pltpu.roll(value - high, 64, 1)
    gw_ref[:, columns - 128 :] = jnp.where(column < 64, high, jnp.where(column < 64 + heads, 0.0, rest)).astype(bf16)


def late_products(shape, width, rest_at, n1, xt, scale, grads, first_w, u_w, gn, two, inner_a, inner_b, basis, head, loss):
    features, length = gn.shape
    return rows_call(
        functools.partial(late_body, shape, width, rest_at),
        [((features, grads.shape[0]), bf16), ((features, length), f32), ((features, length), bf16), ((features, 128), f32)],
        (0, 0, None, None, 0, 0, 0, 1, 0, 0, 0, None, None),
        n1, xt, scale, grads, first_w, u_w, gn, two, inner_a, inner_b, basis, head, loss,
    )[:3]


def finish_body(shape, total_ref, other_ref, count_ref, bc_ref, norm_ref, step_ref, ssm_ref, two_ref, inner_ref, basis_ref, head_ref, loss_ref):
    rows, inner_rows, bc_rows, heads, bc_at = shape
    bc_width = bc_ref.shape[1]
    bc_ref[...] = total_ref[:, bc_at : bc_at + bc_width] + other_ref[:, :bc_width]
    tail = total_ref[:, bc_at + bc_width :]
    own = jnp.where(lax.broadcasted_iota(jnp.int32, tail.shape, 1) < heads, tail, tail + pltpu.roll(tail, 64, 1))
    step_ref[...] = own[:, :heads]
    other = other_ref[:, bc_width:]
    both = own + other + pltpu.roll(other, 64, 1)
    own = jnp.concatenate([own, jnp.zeros((128 - rows, 128), f32)], axis=0) if rows < 128 else own
    both = jnp.concatenate([both, jnp.zeros((128 - rows, 128), f32)], axis=0) if rows < 128 else both
    side, side_both = jnp.transpose(own), jnp.transpose(both)
    norm_ref[...] = side_both[heads : heads + 1, :rows]
    two_ref[...] = side[heads + 1 : heads + 2, :rows]
    ssm_ref[...] = side[heads + 2 : heads + 3, :inner_rows]
    inner_ref[...] = side[heads + 3 : heads + 3 + KC, :inner_rows]
    basis_ref[...] = side_both[heads + 3 + KC : heads + 3 + 2 * KC, :bc_rows]
    at = heads + 3 + 2 * KC
    for j in range(3):
        head_ref[j : j + 1, :] = own[0:1, at + j * heads : at + (j + 1) * heads]
    loss_ref[...] = own[0:1, at + 3 * heads : at + 3 * heads + 1] / (count_ref[0:1, 0:1] * MODEL_WIDTH)


def finished(shape, total, other, count):
    rows, inner_rows, bc_rows, heads, _ = shape
    return call(
        functools.partial(finish_body, shape),
        [
            ((rows, 2 * DS), f32),
            ((1, rows), f32),
            ((rows, heads), f32),
            ((1, inner_rows), f32),
            ((1, rows), f32),
            ((KC, inner_rows), f32),
            ((KC, bc_rows), f32),
            ((3, heads), f32),
            ((1, 1), f32),
        ],
        [],
        total, other, count,
    )


def input_body(own_ref, low_ref, x_ref, res_ref, gain_ref, out_ref):
    length = x_ref.shape[0]
    for at in range(0, length, HALO):
        rows = slice(at, at + HALO)
        grad = jnp.transpose(own_ref[:, rows] + low_ref[:, rows].astype(f32)) * gain_ref[0:1, :]
        x = x_ref[rows, :].astype(f32)
        scale = lax.rsqrt(jnp.mean(x * x, axis=1, keepdims=True) + eps)
        inner = jnp.mean(grad * x, axis=1, keepdims=True)
        out_ref[rows, :] = res_ref[rows, :] + scale * grad - scale * scale * scale * x * inner


def input_grad(own, low, x, res, gain):
    return call(input_body, [(x.shape, f32)], [], own, low, x, res, gain)[0]


def mlp_grads_body(n2_ref, e_ref, ggu_ref, m_ref, out_ref):
    both = ggu_ref.shape[1]
    out_ref[:, :both] = dot(n2_ref[...], ggu_ref[...], 0, 0).astype(bf16)
    out_ref[:, both:] = dot(e_ref[...], m_ref[...], 0, 0).astype(bf16)


def mlp_weight_grads(n2, e, ggu, m):
    length, features = n2.shape
    blocks = 4
    columns = ggu.shape[1] + m.shape[1]
    cut = pl.BlockSpec((length, features // blocks), lambda i: (0, i))
    return pl.pallas_call(
        mlp_grads_body,
        grid=(blocks,),
        out_shape=jax.ShapeDtypeStruct((features, columns), bf16),
        in_specs=[cut, cut, pl.BlockSpec(ggu.shape, lambda i: (0, 0)), pl.BlockSpec(m.shape, lambda i: (0, 0))],
        out_specs=pl.BlockSpec((features // blocks, columns), lambda i: (i, 0)),
        compiler_params=pltpu.CompilerParams(vmem_limit_bytes=VMEM_LIMIT),
        cost_estimate=pl.CostEstimate(flops=1000, bytes_accessed=1000, transcendentals=0),
    )(n2, e, ggu, m)


def residual_body(own_ref, low_ref, res_ref, gf_ref, gain_ref, out_ref, ea_ref, ggain_ref):
    total = jnp.zeros((1, res_ref.shape[1]), f32)
    for at in range(0, res_ref.shape[0], HALO):
        rows = slice(at, at + HALO)
        grad = own_ref[rows, :] + low_ref[rows, :].astype(f32)
        res = res_ref[rows, :]
        scale = lax.rsqrt(jnp.mean(res * res, axis=1, keepdims=True) + eps)
        total = total + jnp.sum(grad * (res * scale), axis=0, keepdims=True)
        grad = grad * gain_ref[0:1, :]
        inner = jnp.mean(grad * res, axis=1, keepdims=True)
        grad = gf_ref[rows, :] + scale * grad - scale * scale * scale * res * inner
        out_ref[rows, :] = grad
        ea_ref[rows, :] = grad.astype(bf16)
    ggain_ref[...] = jnp.broadcast_to(total, ggain_ref.shape)


def residual_back(own, low, res, gf, gain):
    return call(
        residual_body, [(res.shape, f32), (res.shape, bf16), ((8, res.shape[1]), f32)], [], own, low, res, gf, gain
    )


def rms_scale(values):
    return lax.rsqrt(jnp.mean(values * values, axis=-1, keepdims=True) + eps)


def norm_back(inputs, inv_rms, grad_normed):
    inner_mean = jnp.mean(grad_normed * inputs, axis=-1, keepdims=True)
    return inv_rms * grad_normed - inv_rms * inv_rms * inv_rms * inputs * inner_mean


def padded_rows(block, rows):
    return jnp.pad(block, ((0, rows - block.shape[0]), (0, 0)))


def shards(
    hidden,
    teacher,
    positions,
    valid_mask,
    norm_gain,
    w_query,
    key_value_weight,
    w_gatein,
    w_bc,
    w_step,
    ssm_gain,
    mlp_gain,
    w_gateup,
    w_out_attn,
    w_out_ssm,
    w_down,
    conv_inner,
    conv_bc,
    head_params,
):
    ways = lax.axis_size(("fsdp", "ctx"))
    blocks = lax.axis_size("ctx")
    rows = norm_gain.shape[0]
    length = hidden.shape[1]
    heads = w_step.shape[1]
    width = heads * HEAD_SIZE
    attn_width = w_query.shape[1]
    kv_width = key_value_weight.shape[2]
    ff_local = w_down.shape[0]
    inner_rows = ssm_gain.shape[0]
    bc_rows = conv_bc.shape[1]
    qkv_width = attn_width + 2 * kv_width
    step_at = qkv_width + 2 * DS

    live_rows = valid_mask.reshape(length, 1).astype(f32)
    count_at = heads + 3 + 2 * KC
    first_shard = packed(
        w_query,
        key_value_weight.reshape(rows, 2 * kv_width),
        w_bc,
        w_step,
        jnp.stack([norm_gain, mlp_gain]),
        ssm_gain[None],
        conv_inner,
        conv_bc,
        valid_mask,
    )
    mlp_shard = jnp.concatenate([w_gateup.reshape(rows, 2 * ff_local), w_down.T], axis=1)
    mixer_shard = w_gatein.reshape(rows, 2 * width)
    out_shard = jnp.concatenate([w_out_attn, w_out_ssm], axis=0).T

    flat_in = hidden.reshape(length, MODEL_WIDTH)
    first_line = gathered_line(first_shard, False)
    before = passed_along(flat_in[length - 16 :], "ctx", 1)
    mixer_shard, first_line = tied(mixer_shard, first_line)
    mixer_line = gathered_line(mixer_shard)
    first_w = gathered_plane(first_line)
    mlp_w = lax.all_gather(mlp_shard, ("fsdp", "ctx"), axis=0, tiled=True)

    places = positions.reshape(1, length)
    place_rows = jnp.broadcast_to(places, (8, length))
    low_rows = jnp.broadcast_to(jnp.arange(length, dtype=jnp.int32)[None] - places, (8, length))
    half = HEAD_SIZE // 2
    frequency = rope_base ** (-2.0 * jnp.arange(half, dtype=f32) / HEAD_SIZE)
    angle = frequency[:, None] * places.astype(f32)
    cosine, sine = jnp.cos(angle), jnp.sin(angle)
    hp = jnp.pad(head_params.T, ((0, 16 - heads), (0, 125)))
    xt, scale_one = prepared(flat_in, before)
    xt, scale_one, cosine, sine, hp, first_w = lax.optimization_barrier((xt, scale_one, cosine, sine, hp, first_w))

    shape = (ways, rows, inner_rows, bc_rows, heads, step_at)
    par_inner, par_basis, param_rows, n1 = unpacked(shape, first_w, xt, scale_one)
    total_count = jnp.sum(param_rows[count_at]) * 16.0 + jnp.sum(param_rows[count_at + 1])
    gain_ssm = par_inner[:, heads + 2 : heads + 3]
    gain_two = param_rows[heads + 1 : heads + 2]
    gain_two_rows = jnp.broadcast_to(gain_two, (8, MODEL_WIDTH))

    first_lin = dot(first_w, n1, 0, 0)
    query, kv_own = roped(attn_width, first_lin, cosine, sine)
    mixer_line, kv_own = tied(mixer_line, kv_own)
    kv = [kv_own] + [passed_along(kv_own, "ctx", s) for s in range(1, blocks)]
    one, two = plane_first(mixer_line)
    one, two, out_shard, *kv = tied(one, two, out_shard, *kv)
    mixer_w = plane_second(one, two)
    out_line = gathered_line(out_shard)
    attn, log_total = attend(query, low_rows, kv)
    mixer_w, attn, out_line = tied(mixer_w, attn, out_line)
    out_halves = plane_first(out_line)
    mixer_lin = dot(mixer_w, n1, 0, 0)
    gate_z, u_in = mixer_lin[:width, HALO:], mixer_lin[width:]

    xs, b_flat, c_flat, b_side, c_side, dt, cum, cumt, pack = conv_forward(
        heads, qkv_width, u_in, first_lin, par_inner, par_basis, hp, place_rows
    )
    packs = [passed_along(pack, "ctx", s) for s in range(1, blocks)]
    xs, *out_halves = tied(xs, *out_halves)
    out_w = plane_second(*out_halves)
    gateup_w, down_w = mlp_w[:, : 2 * ff_local], mlp_w[:, 2 * ff_local :]
    ssm, states, squares = mix_forward(heads, xs, b_flat, c_side, dt, cum, cumt, hp, place_rows, gate_z, packs)
    inv_ssm = lax.rsqrt((squares + swapped(squares)) / (HS * HEAD_SIZE) + eps)
    gated = ssm * jax.nn.silu(gate_z)
    branches = jnp.concatenate([attn, (gated * gain_ssm * inv_ssm[0:1]).astype(bf16)], axis=0)
    part = dot(branches, out_w, 0, 1)
    residual = flat_in.astype(f32) + (part + swapped(part.astype(bf16)).astype(f32))

    scale_two = rms_scale(residual)
    normed_two = (residual * scale_two * gain_two).astype(bf16)
    gateup = dot(normed_two, gateup_w, 1, 0)
    gate_part, up_part = gateup[:, :ff_local], gateup[:, ff_local:]
    hidden_mlp = (jax.nn.silu(gate_part) * up_part).astype(bf16)
    part = dot(hidden_mlp, down_w, 1, 1)
    final_rows = residual + (part + swapped(part.astype(bf16)).astype(f32))
    difference = (final_rows - teacher.reshape(length, MODEL_WIDTH).astype(f32)) * live_rows
    local_sq = jnp.sum(difference * difference)

    all_tokens = length * ways
    grad_final = difference * (all_tokens / total_count)
    grad_low = grad_final.astype(bf16)
    grad_hidden_mlp = dot(grad_low, down_w, 1, 0)
    sigma = jax.nn.sigmoid(gate_part)
    grad_gate = grad_hidden_mlp * up_part * sigma * (1.0 + gate_part * (1.0 - sigma))
    grad_up = grad_hidden_mlp * gate_part * sigma
    grad_gateup = jnp.concatenate([grad_gate, grad_up], axis=-1).astype(bf16)
    part = dot(grad_gateup, gateup_w, 1, 1)
    low_part, grad_gateup = tied(part.astype(bf16), grad_gateup)
    loss_lane = heads + 3 + 2 * KC + 3 * heads
    loss_row = jnp.where(lax.broadcasted_iota(jnp.int32, (8, 128), 1) == loss_lane, local_sq, 0.0)
    mlp_grads = mlp_weight_grads(normed_two, grad_low, grad_gateup, hidden_mlp)
    mlp_out = lax.psum_scatter(mlp_grads, "fsdp", scatter_dimension=0, tiled=True)
    grad_residual, grad_out, grad_gain_two = residual_back(part, swapped(low_part), residual, grad_final, gain_two_rows)

    grad_branches = dot(out_w, grad_out, 0, 1)
    grad_attn = grad_branches[:attn_width].astype(bf16)
    inner = jnp.sum(grad_branches[attn_width:] * gated * gain_ssm, axis=0, keepdims=True)
    inner = jnp.broadcast_to(inner, (8, length))
    inner = inner + swapped(inner)
    gy, grad_z, grad_gain_ssm, back_pack = gate_back(
        heads, grad_branches, ssm, gate_z, par_inner, inv_ssm, inner, c_flat, cum, place_rows
    )
    out_partial = dot(grad_out, branches, 0, 1).astype(bf16)
    grad_attn, out_partial, back_pack = tied(grad_attn, out_partial, back_pack)
    back_packs = [passed_along(back_pack, "ctx", -s) for s in range(1, blocks)]
    out_parts = scatter_first(out_partial)
    grad_query, *grad_kv = attend_back(query, low_rows, attn, log_total, grad_attn, cosine, sine, kv)
    back_packs, out_parts, grad_kv = lax.optimization_barrier((back_packs, out_parts, grad_kv))
    returned = [passed_along(grad_kv[s], "ctx", -s) for s in range(1, blocks)]
    out_parts = scatter_second(out_parts)
    grad_xs, grad_basis, grad_step, grad_head = mix_back(
        heads, step_at, gy, xs, b_flat, c_flat, b_side, c_side, dt, cum, cumt, first_lin, hp, place_rows, states, back_packs
    )
    *grad_kv, grad_xs = tied(grad_kv[0], *returned, grad_xs)
    early_w, grad_first = early_products(n1, grad_query, grad_z, cosine, sine, first_w, mixer_w, grad_kv)
    grad_xs, early_w = tied(grad_xs, early_w)
    early_parts = scatter_first(early_w)
    grad_conv, halo, grad_inner, grad_bc_taps = conv_back(
        heads, qkv_width, u_in, first_lin, grad_xs, grad_basis, par_inner, par_basis, place_rows
    )
    halo, mlp_out = tied(halo, mlp_out)
    mlp_out = lax.psum_scatter(mlp_out, "ctx", scatter_dimension=0, tiled=True)
    behind = passed_along(halo, "ctx", -1)
    behind, early_parts, out_parts = tied(behind, early_parts, out_parts)
    early_parts = scatter_second(early_parts)
    grad_late = joined(heads, grad_conv, behind, grad_step)
    late_w, grad_normed, low_normed = late_products(
        shape[1:-1], width, qkv_width, n1, xt, scale_one, grad_late, first_w, mixer_w, grad_first,
        grad_gain_two, grad_gain_ssm, grad_inner, grad_bc_taps, grad_head, loss_row,
    )
    gain_one = jnp.broadcast_to(param_rows[heads : heads + 1], (8, MODEL_WIDTH))
    late_w, low_normed, early_parts, out_parts = tied(late_w, low_normed, early_parts, out_parts)
    late_parts = scatter_first(late_w, heads)
    inner_kept, inner_other = halved([*early_parts, *out_parts])
    grad_input = input_grad(grad_normed, swapped(low_normed), flat_in, grad_residual, gain_one)
    gateup_out = mlp_out[:, : 2 * ff_local].astype(f32).reshape(rows, 2, ff_local)
    down_out = mlp_out[:, 2 * ff_local :].astype(f32).T
    late_parts = scatter_second(late_parts, heads)
    late_parts, inner_other, grad_input, gateup_out, down_out = tied(late_parts, inner_other, grad_input, gateup_out, down_out)
    inner_parts = halved_on(inner_kept, inner_other)
    out_at = width + attn_width + 2 * kv_width
    query_out = inner_parts[:, width : width + attn_width]
    kv_out = inner_parts[:, width + attn_width : out_at].reshape(rows, 2, kv_width)
    attn_out = inner_parts[:, out_at : out_at + attn_width].T
    ssm_out = inner_parts[:, out_at + attn_width :].T
    late_out = scatter_third(late_parts)
    count_row = jnp.full((8, 128), total_count, f32)
    bc_out, norm_out, step_out, ssm_gain_out, mlp_gain_out, inner_out, basis_out, head_out, loss_value = finished(
        (rows, inner_rows, bc_rows, heads, width), late_out, swapped(late_out[:, width:]), count_row
    )
    return (
        final_rows.astype(bf16).reshape(1, length, MODEL_WIDTH),
        loss_value.reshape(()),
        grad_input.reshape(1, length, MODEL_WIDTH),
        norm_out.reshape(rows),
        query_out,
        kv_out,
        jnp.stack([inner_parts[:, :width], late_out[:, :width]], axis=1),
        bc_out,
        step_out,
        ssm_gain_out.reshape(inner_rows),
        mlp_gain_out.reshape(rows),
        gateup_out,
        attn_out,
        ssm_out,
        down_out,
        inner_out,
        basis_out,
        head_out,
    )


def solution(mesh):
    placed = (
        P("fsdp", "ctx", None),
        P("fsdp", "ctx", None),
        P("fsdp", "ctx"),
        P("fsdp", "ctx"),
        P(("fsdp", "ctx")),
        P(("fsdp", "ctx"), "tp"),
        P(("fsdp", "ctx"), None, "tp"),
        P(("fsdp", "ctx"), None, "tp"),
        P(("fsdp", "ctx"), None),
        P(("fsdp", "ctx"), "tp"),
        P(("tp", "fsdp", "ctx")),
        P(("fsdp", "ctx")),
        P(("fsdp", "ctx"), None, "tp"),
        P("tp", ("fsdp", "ctx")),
        P("tp", ("fsdp", "ctx")),
        P("tp", ("fsdp", "ctx")),
        P(None, ("tp", "fsdp", "ctx")),
        P(None, ("fsdp", "ctx")),
        P(None, "tp"),
    )
    return jax.shard_map(
        shards,
        mesh=mesh,
        in_specs=placed,
        out_specs=(
            P("fsdp", "ctx", None),
            P(),
            P("fsdp", "ctx", None),
            P(("fsdp", "ctx")),
            P(("fsdp", "ctx"), "tp"),
            P(("fsdp", "ctx"), None, "tp"),
            P(("fsdp", "ctx"), None, "tp"),
            P(("fsdp", "ctx"), None),
            P(("fsdp", "ctx"), "tp"),
            P(("tp", "fsdp", "ctx")),
            P(("fsdp", "ctx")),
            P(("fsdp", "ctx"), None, "tp"),
            P("tp", ("fsdp", "ctx")),
            P("tp", ("fsdp", "ctx")),
            P("tp", ("fsdp", "ctx")),
            P(None, ("tp", "fsdp", "ctx")),
            P(None, ("fsdp", "ctx")),
            P(None, "tp"),
        ),
        check_vma=False,
    )
```

```python
import functools

import jax
import jax.numpy as jnp
from jax import lax
from jax.experimental import pallas as pl
from jax.experimental.pallas import tpu as pltpu
from jax.sharding import PartitionSpec as P

MODEL_WIDTH = 1024
HEAD_SIZE = 64
HS = 24
DS = 128
KC = 4

eps = 1e-05
rope_base = 100000000000.0
masked_score = -1e30
f32 = jnp.float32
bf16 = jnp.bfloat16
CHUNK = 128
HALO = 128
VMEM_LIMIT = 40 * 2**20


def dot(left, right, left_dim, right_dim, precision=None):
    return lax.dot_general(
        left, right, (((left_dim,), (right_dim,)), ((), ())), precision=precision, preferred_element_type=f32
    )


def exact(left, right, left_dim, right_dim):
    return dot(left, right, left_dim, right_dim, lax.Precision.HIGHEST)


def low(value):
    return value.astype(bf16)


def factors():
    fsdp = lax.axis_size("fsdp")
    side = int(round(fsdp**0.5))
    if side * side != fsdp:
        side = 1
    return (
        ("fsdp", fsdp // side, side),
        ("fsdp", side, 1),
        ("ctx", lax.axis_size("ctx"), 1),
    )


def coordinate(dim):
    axis, size, stride = dim
    return lax.rem(lax.axis_index(axis) // stride, size)


def shifted(value, dim, step):
    axis, size, stride = dim
    pairs = []
    for source in range(lax.axis_size(axis)):
        at = source // stride % size
        pairs.append((source, source + ((at + step) % size - at) * stride))
    return lax.ppermute(value, axis, pairs)


def passed_along(value, axis, steps):
    count = lax.axis_size(axis)
    pairs = [(s, s + steps) for s in range(count) if 0 <= s + steps < count]
    return lax.ppermute(value, axis, pairs)


def swapped(value):
    return lax.ppermute(value, "tp", [(0, 1), (1, 0)])


def gathered_along(value, dim):
    size = dim[1]
    if size == 1:
        return value[None]
    at = coordinate(dim)
    if size == 2:
        other = shifted(value, dim, 1)
        return jnp.where(at == 0, jnp.stack([value, other]), jnp.stack([other, value]))
    pieces = [value] + [shifted(value, dim, s) for s in range(1, size)]
    ring = jnp.stack((pieces[::-1]) * 2)
    return lax.dynamic_slice_in_dim(ring, size - 1 - at, size, 0)


def tied(*values):
    return lax.optimization_barrier(values)


def gathered_line(shard, doubling=True):
    zdim = factors()[2]
    size = zdim[1]
    if not doubling or size & (size - 1):
        return gathered_along(shard, zdim)
    at = coordinate(zdim)
    value = shard[None]
    step = 1
    while step < size:
        other = lax.ppermute(value, zdim[0], [(i, i ^ step) for i in range(size)])
        pair = (jnp.concatenate([value, other]), jnp.concatenate([other, value]))
        value = jnp.where(at // step % 2 == 0, *pair)
        step *= 2
    return value


def plane_first(line):
    ydim, xdim, _ = factors()
    half = line.shape[-1] // 256 * 128
    return gathered_along(line[..., :half], ydim), gathered_along(line[..., half:], xdim)


def plane_second(one, two):
    ydim, xdim, _ = factors()
    one = jnp.swapaxes(gathered_along(one, xdim), 0, 1)
    two = gathered_along(two, ydim)
    whole = jnp.concatenate([one, two], axis=-1)
    return whole.reshape(-1, whole.shape[-1])


def gathered_plane(line):
    return plane_second(*plane_first(line))


def in_pair(value, kept):
    body, tail = value[..., :-128], value[..., -128:]
    whole = tail + jnp.roll(tail, 64, axis=-1)
    high = lax.reduce_precision(whole, 8, 7)
    rest = (whole - high).astype(bf16)
    high = high.astype(bf16)
    column = lax.broadcasted_iota(jnp.int32, tail.shape, tail.ndim - 1)
    tail = jnp.where(column < kept, tail.astype(bf16), jnp.where(column < 64, high, rest))
    return jnp.concatenate([body.astype(bf16), tail], axis=-1)


def reduced_along(value, dim, front, kept=None):
    size = dim[1]
    if size == 1:
        return lax.index_in_dim(value, 0, front, False)
    at = coordinate(dim)
    total = lax.dynamic_index_in_dim(value, at, front, False).astype(f32)
    for step in range(1, size):
        piece = lax.dynamic_index_in_dim(value, lax.rem(at + step, size), front, False)
        total = total + shifted(piece, dim, step).astype(f32)
    return total.astype(bf16) if kept is None else in_pair(total, kept)


def scatter_first(partial, kept=None):
    ydim, xdim, zdim = factors()
    columns = partial.shape[1]
    blocks = partial.reshape(ydim[1], xdim[1], zdim[1], -1, columns)
    half = columns // 256 * 128
    return reduced_along(blocks[..., :half], xdim, 1), reduced_along(blocks[..., half:], ydim, 0, kept)


def scatter_second(parts, kept=None):
    ydim, xdim, _ = factors()
    return reduced_along(parts[0], ydim, 0), reduced_along(parts[1], xdim, 0, kept)


def exchanged(blocks, step):
    zdim = factors()[2]
    upper = coordinate(zdim) // step % 2 == 1
    halves = blocks.reshape(2, step, *blocks.shape[1:])
    kept = jnp.where(upper, halves[1], halves[0])
    sent = jnp.where(upper, halves[0], halves[1])
    return kept, lax.ppermute(sent, zdim[0], [(i, i ^ step) for i in range(zdim[1])])


def halved(parts):
    blocks = jnp.concatenate(parts, axis=-1)
    return exchanged(blocks, blocks.shape[0] // 2)


def halved_on(kept, other):
    while True:
        total = kept.astype(f32) + other.astype(f32)
        if total.shape[0] == 1:
            return total[0]
        kept, other = exchanged(total.astype(bf16), total.shape[0] // 2)


def scatter_third(parts):
    zdim = factors()[2]
    blocks = jnp.concatenate(parts, axis=-1)
    at = coordinate(zdim)
    total = lax.dynamic_index_in_dim(blocks, at, 0, False).astype(f32)
    for step in range(1, zdim[1]):
        piece = lax.dynamic_index_in_dim(blocks, lax.rem(at + step, zdim[1]), 0, False)
        total = total + shifted(piece, zdim, step).astype(f32)
    return total


COSTS = {"prep_body": 1, "params_body": 1, "rope_body": 1, "attend_body": 9, "attend_back_body": 14, "conv_body": 7, "mix_body": 3,
    "gate_body": 3, "mix_back_body": 13, "conv_back_body": 8, "residual_body": 2, "input_body": 2}


def call(body, outs, scratch, *args):
    name = getattr(body, "func", body).__name__
    return pl.pallas_call(
        body,
        out_shape=[jax.ShapeDtypeStruct(s, d) for s, d in outs],
        in_specs=[pl.BlockSpec(memory_space=pltpu.VMEM)] * len(args),
        out_specs=[pl.BlockSpec(memory_space=pltpu.VMEM)] * len(outs),
        scratch_shapes=[pltpu.VMEM(s, d) for s, d in scratch],
        compiler_params=pltpu.CompilerParams(vmem_limit_bytes=VMEM_LIMIT),
        cost_estimate=pl.CostEstimate(flops=COSTS.get(name, 1) * 5 * 10**8, bytes_accessed=1000, transcendentals=0),
    )(*args)


def rotated(block, cosine, sine):
    half = block.shape[0] // 2
    one, two = block[:half], block[half:]
    return jnp.concatenate([one * cosine - two * sine, two * cosine + one * sine], axis=0)


def flipped(block):
    return jnp.transpose(block.astype(f32)).astype(block.dtype)


def block_scores(keys, query, low, at, back, width):
    scores = dot(keys, query, 1, 0)
    place = lax.broadcasted_iota(jnp.int32, scores.shape, 0) - back
    allowed = place >= low
    if back == 0:
        token = at + lax.broadcasted_iota(jnp.int32, scores.shape, 1)
        allowed = allowed & (place <= token)
    return jnp.where(allowed, scores, masked_score)


def attend_body(blocks, heads, q_ref, low_ref, *refs):
    kv = refs[:blocks]
    out_ref, log_ref, key_ref, score_ref = refs[blocks:]
    length = q_ref.shape[1]
    width = min(256, length)
    for j in range(blocks):
        key_ref[j] = flipped(kv[j][:HEAD_SIZE, :])

    @pl.loop(0, heads)
    def _(h):
        rows = pl.ds(pl.multiple_of(h * HEAD_SIZE, HEAD_SIZE), HEAD_SIZE)
        for at in range(0, length, width):
            lanes = slice(at, at + width)
            query = q_ref[rows, lanes]
            low = low_ref[0:1, lanes]
            top = jnp.full((1, width), masked_score, f32)
            for j in range(blocks):
                seen = length if j else at + width
                scores = block_scores(key_ref[j, :seen, :], query, low, at, j * length, width)
                score_ref[j, :seen, :] = scores
                top = jnp.maximum(top, jnp.max(scores, axis=0, keepdims=True))
            total = jnp.zeros((1, width), f32)
            mixed = jnp.zeros((HEAD_SIZE, width), f32)
            for j in range(blocks):
                seen = length if j else at + width
                weight = jnp.exp(score_ref[j, :seen, :] - top)
                total = total + jnp.sum(weight, axis=0, keepdims=True)
                mixed = mixed + dot(kv[j][HEAD_SIZE:, :seen], weight.astype(bf16), 1, 0)
            out_ref[rows, lanes] = (mixed / total).astype(bf16)
            log_ref[h, :, lanes] = jnp.broadcast_to(top + jnp.log(total), (8, width))


def attend(query, low, kv):
    heads, length = query.shape[0] // HEAD_SIZE, query.shape[1]
    width = min(256, length)
    return call(
        functools.partial(attend_body, len(kv), heads),
        [(query.shape, bf16), ((heads, 8, length), f32)],
        [((len(kv), length, HEAD_SIZE), bf16), ((len(kv), length, width), f32)],
        query, low, *kv,
    )


def attend_back_body(blocks, heads, q_ref, low_ref, out_ref, log_ref, g_ref, cos_ref, sin_ref, *refs):
    kv = refs[:blocks]
    gq_ref = refs[blocks]
    gkv = refs[blocks + 1 : 2 * blocks + 1]
    key_ref, value_ref, sum_ref = refs[2 * blocks + 1 :]
    length = q_ref.shape[1]
    width = min(256, length)
    for j in range(blocks):
        key_ref[j] = flipped(kv[j][:HEAD_SIZE, :])
        value_ref[j] = flipped(kv[j][HEAD_SIZE:, :])
    sum_ref[...] = jnp.zeros_like(sum_ref)

    @pl.loop(0, heads)
    def _(h):
        rows = pl.ds(pl.multiple_of(h * HEAD_SIZE, HEAD_SIZE), HEAD_SIZE)
        for at in range(0, length, width):
            lanes = slice(at, at + width)
            query = q_ref[rows, lanes]
            grad = g_ref[rows, lanes]
            low = low_ref[0:1, lanes]
            log_total = log_ref[h, 0:1, lanes]
            inner = jnp.sum(grad.astype(f32) * out_ref[rows, lanes].astype(f32), axis=0, keepdims=True)
            gq = jnp.zeros((HEAD_SIZE, width), f32)
            for j in range(blocks):
                seen = length if j else at + width
                scores = block_scores(key_ref[j, :seen, :], query, low, at, j * length, width)
                probs = jnp.exp(scores - log_total)
                grad_probs = dot(value_ref[j, :seen, :], grad, 1, 0)
                grad_scores = (probs * (grad_probs - inner)).astype(bf16)
                gq = gq + dot(kv[j][:HEAD_SIZE, :seen], grad_scores, 1, 0)
                sum_ref[j, :HEAD_SIZE, :seen] += dot(query, grad_scores, 1, 1)
                sum_ref[j, HEAD_SIZE:, :seen] += dot(grad, probs.astype(bf16), 1, 1)
            gq = rotated(gq * HEAD_SIZE**-0.5, cos_ref[:, lanes], -sin_ref[:, lanes])
            gq_ref[rows, lanes] = gq.astype(bf16)

    for j in range(blocks):
        gkv[j][...] = sum_ref[j].astype(gkv[j].dtype)


def attend_back(query, low, out, log_total, grad, cosine, sine, kv):
    heads, length = query.shape[0] // HEAD_SIZE, query.shape[1]
    blocks = len(kv)
    return call(
        functools.partial(attend_back_body, blocks, heads),
        [(query.shape, bf16)] + [((2 * HEAD_SIZE, length), bf16)] * blocks,
        [((blocks, length, HEAD_SIZE), bf16)] * 2 + [((blocks, 2 * HEAD_SIZE, length), f32)],
        query, low, out, log_total, grad, cosine, sine, *kv,
    )


def pack_body(q_ref, kv_ref, bc_ref, step_ref, gains_ref, ssm_ref, inner_ref, basis_ref, valid_ref, out_ref, small_ref):
    rows, heads = step_ref.shape
    small_ref[...] = jnp.zeros_like(small_ref)
    small_ref[heads : heads + 2, :rows] = gains_ref[...].astype(f32)
    small_ref[heads + 2 : heads + 3, : ssm_ref.shape[1]] = ssm_ref[...].astype(f32)
    small_ref[heads + 3 : heads + 3 + KC, : inner_ref.shape[1]] = inner_ref[...].astype(f32)
    small_ref[heads + 3 + KC : heads + 3 + 2 * KC, : basis_ref.shape[1]] = basis_ref[...].astype(f32)
    count = jnp.sum(valid_ref[...].astype(f32), axis=1, keepdims=True)
    high = jnp.floor(count * (1.0 / 16.0))
    small_ref[heads + 3 + 2 * KC : heads + 4 + 2 * KC, 0:1] = high
    small_ref[heads + 4 + 2 * KC : heads + 5 + 2 * KC, 0:1] = count - 16.0 * high
    tail = jnp.transpose(small_ref[...])[:rows, :]
    step = jnp.concatenate([step_ref[...].astype(f32), jnp.zeros((rows, 128 - heads), f32)], axis=1)
    at = 0
    for ref in (q_ref, kv_ref, bc_ref):
        out_ref[:, at : at + ref.shape[1]] = ref[...]
        at += ref.shape[1]
    out_ref[:, at:] = (tail + step).astype(bf16)


def packed(*args):
    columns = sum(a.shape[1] for a in args[:3]) + 128
    return call(pack_body, [((args[0].shape[0], columns), bf16)], [((128, 128), f32)], *args)[0]


def prep_body(x_ref, before_ref, xt_ref, scale_ref):
    length = x_ref.shape[0]
    for at in range(-HALO, length, HALO):
        if at < 0:
            first = HALO - before_ref.shape[0]
            block = jnp.concatenate([jnp.zeros((first, x_ref.shape[1]), f32), before_ref[...].astype(f32)], axis=0)
        else:
            block = x_ref[at : at + HALO, :].astype(f32)
        block = jnp.transpose(block)
        lanes = slice(at + HALO, at + 2 * HALO)
        xt_ref[:, lanes] = block.astype(bf16)
        mean = jnp.mean(block * block, axis=0, keepdims=True)
        scale_ref[:, lanes] = jnp.broadcast_to(lax.rsqrt(mean + eps), (8, HALO))


def prepared(x, before):
    length, features = x.shape
    return call(prep_body, [((features, length + HALO), bf16), ((8, length + HALO), f32)], [], x, before)


def params_body(shape, w_ref, xt_ref, scale_ref, inner_ref, basis_ref, gains_ref, n1_ref):
    ways, rows, inner_rows, bc_rows, heads, step_at = shape
    tail = w_ref[:, step_at:].astype(f32)
    for s in range(ways):
        inner_ref[s * inner_rows : (s + 1) * inner_rows, :] = tail[s * rows : s * rows + inner_rows, :]
        basis_ref[s * bc_rows : (s + 1) * bc_rows, :] = tail[s * rows : s * rows + bc_rows, :]
    gains_ref[...] = jnp.transpose(tail)
    for at in range(0, xt_ref.shape[1], HALO):
        lanes = slice(at, at + HALO)
        normed = xt_ref[:, lanes].astype(f32) * scale_ref[0:1, lanes] * tail[:, heads : heads + 1]
        n1_ref[:, lanes] = normed.astype(bf16)


def unpacked(shape, first_w, xt, scale):
    ways, rows, inner_rows, bc_rows, heads, step_at = shape
    return call(
        functools.partial(params_body, shape),
        [((ways * inner_rows, 128), f32), ((ways * bc_rows, 128), f32), ((128, ways * rows), f32), (xt.shape, bf16)],
        [],
        first_w, xt, scale,
    )


def rope_body(attn_width, lin_ref, cos_ref, sin_ref, q_ref, kv_ref):
    cosine, sine = cos_ref[...], sin_ref[...]
    for at in range(0, attn_width, HEAD_SIZE):
        query = rotated(lin_ref[at : at + HEAD_SIZE, HALO:], cosine, sine)
        q_ref[at : at + HEAD_SIZE, :] = query.astype(bf16) * bf16(HEAD_SIZE**-0.5)
    keys = lin_ref[attn_width : attn_width + HEAD_SIZE, HALO:]
    kv_ref[:HEAD_SIZE, :] = rotated(keys, cosine, sine).astype(bf16)
    kv_ref[HEAD_SIZE:, :] = lin_ref[attn_width + HEAD_SIZE : attn_width + 2 * HEAD_SIZE, HALO:].astype(bf16)


def roped(attn_width, first_lin, cosine, sine):
    length = cosine.shape[1]
    return call(
        functools.partial(rope_body, attn_width),
        [((attn_width, length), bf16), ((2 * HEAD_SIZE, length), bf16)],
        [],
        first_lin, cosine, sine,
    )


def conv_pre(block, taps, places):
    total = None
    for lag in range(KC):
        back = KC - 1 - lag
        moved = pltpu.roll(block, back, 1) if back else block
        term = taps[:, lag : lag + 1] * moved[:, HALO:]
        if back:
            term = jnp.where(places >= back, term, 0.0)
        total = term if total is None else total + term
    return total


def sigmoid(value):
    return 1.0 / (1.0 + jnp.exp(-value))


def running_sum(value, reverse=False):
    width = value.shape[1]
    lane = lax.broadcasted_iota(jnp.int32, value.shape, 1)
    step = 1
    while step < width:
        if reverse:
            value = value + jnp.where(lane < width - step, pltpu.roll(value, width - step, 1), 0.0)
        else:
            value = value + jnp.where(lane >= step, pltpu.roll(value, step, 1), 0.0)
        step *= 2
    return value


def widened(rows):
    return jnp.transpose(jnp.concatenate([rows, jnp.zeros((112, rows.shape[1]), f32)], axis=0))


def pack_decay(ref, decay, first):
    wide = jnp.broadcast_to(decay, (16, DS))
    high = wide.astype(bf16)
    ref[first : first + 16, :] = high
    ref[first + 16 : first + 32, :] = (wide - high.astype(f32)).astype(bf16)


def chain(packs, heads, state_ref):
    width = heads * HEAD_SIZE
    for h in range(heads):
        rows = slice(h * HEAD_SIZE, (h + 1) * HEAD_SIZE)
        state = jnp.zeros((HEAD_SIZE, DS), f32)
        for pack in packs[::-1]:
            decay = pack[width : width + 16, :].astype(f32) + pack[width + 16 : width + 32, :].astype(f32)
            state = pack[rows, :].astype(f32) + decay[h : h + 1, :] * state
        state_ref[rows, :] = state


def conv_body(heads, bc_at, u_ref, lin_ref, inner_ref, basis_ref, hp_ref, place_ref, xs_ref, b_ref, c_ref, bt_ref, ct_ref, dt_ref, cum_ref, cumt_ref, pack_ref, end_ref):
    places = place_ref[0:1, :]
    length = places.shape[1]
    width = heads * HEAD_SIZE
    for at, flat, side in ((0, b_ref, bt_ref), (DS, c_ref, ct_ref)):
        taps = basis_ref[at : at + DS, heads + 3 + KC : heads + 3 + 2 * KC]
        pre = conv_pre(lin_ref[bc_at + at : bc_at + at + DS, :], taps, places)
        basis = pre * sigmoid(pre)
        side[...] = basis
        flat[...] = jnp.transpose(basis)
    raw = lin_ref[bc_at + 2 * DS : bc_at + 2 * DS + 16, HALO:] + hp_ref[:, 0:1]
    dt = jnp.maximum(raw, 0.0) + jnp.log1p(jnp.exp(-jnp.abs(raw)))
    cum = running_sum(dt * -jnp.exp(hp_ref[:, 1:2]))
    dt_ref[...] = dt
    cum_ref[...] = cum
    cumt_ref[...] = widened(cum)
    last = cum[:, length - 1 :]
    lane = lax.broadcasted_iota(jnp.int32, (1, length), 1)
    last_place = places[:, length - 1 :]
    reach = lane >= length - 1 - last_place
    to_end = jnp.where(reach, jnp.exp(jnp.minimum(last - cum, 0.0)) * dt, 0.0)
    end_ref[...] = to_end

    def one(h, _):
        rows = pl.ds(pl.multiple_of(h * HEAD_SIZE, HEAD_SIZE), HEAD_SIZE)
        pre = conv_pre(u_ref[rows, :], inner_ref[rows, :][:, heads + 3 : heads + 3 + KC], places)
        values = pre * sigmoid(pre)
        xs_ref[rows, :] = values
        summary = dot((values * end_ref[pl.ds(h, 1), :]).astype(bf16), low(b_ref[...]), 1, 0)
        pack_ref[rows, :] = summary.astype(bf16)
        return 0

    lax.fori_loop(0, heads, one, 0)
    keep = (last_place > length - 1).astype(f32)
    pack_decay(pack_ref, jnp.exp(last) * keep, width)


def conv_forward(heads, bc_at, u, lin, inner, basis, hp, places):
    length = places.shape[1]
    width = heads * HEAD_SIZE
    return call(
        functools.partial(conv_body, heads, bc_at),
        [
            ((width, length), f32),
            ((length, DS), f32),
            ((length, DS), f32),
            ((DS, length), f32),
            ((DS, length), f32),
            ((16, length), f32),
            ((16, length), f32),
            ((length, 128), f32),
            ((width + 32, DS), bf16),
        ],
        [((16, length), f32)],
        u, lin, inner, basis, hp, places,
    )


def chunk_rows(k, cum_ref, place_ref):
    lanes = slice(k * CHUNK, (k + 1) * CHUNK)
    cum = cum_ref[:, lanes]
    places = place_ref[0:1, lanes]
    base = cum_ref[:, k * CHUNK - 1 : k * CHUNK] if k else jnp.zeros((16, 1), f32)
    last = cum[:, CHUNK - 1 :]
    last_place = places[:, CHUNK - 1 :]
    lane = lax.broadcasted_iota(jnp.int32, (1, CHUNK), 1)
    entry = jnp.where(places > lane, jnp.exp(jnp.minimum(cum - base, 0.0)), 0.0)
    to_end = jnp.where(lane >= CHUNK - 1 - last_place, jnp.exp(jnp.minimum(last - cum, 0.0)), 0.0)
    over = jnp.where(last_place > CHUNK - 1, jnp.exp(jnp.minimum(last - base, 0.0)), 0.0)
    source = lax.broadcasted_iota(jnp.int32, (CHUNK, CHUNK), 0)
    target = lax.broadcasted_iota(jnp.int32, (CHUNK, CHUNK), 1)
    allowed = (source <= target) & (source >= target - places)
    return cum, entry, to_end, over, allowed


def mix_body(heads, packs, xs_ref, b_ref, ct_ref, dt_ref, cum_ref, cumt_ref, hp_ref, place_ref, z_ref, *refs):
    pack_refs = refs[:packs]
    y_ref, states_ref, squares_ref, state_ref, inter_ref, w_ref = refs[packs:]
    length = place_ref.shape[1]
    chain(pack_refs, heads, state_ref)
    for k in range(length // CHUNK):
        lanes = slice(k * CHUNK, (k + 1) * CHUNK)
        cum, entry, to_end, over, allowed = chunk_rows(k, cum_ref, place_ref)
        low_state = state_ref[...].astype(bf16)
        states_ref[k] = low_state
        side = ct_ref[:, lanes]
        match = jnp.where(allowed, exact(b_ref[lanes, :], side, 1, 0), 0.0)
        inter_ref[...] = dot(low_state, low(side), 1, 0)
        squares = jnp.zeros((1, CHUNK), f32)
        for h in range(heads):
            rows = slice(h * HEAD_SIZE, (h + 1) * HEAD_SIZE)
            spread = cum[h : h + 1, :] - cumt_ref[lanes, h : h + 1]
            mixing = (jnp.exp(jnp.minimum(spread, 0.0)) * match).astype(bf16)
            values = xs_ref[rows, lanes]
            stepped = values * dt_ref[h : h + 1, lanes]
            result = dot(stepped.astype(bf16), mixing, 1, 0)
            result = result + inter_ref[rows, :] * entry[h : h + 1, :] + hp_ref[h : h + 1, 2:3] * values
            y_ref[rows, lanes] = result
            w_ref[rows, :] = (stepped * to_end[h : h + 1, :]).astype(bf16)
            gate = z_ref[rows, lanes]
            gated = result * gate * sigmoid(gate)
            squares = squares + jnp.sum(gated * gated, axis=0, keepdims=True)
        squares_ref[:, lanes] = jnp.broadcast_to(squares, (8, CHUNK))
        if k + 1 < length // CHUNK:
            added = dot(w_ref[...], low(b_ref[lanes, :]), 1, 0)
            for h in range(heads):
                rows = slice(h * HEAD_SIZE, (h + 1) * HEAD_SIZE)
                state_ref[rows, :] = over[h : h + 1, :] * state_ref[rows, :] + added[rows, :]


def mix_forward(heads, xs, b, ct, dt, cum, cumt, hp, places, z, packs):
    length = places.shape[1]
    width = heads * HEAD_SIZE
    return call(
        functools.partial(mix_body, heads, len(packs)),
        [
            ((width, length), f32),
            ((length // CHUNK, width, DS), bf16),
            ((8, length), f32),
        ],
        [((width, DS), f32), ((width, CHUNK), f32), ((width, CHUNK), bf16)],
        xs, b, ct, dt, cum, cumt, hp, places, z, *packs,
    )


def gate_body(heads, g_ref, y_ref, z_ref, gain_ref, inv_ref, dot_ref, c_ref, cum_ref, place_ref, gy_ref, gz_ref, ggain_ref, pack_ref, entry_ref):
    length = place_ref.shape[1]
    width = heads * HEAD_SIZE
    first = g_ref.shape[0] - width
    places = place_ref[0:1, :]
    inv = inv_ref[0:1, :]
    shrink = inv * inv * inv * dot_ref[0:1, :] * (1.0 / (HS * HEAD_SIZE))
    lane = lax.broadcasted_iota(jnp.int32, (1, length), 1)
    entry_ref[...] = jnp.where(places > lane, jnp.exp(jnp.minimum(cum_ref[...], 0.0)), 0.0)

    def one(h, _):
        start = pl.multiple_of(h * HEAD_SIZE, HEAD_SIZE)
        rows = pl.ds(start, HEAD_SIZE)
        grad = g_ref[pl.ds(start + first, HEAD_SIZE), :] * inv
        values = y_ref[rows, :]
        gate = z_ref[rows, :]
        sig = sigmoid(gate)
        silu = gate * sig
        gated = values * silu
        column = lax.broadcasted_iota(jnp.int32, (HEAD_SIZE, 128), 1)
        ggain_ref[rows, :] = jnp.where(column == heads + 2, jnp.sum(grad * gated, axis=1, keepdims=True), 0.0)
        grad_gated = grad * gain_ref[rows, :][:, heads + 2 : heads + 3] - shrink * gated
        grad_values = grad_gated * silu
        gy_ref[rows, :] = grad_values
        gz_ref[rows, :] = (grad_gated * values * sig * (1.0 + gate * (1.0 - sig))).astype(bf16)
        entered = (grad_values * entry_ref[pl.ds(h, 1), :]).astype(bf16)
        pack_ref[rows, :] = dot(entered, low(c_ref[...]), 1, 0).astype(bf16)
        return 0

    lax.fori_loop(0, heads, one, 0)
    last = length - 1
    keep = (places[:, last:] > last).astype(f32)
    pack_decay(pack_ref, jnp.exp(cum_ref[:, last:]) * keep, width)


def gate_back(heads, grads, y, z, gain, inv, inner, c, cum, places):
    length = places.shape[1]
    width = heads * HEAD_SIZE
    return call(
        functools.partial(gate_body, heads),
        [
            ((width, length), f32),
            ((width, length), bf16),
            ((width, 128), f32),
            ((width + 32, DS), bf16),
        ],
        [((16, length), f32)],
        grads, y, z, gain, inv, inner, c, cum, places,
    )


def mix_back_body(heads, packs, step_at, gy_ref, xs_ref, b_ref, c_ref, bt_ref, ct_ref, dt_ref, cum_ref, cumt_ref, lin_ref, hp_ref, place_ref, states_ref, *refs):
    pack_refs = refs[:packs]
    gxs_ref, gbc_ref, gstep_ref, grow_ref, ghead_ref, grad_ref, reach_ref, inter_ref, gye_ref, w_ref, col_ref, cumg_ref, dtg_ref = refs[packs:]
    length = place_ref.shape[1]
    chain(pack_refs, heads, grad_ref)
    col_ref[...] = jnp.zeros_like(col_ref)
    cumg_ref[...] = jnp.zeros_like(cumg_ref)
    dtg_ref[...] = jnp.zeros_like(dtg_ref)
    rate = -jnp.exp(hp_ref[:, 1:2])
    bias_sum = jnp.zeros((16, CHUNK), f32)
    rate_sum = jnp.zeros((16, CHUNK), f32)
    ghead_ref[...] = jnp.zeros_like(ghead_ref)
    at_last = lax.broadcasted_iota(jnp.int32, (1, CHUNK), 1) == CHUNK - 1
    for k in reversed(range(length // CHUNK)):
        lanes = slice(k * CHUNK, (k + 1) * CHUNK)
        cum, entry, to_end, over, allowed = chunk_rows(k, cum_ref, place_ref)
        b_side, c_side = bt_ref[:, lanes], ct_ref[:, lanes]
        b_flat, c_flat = b_ref[lanes, :], c_ref[lanes, :]
        match = jnp.where(allowed, exact(b_flat, c_side, 1, 0), 0.0)
        low_grad = grad_ref[...].astype(bf16)
        reach_ref[...] = dot(low_grad, low(b_side), 1, 0)
        inter_ref[...] = dot(states_ref[k], low(c_side), 1, 0)
        grad_match = jnp.zeros((CHUNK, CHUNK), f32)
        for h in range(heads):
            rows = slice(h * HEAD_SIZE, (h + 1) * HEAD_SIZE)
            head = slice(h, h + 1)
            grad = gy_ref[rows, lanes]
            values = xs_ref[rows, lanes]
            dt = dt_ref[head, lanes]
            stepped = values * dt
            decay = jnp.exp(jnp.minimum(cum[head, :] - cumt_ref[lanes, head], 0.0))
            mixing = decay * match
            low_y = grad.astype(bf16)
            grad_mixing = dot(stepped.astype(bf16), low_y, 0, 0)
            grad_match = grad_match + grad_mixing * decay
            spread = grad_mixing * mixing
            to = to_end[head, :]
            reached = reach_ref[rows, :] * to
            grad_stepped = dot(low_y, mixing.astype(bf16), 1, 1) + reached
            ended = jnp.sum(reached * stepped, axis=0, keepdims=True)
            entered = grad * entry[head, :]
            entry_sum = jnp.sum(entered * inter_ref[rows, :], axis=0, keepdims=True)
            kept = over[head, :] * jnp.sum(
                jnp.sum(grad_ref[rows, :] * states_ref[k, rows, :].astype(f32), axis=0, keepdims=True),
                axis=1, keepdims=True,
            )
            at_end = jnp.sum(ended, axis=1, keepdims=True) + kept
            cumg_ref[head, :] = (
                jnp.sum(spread, axis=0, keepdims=True) + entry_sum - ended + jnp.where(at_last, at_end, 0.0)
            )
            col_ref[:, head] = jnp.sum(spread, axis=1, keepdims=True)
            dtg_ref[head, :] = jnp.sum(grad_stepped * values, axis=0, keepdims=True)
            gxs_ref[rows, lanes] = grad_stepped * dt + hp_ref[head, 2:3] * grad
            ghead_ref[head, 2:3] += jnp.sum(
                jnp.sum(grad * values, axis=0, keepdims=True), axis=1, keepdims=True
            )
            gye_ref[rows, :] = entered.astype(bf16)
            w_ref[rows, :] = (stepped * to).astype(bf16)
        low_match = jnp.where(allowed, grad_match, 0.0)
        gbc_ref[:DS, lanes] = exact(c_side, low_match, 1, 1) + dot(low_grad, w_ref[...], 0, 0)
        gbc_ref[DS:, lanes] = exact(b_side, low_match, 1, 0) + dot(states_ref[k], gye_ref[...], 0, 0)
        if k:
            added = dot(gye_ref[...], low(c_flat), 1, 0)
            for h in range(heads):
                rows = slice(h * HEAD_SIZE, (h + 1) * HEAD_SIZE)
                grad_ref[rows, :] = over[h : h + 1, :] * grad_ref[rows, :] + added[rows, :]
        grad_log = running_sum(cumg_ref[...] - jnp.transpose(col_ref[...])[:16, :], reverse=True)
        dt = dt_ref[:, lanes]
        rate_sum = rate_sum + grad_log * dt
        grad_step = (dtg_ref[...] + grad_log * rate) * sigmoid(lin_ref[step_at : step_at + 16, HALO:][:, lanes] + hp_ref[:, 0:1])
        gstep_ref[:, lanes] = grad_step
        bias_sum = bias_sum + grad_step
    ghead_ref[:, 0:1] = jnp.sum(bias_sum, axis=1, keepdims=True)
    ghead_ref[:, 1:2] = jnp.sum(rate_sum, axis=1, keepdims=True) * rate
    side = jnp.transpose(jnp.concatenate([ghead_ref[...], jnp.zeros((112, 128), f32)], axis=0))
    lane = lax.broadcasted_iota(jnp.int32, (8, 128), 1)
    row = jnp.zeros((8, 128), f32)
    for j in range(3):
        own = jnp.where(lane < heads, jnp.broadcast_to(side[j : j + 1, :], (8, 128)), 0.0)
        row = row + pltpu.roll(own, heads + 3 + 2 * KC + j * heads, 1)
    grow_ref[...] = row


def mix_back(heads, step_at, gy, xs, b, c, bt, ct, dt, cum, cumt, lin, hp, places, states, packs):
    length = places.shape[1]
    width = heads * HEAD_SIZE
    return call(
        functools.partial(mix_back_body, heads, len(packs), step_at),
        [
            ((width, length), f32),
            ((2 * DS, length), f32),
            ((16, length), f32),
            ((8, 128), f32),
        ],
        [
            ((16, 128), f32),
            ((width, DS), f32),
            ((width, CHUNK), f32),
            ((width, CHUNK), f32),
            ((width, CHUNK), bf16),
            ((width, CHUNK), bf16),
            ((CHUNK, 128), f32),
            ((16, CHUNK), f32),
            ((16, CHUNK), f32),
        ],
        gy, xs, b, c, bt, ct, dt, cum, cumt, lin, hp, places, states, *packs,
    )


def conv_back_body(heads, bc_at, u_ref, lin_ref, gxs_ref, gbc_ref, inner_ref, basis_ref, place_ref, g_ref, halo_ref, ginner_ref, gbasis_ref):
    places = place_ref[0:1, :]
    length = places.shape[1]
    width = u_ref.shape[0]

    def one(block, grads, taps, first, sums_ref, at):
        pre = conv_pre(block, taps, places)
        sig = sigmoid(pre)
        grad_pre = grads * sig * (1.0 + pre * (1.0 - sig))
        total = None
        for lag in range(KC):
            back = KC - 1 - lag
            counted = jnp.where(places >= back, grad_pre, 0.0) if back else grad_pre
            moved = pltpu.roll(block, back, 1) if back else block
            sums_ref[at, first + lag : first + lag + 1] = jnp.sum(counted * moved[:, HALO:], axis=1, keepdims=True)
            wide = jnp.concatenate([jnp.zeros((counted.shape[0], HALO), f32), counted * taps[:, lag : lag + 1]], axis=1)
            wide = pltpu.roll(wide, length + HALO - back, 1) if back else wide
            total = wide if total is None else total + wide
        return total[:, HALO:], jnp.transpose(total[:, :HALO])[HALO - 8 :, :]

    ginner_ref[...] = jnp.zeros_like(ginner_ref)
    gbasis_ref[...] = jnp.zeros_like(gbasis_ref)

    def inner(i, _):
        start = pl.multiple_of(i * 128, 128)
        rows = pl.ds(start, 128)
        taps = inner_ref[rows, :][:, heads + 3 : heads + 3 + KC]
        own, halo = one(u_ref[rows, :], gxs_ref[rows, :], taps, heads + 3, ginner_ref, rows)
        g_ref[rows, :] = own
        halo_ref[:, pl.ds(start, 128)] = halo
        return 0

    lax.fori_loop(0, width // 128, inner, 0)
    for i in range(0, 2 * DS, 128):
        rows = slice(i, i + 128)
        first = heads + 3 + KC
        block = lin_ref[bc_at + i : bc_at + i + 128, :]
        own, halo = one(block, gbc_ref[rows, :], basis_ref[rows, first : first + KC], first, gbasis_ref, rows)
        g_ref[width + i : width + i + 128, :] = own
        halo_ref[:, width + i : width + i + 128] = halo


def conv_back(heads, bc_at, u, lin, gxs, gbc, inner, basis, places):
    length = places.shape[1]
    width = u.shape[0]
    return call(
        functools.partial(conv_back_body, heads, bc_at),
        [((width + 2 * DS, length), f32), ((8, width + 2 * DS), f32), ((width, 128), f32), ((2 * DS, 128), f32)],
        [],
        u, lin, gxs, gbc, inner, basis, places,
    )


def early_body(pieces, n1_ref, gq_ref, gz_ref, cos_ref, sin_ref, first_ref, z_ref, *refs):
    kv_refs = refs[:pieces]
    gw_ref, gn_ref = refs[pieces:]
    n1 = n1_ref[:, HALO:]
    gkv = kv_refs[0][...].astype(f32)
    for ref in kv_refs[1:]:
        gkv = gkv + ref[...].astype(f32)
    gkv = jnp.concatenate([rotated(gkv[:HEAD_SIZE], cos_ref[...], -sin_ref[...]), gkv[HEAD_SIZE:]], axis=0).astype(bf16)
    at = 0
    total = None
    for grad, weights in ((gz_ref[...], z_ref[...]), (gq_ref[...], first_ref), (gkv, first_ref)):
        rows = grad.shape[0]
        gw_ref[:, at : at + rows] = dot(n1, grad, 1, 1).astype(bf16)
        if weights is first_ref:
            first = at - gz_ref.shape[0]
            weights = first_ref[:, first : first + rows]
        term = dot(weights, grad, 1, 0)
        total = term if total is None else total + term
        at += rows
    gn_ref[...] = total.astype(bf16)


def rows_call(body, outs, cuts, *args):
    blocks = 4

    def spec(shape, cut=0):
        if cut is None:
            return pl.BlockSpec(shape, lambda i: (0,) * len(shape))
        if cut == 1:
            return pl.BlockSpec((shape[0], shape[1] // blocks), lambda i: (0, i))
        return pl.BlockSpec((shape[0] // blocks, cut or shape[1]), lambda i: (i, 0))

    return pl.pallas_call(
        body,
        grid=(blocks,),
        out_shape=[jax.ShapeDtypeStruct(s, d) for s, d in outs],
        in_specs=[spec(a.shape, cut) for a, cut in zip(args, cuts, strict=True)],
        out_specs=[spec(s) for s, _ in outs],
        compiler_params=pltpu.CompilerParams(vmem_limit_bytes=VMEM_LIMIT),
        cost_estimate=pl.CostEstimate(flops=4 * 5 * 10**8, bytes_accessed=1000, transcendentals=0),
    )(*args)


def early_products(n1, gq, gz, cosine, sine, first_w, last_w, gkv):
    features, length = n1.shape[0], gq.shape[1]
    columns = gq.shape[0] + gkv[0].shape[0] + gz.shape[0]
    return rows_call(
        functools.partial(early_body, len(gkv)),
        [((features, columns), bf16), ((features, length), bf16)],
        (0, None, None, None, None, 0, gz.shape[0]) + (None,) * len(gkv),
        n1, gq, gz, cosine, sine, first_w, last_w, *gkv,
    )


def join_body(width, heads, g_ref, behind_ref, step_ref, low_ref):
    length = g_ref.shape[1]
    if length > 128:
        low_ref[: g_ref.shape[0], : length - 128] = g_ref[:, : length - 128].astype(bf16)
    behind = jnp.concatenate([jnp.zeros((120, behind_ref.shape[1]), f32), behind_ref[...]], axis=0)
    low_ref[: g_ref.shape[0], length - 128 :] = (g_ref[:, length - 128 :] + jnp.transpose(behind)).astype(bf16)
    row = lax.broadcasted_iota(jnp.int32, (16, length), 0)
    step = jnp.where(row < heads, step_ref[...], 0.0)
    low_ref[g_ref.shape[0] :, :] = jnp.concatenate([step, jnp.zeros((112, length), f32)], axis=0).astype(bf16)


def joined(heads, grads, behind, step):
    rows, length = grads.shape
    return call(functools.partial(join_body, rows, heads), [((rows + 128, length), bf16)], [], grads, behind, step)[0]


def late_body(shape, width, rest_at, n1_ref, xt_ref, scale_ref, g_ref, first_ref, u_ref, gn_ref, two_ref, inner_a_ref, inner_b_ref, basis_ref, head_ref, loss_ref, gw_ref, low_ref, tail_ref):
    rows, inner_rows, bc_rows, heads = shape
    grad = g_ref[...]
    columns = grad.shape[0]
    made = dot(n1_ref[:, HALO:], grad, 1, 1)
    gw_ref[:, : columns - 128] = made[:, : columns - 128].astype(bf16)
    total = gn_ref[...].astype(f32) + dot(u_ref[:, width:], grad[:width], 1, 0) + dot(first_ref[:, rest_at:], grad[width:], 1, 0)
    low_ref[...] = total.astype(bf16)
    scaled = xt_ref[:, HALO:].astype(f32) * scale_ref[0:1, HALO:]
    column = lax.broadcasted_iota(jnp.int32, tail_ref.shape, 1)
    one = jnp.sum(total * scaled, axis=1, keepdims=True)
    two = jnp.concatenate([two_ref[...], jnp.zeros((120, two_ref.shape[1]), f32)], axis=0)
    two = jnp.transpose(two)[:, 0:1]
    tail_ref[...] = made[:, columns - 128 :] + jnp.where(column == heads, one, jnp.where(column == heads + 1, two, 0.0))
    for s in range(tail_ref.shape[0] // rows):
        inner = slice(s * inner_rows, (s + 1) * inner_rows)
        tail_ref[s * rows : s * rows + inner_rows, :] += inner_a_ref[inner, :] + inner_b_ref[inner, :]
        tail_ref[s * rows : s * rows + bc_rows, :] += basis_ref[s * bc_rows : (s + 1) * bc_rows, :]
        tail_ref[s * rows : s * rows + 1, :] += head_ref[0:1, :] + loss_ref[0:1, :]
    value = tail_ref[...]
    high = value.astype(bf16).astype(f32)
    rest = pltpu.roll(value - high, 64, 1)
    gw_ref[:, columns - 128 :] = jnp.where(column < 64, high, jnp.where(column < 64 + heads, 0.0, rest)).astype(bf16)


def late_products(shape, width, rest_at, n1, xt, scale, grads, first_w, u_w, gn, two, inner_a, inner_b, basis, head, loss):
    features, length = gn.shape
    return rows_call(
        functools.partial(late_body, shape, width, rest_at),
        [((features, grads.shape[0]), bf16), ((features, length), bf16), ((features, 128), f32)],
        (0, 0, None, None, 0, 0, 0, 1, 0, 0, 0, None, None),
        n1, xt, scale, grads, first_w, u_w, gn, two, inner_a, inner_b, basis, head, loss,
    )[:2]


def finish_body(shape, total_ref, other_ref, count_ref, bc_ref, norm_ref, step_ref, ssm_ref, two_ref, inner_ref, basis_ref, head_ref, loss_ref):
    rows, inner_rows, bc_rows, heads, bc_at = shape
    bc_width = bc_ref.shape[1]
    bc_ref[...] = total_ref[:, bc_at : bc_at + bc_width] + other_ref[:, :bc_width]
    tail = total_ref[:, bc_at + bc_width :]
    own = jnp.where(lax.broadcasted_iota(jnp.int32, tail.shape, 1) < heads, tail, tail + pltpu.roll(tail, 64, 1))
    step_ref[...] = own[:, :heads]
    other = other_ref[:, bc_width:]
    both = own + other + pltpu.roll(other, 64, 1)
    own = jnp.concatenate([own, jnp.zeros((128 - rows, 128), f32)], axis=0) if rows < 128 else own
    both = jnp.concatenate([both, jnp.zeros((128 - rows, 128), f32)], axis=0) if rows < 128 else both
    side, side_both = jnp.transpose(own), jnp.transpose(both)
    norm_ref[...] = side_both[heads : heads + 1, :rows]
    two_ref[...] = side[heads + 1 : heads + 2, :rows]
    ssm_ref[...] = side[heads + 2 : heads + 3, :inner_rows]
    inner_ref[...] = side[heads + 3 : heads + 3 + KC, :inner_rows]
    basis_ref[...] = side_both[heads + 3 + KC : heads + 3 + 2 * KC, :bc_rows]
    at = heads + 3 + 2 * KC
    for j in range(3):
        head_ref[j : j + 1, :] = own[0:1, at + j * heads : at + (j + 1) * heads]
    loss_ref[...] = own[0:1, at + 3 * heads : at + 3 * heads + 1] / (count_ref[0:1, 0:1] * MODEL_WIDTH)


def finished(shape, total, other, count):
    rows, inner_rows, bc_rows, heads, _ = shape
    return call(
        functools.partial(finish_body, shape),
        [
            ((rows, 2 * DS), f32),
            ((1, rows), f32),
            ((rows, heads), f32),
            ((1, inner_rows), f32),
            ((1, rows), f32),
            ((KC, inner_rows), f32),
            ((KC, bc_rows), f32),
            ((3, heads), f32),
            ((1, 1), f32),
        ],
        [],
        total, other, count,
    )


def input_body(own_ref, low_ref, x_ref, res_ref, gain_ref, out_ref):
    length = x_ref.shape[0]
    for at in range(0, length, HALO):
        rows = slice(at, at + HALO)
        grad = jnp.transpose(own_ref[:, rows].astype(f32) + low_ref[:, rows].astype(f32)) * gain_ref[0:1, :]
        x = x_ref[rows, :].astype(f32)
        scale = lax.rsqrt(jnp.mean(x * x, axis=1, keepdims=True) + eps)
        inner = jnp.mean(grad * x, axis=1, keepdims=True)
        out_ref[rows, :] = res_ref[rows, :] + scale * grad - scale * scale * scale * x * inner


def input_grad(own, low, x, res, gain):
    return call(input_body, [(x.shape, f32)], [], own, low, x, res, gain)[0]


def mlp_grads_body(n2_ref, e_ref, ggu_ref, m_ref, out_ref):
    both = ggu_ref.shape[1]
    out_ref[:, :both] = dot(n2_ref[...], ggu_ref[...], 0, 0).astype(bf16)
    out_ref[:, both:] = dot(e_ref[...], m_ref[...], 0, 0).astype(bf16)


def mlp_weight_grads(n2, e, ggu, m):
    length, features = n2.shape
    blocks = 4
    columns = ggu.shape[1] + m.shape[1]
    cut = pl.BlockSpec((length, features // blocks), lambda i: (0, i))
    return pl.pallas_call(
        mlp_grads_body,
        grid=(blocks,),
        out_shape=jax.ShapeDtypeStruct((features, columns), bf16),
        in_specs=[cut, cut, pl.BlockSpec(ggu.shape, lambda i: (0, 0)), pl.BlockSpec(m.shape, lambda i: (0, 0))],
        out_specs=pl.BlockSpec((features // blocks, columns), lambda i: (i, 0)),
        compiler_params=pltpu.CompilerParams(vmem_limit_bytes=VMEM_LIMIT),
        cost_estimate=pl.CostEstimate(flops=4 * 5 * 10**8, bytes_accessed=1000, transcendentals=0),
    )(n2, e, ggu, m)


def residual_body(own_ref, low_ref, res_ref, gf_ref, gain_ref, out_ref, ea_ref, ggain_ref):
    total = jnp.zeros((1, res_ref.shape[1]), f32)
    for at in range(0, res_ref.shape[0], HALO):
        rows = slice(at, at + HALO)
        grad = own_ref[rows, :] + low_ref[rows, :].astype(f32)
        res = res_ref[rows, :]
        scale = lax.rsqrt(jnp.mean(res * res, axis=1, keepdims=True) + eps)
        total = total + jnp.sum(grad * (res * scale), axis=0, keepdims=True)
        grad = grad * gain_ref[0:1, :]
        inner = jnp.mean(grad * res, axis=1, keepdims=True)
        grad = gf_ref[rows, :] + scale * grad - scale * scale * scale * res * inner
        out_ref[rows, :] = grad
        ea_ref[rows, :] = grad.astype(bf16)
    ggain_ref[...] = jnp.broadcast_to(total, ggain_ref.shape)


def residual_back(own, low, res, gf, gain):
    return call(
        residual_body, [(res.shape, f32), (res.shape, bf16), ((8, res.shape[1]), f32)], [], own, low, res, gf, gain
    )


def rms_scale(values):
    return lax.rsqrt(jnp.mean(values * values, axis=-1, keepdims=True) + eps)


def norm_back(inputs, inv_rms, grad_normed):
    inner_mean = jnp.mean(grad_normed * inputs, axis=-1, keepdims=True)
    return inv_rms * grad_normed - inv_rms * inv_rms * inv_rms * inputs * inner_mean


def padded_rows(block, rows):
    return jnp.pad(block, ((0, rows - block.shape[0]), (0, 0)))


def shards(
    hidden,
    teacher,
    positions,
    valid_mask,
    norm_gain,
    w_query,
    key_value_weight,
    w_gatein,
    w_bc,
    w_step,
    ssm_gain,
    mlp_gain,
    w_gateup,
    w_out_attn,
    w_out_ssm,
    w_down,
    conv_inner,
    conv_bc,
    head_params,
):
    ways = lax.axis_size(("fsdp", "ctx"))
    blocks = lax.axis_size("ctx")
    rows = norm_gain.shape[0]
    length = hidden.shape[1]
    heads = w_step.shape[1]
    width = heads * HEAD_SIZE
    attn_width = w_query.shape[1]
    kv_width = key_value_weight.shape[2]
    ff_local = w_down.shape[0]
    inner_rows = ssm_gain.shape[0]
    bc_rows = conv_bc.shape[1]
    qkv_width = attn_width + 2 * kv_width
    step_at = qkv_width + 2 * DS

    live_rows = valid_mask.reshape(length, 1).astype(f32)
    count_at = heads + 3 + 2 * KC
    first_shard = packed(
        w_query,
        key_value_weight.reshape(rows, 2 * kv_width),
        w_bc,
        w_step,
        jnp.stack([norm_gain, mlp_gain]),
        ssm_gain[None],
        conv_inner,
        conv_bc,
        valid_mask,
    )
    mlp_shard = jnp.concatenate([w_gateup.reshape(rows, 2 * ff_local), w_down.T], axis=1)
    mixer_shard = w_gatein.reshape(rows, 2 * width)
    out_shard = jnp.concatenate([w_out_attn, w_out_ssm], axis=0).T

    flat_in = hidden.reshape(length, MODEL_WIDTH)
    first_line = gathered_line(first_shard, False)
    before = passed_along(flat_in[length - 16 :], "ctx", 1)
    mixer_shard, first_line = tied(mixer_shard, first_line)
    mixer_line = gathered_line(mixer_shard)
    first_w = gathered_plane(first_line)
    mlp_w = lax.all_gather(mlp_shard, ("fsdp", "ctx"), axis=0, tiled=True)

    places = positions.reshape(1, length)
    place_rows = jnp.broadcast_to(places, (8, length))
    low_rows = jnp.broadcast_to(jnp.arange(length, dtype=jnp.int32)[None] - places, (8, length))
    half = HEAD_SIZE // 2
    frequency = rope_base ** (-2.0 * jnp.arange(half, dtype=f32) / HEAD_SIZE)
    angle = frequency[:, None] * places.astype(f32)
    cosine, sine = jnp.cos(angle), jnp.sin(angle)
    hp = jnp.pad(head_params.T, ((0, 16 - heads), (0, 125)))
    xt, scale_one = prepared(flat_in, before)
    xt, scale_one, cosine, sine, hp, first_w = lax.optimization_barrier((xt, scale_one, cosine, sine, hp, first_w))

    shape = (ways, rows, inner_rows, bc_rows, heads, step_at)
    par_inner, par_basis, param_rows, n1 = unpacked(shape, first_w, xt, scale_one)
    total_count = jnp.sum(param_rows[count_at]) * 16.0 + jnp.sum(param_rows[count_at + 1])
    gain_ssm = par_inner[:, heads + 2 : heads + 3]
    gain_two = param_rows[heads + 1 : heads + 2]
    gain_two_rows = jnp.broadcast_to(gain_two, (8, MODEL_WIDTH))

    first_lin = dot(first_w, n1, 0, 0)
    query, kv_own = roped(attn_width, first_lin, cosine, sine)
    mixer_line, kv_own = tied(mixer_line, kv_own)
    kv = [kv_own] + [passed_along(kv_own, "ctx", s) for s in range(1, blocks)]
    one, two = plane_first(mixer_line)
    one, two, out_shard, *kv = tied(one, two, out_shard, *kv)
    mixer_w = plane_second(one, two)
    out_line = gathered_line(out_shard)
    attn, log_total = attend(query, low_rows, kv)
    mixer_w, attn, out_line = tied(mixer_w, attn, out_line)
    out_halves = plane_first(out_line)
    mixer_lin = dot(mixer_w, n1, 0, 0)
    gate_z, u_in = mixer_lin[:width, HALO:], mixer_lin[width:]

    xs, b_flat, c_flat, b_side, c_side, dt, cum, cumt, pack = conv_forward(
        heads, qkv_width, u_in, first_lin, par_inner, par_basis, hp, place_rows
    )
    packs = [passed_along(pack, "ctx", s) for s in range(1, blocks)]
    xs, *out_halves = tied(xs, *out_halves)
    out_w = plane_second(*out_halves)
    gateup_w, down_w = mlp_w[:, : 2 * ff_local], mlp_w[:, 2 * ff_local :]
    ssm, states, squares = mix_forward(heads, xs, b_flat, c_side, dt, cum, cumt, hp, place_rows, gate_z, packs)
    inv_ssm = lax.rsqrt((squares + swapped(squares)) / (HS * HEAD_SIZE) + eps)
    gated = ssm * jax.nn.silu(gate_z)
    branches = jnp.concatenate([attn, (gated * gain_ssm * inv_ssm[0:1]).astype(bf16)], axis=0)
    part = dot(branches, out_w, 0, 1)
    residual = flat_in.astype(f32) + (part + swapped(part.astype(bf16)).astype(f32))

    scale_two = rms_scale(residual)
    normed_two = (residual * scale_two * gain_two).astype(bf16)
    gateup = dot(normed_two, gateup_w, 1, 0)
    hidden_mlp = (jax.nn.silu(gateup[:, :ff_local]) * gateup[:, ff_local:]).astype(bf16)
    gateup, hidden_mlp = tied(gateup.astype(bf16), hidden_mlp)
    gate_part, up_part = gateup[:, :ff_local].astype(f32), gateup[:, ff_local:].astype(f32)
    part = dot(hidden_mlp, down_w, 1, 1)
    final_rows = residual + (part + swapped(part.astype(bf16)).astype(f32))
    difference = (final_rows - teacher.reshape(length, MODEL_WIDTH).astype(f32)) * live_rows
    local_sq = jnp.sum(difference * difference)

    all_tokens = length * ways
    grad_final = difference * (all_tokens / total_count)
    grad_low = grad_final.astype(bf16)
    grad_hidden_mlp = dot(grad_low, down_w, 1, 0)
    sigma = jax.nn.sigmoid(gate_part)
    grad_gate = grad_hidden_mlp * up_part * sigma * (1.0 + gate_part * (1.0 - sigma))
    grad_up = grad_hidden_mlp * gate_part * sigma
    grad_gateup = jnp.concatenate([grad_gate, grad_up], axis=-1).astype(bf16)
    part = dot(grad_gateup, gateup_w, 1, 1)
    low_part, grad_gateup = tied(part.astype(bf16), grad_gateup)
    loss_lane = heads + 3 + 2 * KC + 3 * heads
    loss_row = jnp.where(lax.broadcasted_iota(jnp.int32, (8, 128), 1) == loss_lane, local_sq, 0.0)
    mlp_grads = mlp_weight_grads(normed_two, grad_low, grad_gateup, hidden_mlp)
    mlp_out = lax.psum_scatter(mlp_grads, "fsdp", scatter_dimension=0, tiled=True)
    grad_residual, grad_out, grad_gain_two = residual_back(part, swapped(low_part), residual, grad_final, gain_two_rows)

    grad_branches = dot(out_w, grad_out, 0, 1)
    grad_attn = grad_branches[:attn_width].astype(bf16)
    inner = jnp.sum(grad_branches[attn_width:] * gated * gain_ssm, axis=0, keepdims=True)
    inner = jnp.broadcast_to(inner, (8, length))
    inner = inner + swapped(inner)
    gy, grad_z, grad_gain_ssm, back_pack = gate_back(
        heads, grad_branches, ssm, gate_z, par_inner, inv_ssm, inner, c_flat, cum, place_rows
    )
    out_partial = dot(grad_out, branches, 0, 1).astype(bf16)
    grad_attn, out_partial, back_pack = tied(grad_attn, out_partial, back_pack)
    back_packs = [passed_along(back_pack, "ctx", -s) for s in range(1, blocks)]
    out_parts = scatter_first(out_partial)
    grad_query, *grad_kv = attend_back(query, low_rows, attn, log_total, grad_attn, cosine, sine, kv)
    back_packs, out_parts, grad_kv = lax.optimization_barrier((back_packs, out_parts, grad_kv))
    returned = [passed_along(grad_kv[s], "ctx", -s) for s in range(1, blocks)]
    out_parts = scatter_second(out_parts)
    grad_xs, grad_basis, grad_step, grad_head = mix_back(
        heads, step_at, gy, xs, b_flat, c_flat, b_side, c_side, dt, cum, cumt, first_lin, hp, place_rows, states, back_packs
    )
    *grad_kv, grad_xs = tied(grad_kv[0], *returned, grad_xs)
    early_w, grad_first = early_products(n1, grad_query, grad_z, cosine, sine, first_w, mixer_w, grad_kv)
    grad_xs, early_w = tied(grad_xs, early_w)
    early_parts = scatter_first(early_w)
    grad_conv, halo, grad_inner, grad_bc_taps = conv_back(
        heads, qkv_width, u_in, first_lin, grad_xs, grad_basis, par_inner, par_basis, place_rows
    )
    halo, mlp_out = tied(halo, mlp_out)
    mlp_out = lax.psum_scatter(mlp_out, "ctx", scatter_dimension=0, tiled=True)
    behind = passed_along(halo, "ctx", -1)
    behind, early_parts, out_parts = tied(behind, early_parts, out_parts)
    early_parts = scatter_second(early_parts)
    grad_late = joined(heads, grad_conv, behind, grad_step)
    late_w, low_normed = late_products(
        shape[1:-1], width, qkv_width, n1, xt, scale_one, grad_late, first_w, mixer_w, grad_first,
        grad_gain_two, grad_gain_ssm, grad_inner, grad_bc_taps, grad_head, loss_row,
    )
    gain_one = jnp.broadcast_to(param_rows[heads : heads + 1], (8, MODEL_WIDTH))
    late_w, low_normed, early_parts, out_parts = tied(late_w, low_normed, early_parts, out_parts)
    late_parts = scatter_first(late_w, heads)
    inner_kept, inner_other = halved([*early_parts, *out_parts])
    grad_input = input_grad(low_normed, swapped(low_normed), flat_in, grad_residual, gain_one)
    gateup_out = mlp_out[:, : 2 * ff_local].astype(f32).reshape(rows, 2, ff_local)
    down_out = mlp_out[:, 2 * ff_local :].astype(f32).T
    late_parts = scatter_second(late_parts, heads)
    late_parts, inner_other, grad_input, gateup_out, down_out = tied(late_parts, inner_other, grad_input, gateup_out, down_out)
    inner_parts = halved_on(inner_kept, inner_other)
    out_at = width + attn_width + 2 * kv_width
    query_out = inner_parts[:, width : width + attn_width]
    kv_out = inner_parts[:, width + attn_width : out_at].reshape(rows, 2, kv_width)
    attn_out = inner_parts[:, out_at : out_at + attn_width].T
    ssm_out = inner_parts[:, out_at + attn_width :].T
    late_out = scatter_third(late_parts)
    count_row = jnp.full((8, 128), total_count, f32)
    bc_out, norm_out, step_out, ssm_gain_out, mlp_gain_out, inner_out, basis_out, head_out, loss_value = finished(
        (rows, inner_rows, bc_rows, heads, width), late_out, swapped(late_out[:, width:]), count_row
    )
    return (
        final_rows.astype(bf16).reshape(1, length, MODEL_WIDTH),
        loss_value.reshape(()),
        grad_input.reshape(1, length, MODEL_WIDTH),
        norm_out.reshape(rows),
        query_out,
        kv_out,
        jnp.stack([inner_parts[:, :width], late_out[:, :width]], axis=1),
        bc_out,
        step_out,
        ssm_gain_out.reshape(inner_rows),
        mlp_gain_out.reshape(rows),
        gateup_out,
        attn_out,
        ssm_out,
        down_out,
        inner_out,
        basis_out,
        head_out,
    )


def solution(mesh):
    placed = (
        P("fsdp", "ctx", None),
        P("fsdp", "ctx", None),
        P("fsdp", "ctx"),
        P("fsdp", "ctx"),
        P(("fsdp", "ctx")),
        P(("fsdp", "ctx"), "tp"),
        P(("fsdp", "ctx"), None, "tp"),
        P(("fsdp", "ctx"), None, "tp"),
        P(("fsdp", "ctx"), None),
        P(("fsdp", "ctx"), "tp"),
        P(("tp", "fsdp", "ctx")),
        P(("fsdp", "ctx")),
        P(("fsdp", "ctx"), None, "tp"),
        P("tp", ("fsdp", "ctx")),
        P("tp", ("fsdp", "ctx")),
        P("tp", ("fsdp", "ctx")),
        P(None, ("tp", "fsdp", "ctx")),
        P(None, ("fsdp", "ctx")),
        P(None, "tp"),
    )
    return jax.shard_map(
        shards,
        mesh=mesh,
        in_specs=placed,
        out_specs=(
            P("fsdp", "ctx", None),
            P(),
            P("fsdp", "ctx", None),
            P(("fsdp", "ctx")),
            P(("fsdp", "ctx"), "tp"),
            P(("fsdp", "ctx"), None, "tp"),
            P(("fsdp", "ctx"), None, "tp"),
            P(("fsdp", "ctx"), None),
            P(("fsdp", "ctx"), "tp"),
            P(("tp", "fsdp", "ctx")),
            P(("fsdp", "ctx")),
            P(("fsdp", "ctx"), None, "tp"),
            P("tp", ("fsdp", "ctx")),
            P("tp", ("fsdp", "ctx")),
            P("tp", ("fsdp", "ctx")),
            P(None, ("tp", "fsdp", "ctx")),
            P(None, ("fsdp", "ctx")),
            P(None, "tp"),
        ),
        check_vma=False,
    )
```

```python
import functools

import jax
import jax.numpy as jnp
from jax import lax
from jax.experimental import pallas as pl
from jax.experimental.pallas import tpu as pltpu
from jax.sharding import PartitionSpec as P

MODEL_WIDTH = 1024
HEAD_SIZE = 64
HS = 24
DS = 128
KC = 4

eps = 1e-05
rope_base = 100000000000.0
masked_score = -1e30
f32 = jnp.float32
bf16 = jnp.bfloat16
CHUNK = 128
HALO = 128
VMEM_LIMIT = 40 * 2**20


def dot(left, right, left_dim, right_dim, precision=None):
    return lax.dot_general(
        left, right, (((left_dim,), (right_dim,)), ((), ())), precision=precision, preferred_element_type=f32
    )


def exact(left, right, left_dim, right_dim):
    return dot(left, right, left_dim, right_dim, lax.Precision.HIGHEST)


def low(value):
    return value.astype(bf16)


def factors():
    fsdp = lax.axis_size("fsdp")
    side = int(round(fsdp**0.5))
    if side * side != fsdp:
        side = 1
    return (
        ("fsdp", fsdp // side, side),
        ("fsdp", side, 1),
        ("ctx", lax.axis_size("ctx"), 1),
    )


def coordinate(dim):
    axis, size, stride = dim
    return lax.rem(lax.axis_index(axis) // stride, size)


def shifted(value, dim, step):
    axis, size, stride = dim
    pairs = []
    for source in range(lax.axis_size(axis)):
        at = source // stride % size
        pairs.append((source, source + ((at + step) % size - at) * stride))
    return lax.ppermute(value, axis, pairs)


def passed_along(value, axis, steps):
    count = lax.axis_size(axis)
    pairs = [(s, s + steps) for s in range(count) if 0 <= s + steps < count]
    return lax.ppermute(value, axis, pairs)


def swapped(value):
    return lax.ppermute(value, "tp", [(0, 1), (1, 0)])


def gathered_along(value, dim):
    size = dim[1]
    if size == 1:
        return value[None]
    at = coordinate(dim)
    if size == 2:
        other = shifted(value, dim, 1)
        return jnp.where(at == 0, jnp.stack([value, other]), jnp.stack([other, value]))
    pieces = [value] + [shifted(value, dim, s) for s in range(1, size)]
    ring = jnp.stack((pieces[::-1]) * 2)
    return lax.dynamic_slice_in_dim(ring, size - 1 - at, size, 0)


def tied(*values):
    return lax.optimization_barrier(values)


def gathered_line(shard, doubling=True):
    zdim = factors()[2]
    size = zdim[1]
    if not doubling or size & (size - 1):
        return gathered_along(shard, zdim)
    at = coordinate(zdim)
    value = shard[None]
    step = 1
    while step < size:
        other = lax.ppermute(value, zdim[0], [(i, i ^ step) for i in range(size)])
        pair = (jnp.concatenate([value, other]), jnp.concatenate([other, value]))
        value = jnp.where(at // step % 2 == 0, *pair)
        step *= 2
    return value


def plane_first(line):
    ydim, xdim, _ = factors()
    half = line.shape[-1] // 256 * 128
    return gathered_along(line[..., :half], ydim), gathered_along(line[..., half:], xdim)


def plane_second(one, two):
    ydim, xdim, _ = factors()
    one = jnp.swapaxes(gathered_along(one, xdim), 0, 1)
    two = gathered_along(two, ydim)
    whole = jnp.concatenate([one, two], axis=-1)
    return whole.reshape(-1, whole.shape[-1])


def gathered_plane(line):
    return plane_second(*plane_first(line))


def in_pair(value, kept):
    body, tail = value[..., :-128], value[..., -128:]
    whole = tail + jnp.roll(tail, 64, axis=-1)
    high = lax.reduce_precision(whole, 8, 7)
    rest = (whole - high).astype(bf16)
    high = high.astype(bf16)
    column = lax.broadcasted_iota(jnp.int32, tail.shape, tail.ndim - 1)
    tail = jnp.where(column < kept, tail.astype(bf16), jnp.where(column < 64, high, rest))
    return jnp.concatenate([body.astype(bf16), tail], axis=-1)


def reduced_along(value, dim, front, kept=None):
    size = dim[1]
    if size == 1:
        return lax.index_in_dim(value, 0, front, False)
    at = coordinate(dim)
    total = lax.dynamic_index_in_dim(value, at, front, False).astype(f32)
    for step in range(1, size):
        piece = lax.dynamic_index_in_dim(value, lax.rem(at + step, size), front, False)
        total = total + shifted(piece, dim, step).astype(f32)
    return total.astype(bf16) if kept is None else in_pair(total, kept)


def scatter_first(partial, kept=None):
    ydim, xdim, zdim = factors()
    columns = partial.shape[1]
    blocks = partial.reshape(ydim[1], xdim[1], zdim[1], -1, columns)
    half = columns // 256 * 128
    return reduced_along(blocks[..., :half], xdim, 1), reduced_along(blocks[..., half:], ydim, 0, kept)


def scatter_second(parts, kept=None):
    ydim, xdim, _ = factors()
    return reduced_along(parts[0], ydim, 0), reduced_along(parts[1], xdim, 0, kept)


def exchanged(blocks, step):
    zdim = factors()[2]
    upper = coordinate(zdim) // step % 2 == 1
    halves = blocks.reshape(2, step, *blocks.shape[1:])
    kept = jnp.where(upper, halves[1], halves[0])
    sent = jnp.where(upper, halves[0], halves[1])
    return kept, lax.ppermute(sent, zdim[0], [(i, i ^ step) for i in range(zdim[1])])


def halved(parts):
    blocks = jnp.concatenate(parts, axis=-1)
    return exchanged(blocks, blocks.shape[0] // 2)


def halved_on(kept, other):
    while True:
        total = kept.astype(f32) + other.astype(f32)
        if total.shape[0] == 1:
            return total[0]
        kept, other = exchanged(total.astype(bf16), total.shape[0] // 2)


def scatter_third(parts):
    zdim = factors()[2]
    blocks = jnp.concatenate(parts, axis=-1)
    at = coordinate(zdim)
    total = lax.dynamic_index_in_dim(blocks, at, 0, False).astype(f32)
    for step in range(1, zdim[1]):
        piece = lax.dynamic_index_in_dim(blocks, lax.rem(at + step, zdim[1]), 0, False)
        total = total + shifted(piece, zdim, step).astype(f32)
    return total


COSTS = {"prep_body": 1, "params_body": 1, "rope_body": 1, "attend_body": 9, "attend_back_body": 14, "conv_body": 7, "mix_body": 3,
    "gate_body": 3, "mix_back_body": 13, "conv_back_body": 8, "residual_body": 2, "input_body": 2}


def call(body, outs, scratch, *args):
    name = getattr(body, "func", body).__name__
    return pl.pallas_call(
        body,
        out_shape=[jax.ShapeDtypeStruct(s, d) for s, d in outs],
        in_specs=[pl.BlockSpec(memory_space=pltpu.VMEM)] * len(args),
        out_specs=[pl.BlockSpec(memory_space=pltpu.VMEM)] * len(outs),
        scratch_shapes=[pltpu.VMEM(s, d) for s, d in scratch],
        compiler_params=pltpu.CompilerParams(vmem_limit_bytes=VMEM_LIMIT),
        cost_estimate=pl.CostEstimate(flops=COSTS.get(name, 1) * 5 * 10**8, bytes_accessed=1000, transcendentals=0),
    )(*args)


def rotated(block, cosine, sine):
    half = block.shape[0] // 2
    one, two = block[:half], block[half:]
    return jnp.concatenate([one * cosine - two * sine, two * cosine + one * sine], axis=0)


def flipped(block):
    return jnp.transpose(block.astype(f32)).astype(block.dtype)


def block_scores(keys, query, low, at, back, width):
    scores = dot(keys, query, 1, 0)
    place = lax.broadcasted_iota(jnp.int32, scores.shape, 0) - back
    allowed = place >= low
    if back == 0:
        token = at + lax.broadcasted_iota(jnp.int32, scores.shape, 1)
        allowed = allowed & (place <= token)
    return jnp.where(allowed, scores, masked_score)


def attend_body(blocks, heads, q_ref, low_ref, *refs):
    kv = refs[:blocks]
    out_ref, log_ref, key_ref, score_ref = refs[blocks:]
    length = q_ref.shape[1]
    width = min(256, length)
    for j in range(blocks):
        key_ref[j] = flipped(kv[j][:HEAD_SIZE, :])

    @pl.loop(0, heads)
    def _(h):
        rows = pl.ds(pl.multiple_of(h * HEAD_SIZE, HEAD_SIZE), HEAD_SIZE)
        for at in range(0, length, width):
            lanes = slice(at, at + width)
            query = q_ref[rows, lanes]
            low = low_ref[0:1, lanes]
            top = jnp.full((1, width), masked_score, f32)
            for j in range(blocks):
                seen = length if j else at + width
                scores = block_scores(key_ref[j, :seen, :], query, low, at, j * length, width)
                score_ref[j, :seen, :] = scores
                top = jnp.maximum(top, jnp.max(scores, axis=0, keepdims=True))
            total = jnp.zeros((1, width), f32)
            mixed = jnp.zeros((HEAD_SIZE, width), f32)
            for j in range(blocks):
                seen = length if j else at + width
                weight = jnp.exp(score_ref[j, :seen, :] - top)
                total = total + jnp.sum(weight, axis=0, keepdims=True)
                mixed = mixed + dot(kv[j][HEAD_SIZE:, :seen], weight.astype(bf16), 1, 0)
            out_ref[rows, lanes] = (mixed / total).astype(bf16)
            log_ref[h, :, lanes] = jnp.broadcast_to(top + jnp.log(total), (8, width))


def attend(query, low, kv):
    heads, length = query.shape[0] // HEAD_SIZE, query.shape[1]
    width = min(256, length)
    return call(
        functools.partial(attend_body, len(kv), heads),
        [(query.shape, bf16), ((heads, 8, length), f32)],
        [((len(kv), length, HEAD_SIZE), bf16), ((len(kv), length, width), f32)],
        query, low, *kv,
    )


def attend_back_body(blocks, heads, q_ref, low_ref, out_ref, log_ref, g_ref, cos_ref, sin_ref, *refs):
    kv = refs[:blocks]
    gq_ref = refs[blocks]
    gkv = refs[blocks + 1 : 2 * blocks + 1]
    key_ref, value_ref, sum_ref = refs[2 * blocks + 1 :]
    length = q_ref.shape[1]
    width = min(256, length)
    for j in range(blocks):
        key_ref[j] = flipped(kv[j][:HEAD_SIZE, :])
        value_ref[j] = flipped(kv[j][HEAD_SIZE:, :])
    sum_ref[...] = jnp.zeros_like(sum_ref)

    @pl.loop(0, heads)
    def _(h):
        rows = pl.ds(pl.multiple_of(h * HEAD_SIZE, HEAD_SIZE), HEAD_SIZE)
        for at in range(0, length, width):
            lanes = slice(at, at + width)
            query = q_ref[rows, lanes]
            grad = g_ref[rows, lanes]
            low = low_ref[0:1, lanes]
            log_total = log_ref[h, 0:1, lanes]
            inner = jnp.sum(grad.astype(f32) * out_ref[rows, lanes].astype(f32), axis=0, keepdims=True)
            gq = jnp.zeros((HEAD_SIZE, width), f32)
            for j in range(blocks):
                seen = length if j else at + width
                scores = block_scores(key_ref[j, :seen, :], query, low, at, j * length, width)
                probs = jnp.exp(scores - log_total)
                grad_probs = dot(value_ref[j, :seen, :], grad, 1, 0)
                grad_scores = (probs * (grad_probs - inner)).astype(bf16)
                gq = gq + dot(kv[j][:HEAD_SIZE, :seen], grad_scores, 1, 0)
                sum_ref[j, :HEAD_SIZE, :seen] += dot(query, grad_scores, 1, 1)
                sum_ref[j, HEAD_SIZE:, :seen] += dot(grad, probs.astype(bf16), 1, 1)
            gq = rotated(gq * HEAD_SIZE**-0.5, cos_ref[:, lanes], -sin_ref[:, lanes])
            gq_ref[rows, lanes] = gq.astype(bf16)

    for j in range(blocks):
        gkv[j][...] = sum_ref[j].astype(gkv[j].dtype)


def attend_back(query, low, out, log_total, grad, cosine, sine, kv):
    heads, length = query.shape[0] // HEAD_SIZE, query.shape[1]
    blocks = len(kv)
    return call(
        functools.partial(attend_back_body, blocks, heads),
        [(query.shape, bf16)] + [((2 * HEAD_SIZE, length), bf16)] * blocks,
        [((blocks, length, HEAD_SIZE), bf16)] * 2 + [((blocks, 2 * HEAD_SIZE, length), f32)],
        query, low, out, log_total, grad, cosine, sine, *kv,
    )


def pack_body(q_ref, kv_ref, bc_ref, step_ref, gains_ref, ssm_ref, inner_ref, basis_ref, valid_ref, out_ref, small_ref):
    rows, heads = step_ref.shape
    small_ref[...] = jnp.zeros_like(small_ref)
    small_ref[heads : heads + 2, :rows] = gains_ref[...].astype(f32)
    small_ref[heads + 2 : heads + 3, : ssm_ref.shape[1]] = ssm_ref[...].astype(f32)
    small_ref[heads + 3 : heads + 3 + KC, : inner_ref.shape[1]] = inner_ref[...].astype(f32)
    small_ref[heads + 3 + KC : heads + 3 + 2 * KC, : basis_ref.shape[1]] = basis_ref[...].astype(f32)
    count = jnp.sum(valid_ref[...].astype(f32), axis=1, keepdims=True)
    high = jnp.floor(count * (1.0 / 16.0))
    small_ref[heads + 3 + 2 * KC : heads + 4 + 2 * KC, 0:1] = high
    small_ref[heads + 4 + 2 * KC : heads + 5 + 2 * KC, 0:1] = count - 16.0 * high
    tail = jnp.transpose(small_ref[...])[:rows, :]
    step = jnp.concatenate([step_ref[...].astype(f32), jnp.zeros((rows, 128 - heads), f32)], axis=1)
    at = 0
    for ref in (q_ref, kv_ref, bc_ref):
        out_ref[:, at : at + ref.shape[1]] = ref[...]
        at += ref.shape[1]
    out_ref[:, at:] = (tail + step).astype(bf16)


def packed(*args):
    columns = sum(a.shape[1] for a in args[:3]) + 128
    return call(pack_body, [((args[0].shape[0], columns), bf16)], [((128, 128), f32)], *args)[0]


def prep_body(x_ref, before_ref, xt_ref, scale_ref):
    length = x_ref.shape[0]
    for at in range(-HALO, length, HALO):
        if at < 0:
            first = HALO - before_ref.shape[0]
            block = jnp.concatenate([jnp.zeros((first, x_ref.shape[1]), f32), before_ref[...].astype(f32)], axis=0)
        else:
            block = x_ref[at : at + HALO, :].astype(f32)
        block = jnp.transpose(block)
        lanes = slice(at + HALO, at + 2 * HALO)
        xt_ref[:, lanes] = block.astype(bf16)
        mean = jnp.mean(block * block, axis=0, keepdims=True)
        scale_ref[:, lanes] = jnp.broadcast_to(lax.rsqrt(mean + eps), (8, HALO))


def prepared(x, before):
    length, features = x.shape
    return call(prep_body, [((features, length + HALO), bf16), ((8, length + HALO), f32)], [], x, before)


def params_body(shape, w_ref, xt_ref, scale_ref, inner_ref, basis_ref, gains_ref, n1_ref):
    ways, rows, inner_rows, bc_rows, heads, step_at = shape
    tail = w_ref[:, step_at:].astype(f32)
    for s in range(ways):
        inner_ref[s * inner_rows : (s + 1) * inner_rows, :] = tail[s * rows : s * rows + inner_rows, :]
        basis_ref[s * bc_rows : (s + 1) * bc_rows, :] = tail[s * rows : s * rows + bc_rows, :]
    gains_ref[...] = jnp.transpose(tail)
    for at in range(0, xt_ref.shape[1], HALO):
        lanes = slice(at, at + HALO)
        normed = xt_ref[:, lanes].astype(f32) * scale_ref[0:1, lanes] * tail[:, heads : heads + 1]
        n1_ref[:, lanes] = normed.astype(bf16)


def unpacked(shape, first_w, xt, scale):
    ways, rows, inner_rows, bc_rows, heads, step_at = shape
    return call(
        functools.partial(params_body, shape),
        [((ways * inner_rows, 128), f32), ((ways * bc_rows, 128), f32), ((128, ways * rows), f32), (xt.shape, bf16)],
        [],
        first_w, xt, scale,
    )


def rope_body(attn_width, lin_ref, cos_ref, sin_ref, q_ref, kv_ref):
    cosine, sine = cos_ref[...], sin_ref[...]
    for at in range(0, attn_width, HEAD_SIZE):
        query = rotated(lin_ref[at : at + HEAD_SIZE, HALO:], cosine, sine)
        q_ref[at : at + HEAD_SIZE, :] = query.astype(bf16) * bf16(HEAD_SIZE**-0.5)
    keys = lin_ref[attn_width : attn_width + HEAD_SIZE, HALO:]
    kv_ref[:HEAD_SIZE, :] = rotated(keys, cosine, sine).astype(bf16)
    kv_ref[HEAD_SIZE:, :] = lin_ref[attn_width + HEAD_SIZE : attn_width + 2 * HEAD_SIZE, HALO:].astype(bf16)


def roped(attn_width, first_lin, cosine, sine):
    length = cosine.shape[1]
    return call(
        functools.partial(rope_body, attn_width),
        [((attn_width, length), bf16), ((2 * HEAD_SIZE, length), bf16)],
        [],
        first_lin, cosine, sine,
    )


def conv_pre(block, taps, places):
    total = None
    for lag in range(KC):
        back = KC - 1 - lag
        moved = pltpu.roll(block, back, 1) if back else block
        term = taps[:, lag : lag + 1] * moved[:, HALO:]
        if back:
            term = jnp.where(places >= back, term, 0.0)
        total = term if total is None else total + term
    return total


def sigmoid(value):
    return 1.0 / (1.0 + jnp.exp(-value))


def running_sum(value, reverse=False):
    width = value.shape[1]
    lane = lax.broadcasted_iota(jnp.int32, value.shape, 1)
    step = 1
    while step < width:
        if reverse:
            value = value + jnp.where(lane < width - step, pltpu.roll(value, width - step, 1), 0.0)
        else:
            value = value + jnp.where(lane >= step, pltpu.roll(value, step, 1), 0.0)
        step *= 2
    return value


def widened(rows):
    return jnp.transpose(jnp.concatenate([rows, jnp.zeros((112, rows.shape[1]), f32)], axis=0))


def pack_decay(ref, decay, first):
    wide = jnp.broadcast_to(decay, (16, DS))
    high = wide.astype(bf16)
    ref[first : first + 16, :] = high
    ref[first + 16 : first + 32, :] = (wide - high.astype(f32)).astype(bf16)


def chain(packs, heads, state_ref):
    width = heads * HEAD_SIZE
    for h in range(heads):
        rows = slice(h * HEAD_SIZE, (h + 1) * HEAD_SIZE)
        state = jnp.zeros((HEAD_SIZE, DS), f32)
        for pack in packs[::-1]:
            decay = pack[width : width + 16, :].astype(f32) + pack[width + 16 : width + 32, :].astype(f32)
            state = pack[rows, :].astype(f32) + decay[h : h + 1, :] * state
        state_ref[rows, :] = state


def conv_body(heads, bc_at, u_ref, lin_ref, inner_ref, basis_ref, hp_ref, place_ref, xs_ref, b_ref, c_ref, bt_ref, ct_ref, dt_ref, cum_ref, cumt_ref, pack_ref, end_ref):
    places = place_ref[0:1, :]
    length = places.shape[1]
    width = heads * HEAD_SIZE
    for at, flat, side in ((0, b_ref, bt_ref), (DS, c_ref, ct_ref)):
        taps = basis_ref[at : at + DS, heads + 3 + KC : heads + 3 + 2 * KC]
        pre = conv_pre(lin_ref[bc_at + at : bc_at + at + DS, :], taps, places)
        basis = pre * sigmoid(pre)
        side[...] = basis
        flat[...] = jnp.transpose(basis)
    raw = lin_ref[bc_at + 2 * DS : bc_at + 2 * DS + 16, HALO:] + hp_ref[:, 0:1]
    dt = jnp.maximum(raw, 0.0) + jnp.log1p(jnp.exp(-jnp.abs(raw)))
    cum = running_sum(dt * -jnp.exp(hp_ref[:, 1:2]))
    dt_ref[...] = dt
    cum_ref[...] = cum
    cumt_ref[...] = widened(cum)
    last = cum[:, length - 1 :]
    lane = lax.broadcasted_iota(jnp.int32, (1, length), 1)
    last_place = places[:, length - 1 :]
    reach = lane >= length - 1 - last_place
    to_end = jnp.where(reach, jnp.exp(jnp.minimum(last - cum, 0.0)) * dt, 0.0)
    end_ref[...] = to_end

    def one(h, _):
        rows = pl.ds(pl.multiple_of(h * HEAD_SIZE, HEAD_SIZE), HEAD_SIZE)
        pre = conv_pre(u_ref[rows, :], inner_ref[rows, :][:, heads + 3 : heads + 3 + KC], places)
        values = pre * sigmoid(pre)
        xs_ref[rows, :] = values
        summary = dot((values * end_ref[pl.ds(h, 1), :]).astype(bf16), low(b_ref[...]), 1, 0)
        pack_ref[rows, :] = summary.astype(bf16)
        return 0

    lax.fori_loop(0, heads, one, 0)
    keep = (last_place > length - 1).astype(f32)
    pack_decay(pack_ref, jnp.exp(last) * keep, width)


def conv_forward(heads, bc_at, u, lin, inner, basis, hp, places):
    length = places.shape[1]
    width = heads * HEAD_SIZE
    return call(
        functools.partial(conv_body, heads, bc_at),
        [
            ((width, length), f32),
            ((length, DS), f32),
            ((length, DS), f32),
            ((DS, length), f32),
            ((DS, length), f32),
            ((16, length), f32),
            ((16, length), f32),
            ((length, 128), f32),
            ((width + 32, DS), bf16),
        ],
        [((16, length), f32)],
        u, lin, inner, basis, hp, places,
    )


def chunk_rows(k, cum_ref, place_ref):
    lanes = slice(k * CHUNK, (k + 1) * CHUNK)
    cum = cum_ref[:, lanes]
    places = place_ref[0:1, lanes]
    base = cum_ref[:, k * CHUNK - 1 : k * CHUNK] if k else jnp.zeros((16, 1), f32)
    last = cum[:, CHUNK - 1 :]
    last_place = places[:, CHUNK - 1 :]
    lane = lax.broadcasted_iota(jnp.int32, (1, CHUNK), 1)
    entry = jnp.where(places > lane, jnp.exp(jnp.minimum(cum - base, 0.0)), 0.0)
    to_end = jnp.where(lane >= CHUNK - 1 - last_place, jnp.exp(jnp.minimum(last - cum, 0.0)), 0.0)
    over = jnp.where(last_place > CHUNK - 1, jnp.exp(jnp.minimum(last - base, 0.0)), 0.0)
    source = lax.broadcasted_iota(jnp.int32, (CHUNK, CHUNK), 0)
    target = lax.broadcasted_iota(jnp.int32, (CHUNK, CHUNK), 1)
    allowed = (source <= target) & (source >= target - places)
    return cum, entry, to_end, over, allowed


def mix_body(heads, packs, xs_ref, b_ref, ct_ref, dt_ref, cum_ref, cumt_ref, hp_ref, place_ref, z_ref, *refs):
    pack_refs = refs[:packs]
    y_ref, states_ref, squares_ref, state_ref, inter_ref, w_ref = refs[packs:]
    length = place_ref.shape[1]
    chain(pack_refs, heads, state_ref)
    for k in range(length // CHUNK):
        lanes = slice(k * CHUNK, (k + 1) * CHUNK)
        cum, entry, to_end, over, allowed = chunk_rows(k, cum_ref, place_ref)
        low_state = state_ref[...].astype(bf16)
        states_ref[k] = low_state
        side = ct_ref[:, lanes]
        match = jnp.where(allowed, exact(b_ref[lanes, :], side, 1, 0), 0.0)
        inter_ref[...] = dot(low_state, low(side), 1, 0)
        squares = jnp.zeros((1, CHUNK), f32)
        for h in range(heads):
            rows = slice(h * HEAD_SIZE, (h + 1) * HEAD_SIZE)
            spread = cum[h : h + 1, :] - cumt_ref[lanes, h : h + 1]
            mixing = (jnp.exp(jnp.minimum(spread, 0.0)) * match).astype(bf16)
            values = xs_ref[rows, lanes]
            stepped = values * dt_ref[h : h + 1, lanes]
            result = dot(stepped.astype(bf16), mixing, 1, 0)
            result = result + inter_ref[rows, :] * entry[h : h + 1, :] + hp_ref[h : h + 1, 2:3] * values
            y_ref[rows, lanes] = result
            w_ref[rows, :] = (stepped * to_end[h : h + 1, :]).astype(bf16)
            gate = z_ref[rows, lanes]
            gated = result * gate * sigmoid(gate)
            squares = squares + jnp.sum(gated * gated, axis=0, keepdims=True)
        squares_ref[:, lanes] = jnp.broadcast_to(squares, (8, CHUNK))
        if k + 1 < length // CHUNK:
            added = dot(w_ref[...], low(b_ref[lanes, :]), 1, 0)
            for h in range(heads):
                rows = slice(h * HEAD_SIZE, (h + 1) * HEAD_SIZE)
                state_ref[rows, :] = over[h : h + 1, :] * state_ref[rows, :] + added[rows, :]


def mix_forward(heads, xs, b, ct, dt, cum, cumt, hp, places, z, packs):
    length = places.shape[1]
    width = heads * HEAD_SIZE
    return call(
        functools.partial(mix_body, heads, len(packs)),
        [
            ((width, length), f32),
            ((length // CHUNK, width, DS), bf16),
            ((8, length), f32),
        ],
        [((width, DS), f32), ((width, CHUNK), f32), ((width, CHUNK), bf16)],
        xs, b, ct, dt, cum, cumt, hp, places, z, *packs,
    )


def gate_body(heads, g_ref, y_ref, z_ref, gain_ref, inv_ref, dot_ref, c_ref, cum_ref, place_ref, gy_ref, gz_ref, ggain_ref, pack_ref, entry_ref):
    length = place_ref.shape[1]
    width = heads * HEAD_SIZE
    first = g_ref.shape[0] - width
    places = place_ref[0:1, :]
    inv = inv_ref[0:1, :]
    shrink = inv * inv * inv * dot_ref[0:1, :] * (1.0 / (HS * HEAD_SIZE))
    lane = lax.broadcasted_iota(jnp.int32, (1, length), 1)
    entry_ref[...] = jnp.where(places > lane, jnp.exp(jnp.minimum(cum_ref[...], 0.0)), 0.0)

    def one(h, _):
        start = pl.multiple_of(h * HEAD_SIZE, HEAD_SIZE)
        rows = pl.ds(start, HEAD_SIZE)
        grad = g_ref[pl.ds(start + first, HEAD_SIZE), :] * inv
        values = y_ref[rows, :]
        gate = z_ref[rows, :]
        sig = sigmoid(gate)
        silu = gate * sig
        gated = values * silu
        column = lax.broadcasted_iota(jnp.int32, (HEAD_SIZE, 128), 1)
        ggain_ref[rows, :] = jnp.where(column == heads + 2, jnp.sum(grad * gated, axis=1, keepdims=True), 0.0)
        grad_gated = grad * gain_ref[rows, :][:, heads + 2 : heads + 3] - shrink * gated
        grad_values = grad_gated * silu
        gy_ref[rows, :] = grad_values
        gz_ref[rows, :] = (grad_gated * values * sig * (1.0 + gate * (1.0 - sig))).astype(bf16)
        entered = (grad_values * entry_ref[pl.ds(h, 1), :]).astype(bf16)
        pack_ref[rows, :] = dot(entered, low(c_ref[...]), 1, 0).astype(bf16)
        return 0

    lax.fori_loop(0, heads, one, 0)
    last = length - 1
    keep = (places[:, last:] > last).astype(f32)
    pack_decay(pack_ref, jnp.exp(cum_ref[:, last:]) * keep, width)


def gate_back(heads, grads, y, z, gain, inv, inner, c, cum, places):
    length = places.shape[1]
    width = heads * HEAD_SIZE
    return call(
        functools.partial(gate_body, heads),
        [
            ((width, length), f32),
            ((width, length), bf16),
            ((width, 128), f32),
            ((width + 32, DS), bf16),
        ],
        [((16, length), f32)],
        grads, y, z, gain, inv, inner, c, cum, places,
    )


def mix_back_body(heads, packs, step_at, gy_ref, xs_ref, b_ref, c_ref, bt_ref, ct_ref, dt_ref, cum_ref, cumt_ref, lin_ref, hp_ref, place_ref, states_ref, *refs):
    pack_refs = refs[:packs]
    gxs_ref, gbc_ref, gstep_ref, grow_ref, ghead_ref, grad_ref, reach_ref, inter_ref, gye_ref, w_ref, col_ref, cumg_ref, dtg_ref = refs[packs:]
    length = place_ref.shape[1]
    chain(pack_refs, heads, grad_ref)
    col_ref[...] = jnp.zeros_like(col_ref)
    cumg_ref[...] = jnp.zeros_like(cumg_ref)
    dtg_ref[...] = jnp.zeros_like(dtg_ref)
    rate = -jnp.exp(hp_ref[:, 1:2])
    bias_sum = jnp.zeros((16, CHUNK), f32)
    rate_sum = jnp.zeros((16, CHUNK), f32)
    ghead_ref[...] = jnp.zeros_like(ghead_ref)
    at_last = lax.broadcasted_iota(jnp.int32, (1, CHUNK), 1) == CHUNK - 1
    for k in reversed(range(length // CHUNK)):
        lanes = slice(k * CHUNK, (k + 1) * CHUNK)
        cum, entry, to_end, over, allowed = chunk_rows(k, cum_ref, place_ref)
        b_side, c_side = bt_ref[:, lanes], ct_ref[:, lanes]
        b_flat, c_flat = b_ref[lanes, :], c_ref[lanes, :]
        match = jnp.where(allowed, exact(b_flat, c_side, 1, 0), 0.0)
        low_grad = grad_ref[...].astype(bf16)
        reach_ref[...] = dot(low_grad, low(b_side), 1, 0)
        inter_ref[...] = dot(states_ref[k], low(c_side), 1, 0)
        grad_match = jnp.zeros((CHUNK, CHUNK), f32)
        for h in range(heads):
            rows = slice(h * HEAD_SIZE, (h + 1) * HEAD_SIZE)
            head = slice(h, h + 1)
            grad = gy_ref[rows, lanes]
            values = xs_ref[rows, lanes]
            dt = dt_ref[head, lanes]
            stepped = values * dt
            decay = jnp.exp(jnp.minimum(cum[head, :] - cumt_ref[lanes, head], 0.0))
            mixing = decay * match
            low_y = grad.astype(bf16)
            grad_mixing = dot(stepped.astype(bf16), low_y, 0, 0)
            grad_match = grad_match + grad_mixing * decay
            spread = grad_mixing * mixing
            to = to_end[head, :]
            reached = reach_ref[rows, :] * to
            grad_stepped = dot(low_y, mixing.astype(bf16), 1, 1) + reached
            ended = jnp.sum(reached * stepped, axis=0, keepdims=True)
            entered = grad * entry[head, :]
            entry_sum = jnp.sum(entered * inter_ref[rows, :], axis=0, keepdims=True)
            kept = over[head, :] * jnp.sum(
                jnp.sum(grad_ref[rows, :] * states_ref[k, rows, :].astype(f32), axis=0, keepdims=True),
                axis=1, keepdims=True,
            )
            at_end = jnp.sum(ended, axis=1, keepdims=True) + kept
            cumg_ref[head, :] = (
                jnp.sum(spread, axis=0, keepdims=True) + entry_sum - ended + jnp.where(at_last, at_end, 0.0)
            )
            col_ref[:, head] = jnp.sum(spread, axis=1, keepdims=True)
            dtg_ref[head, :] = jnp.sum(grad_stepped * values, axis=0, keepdims=True)
            gxs_ref[rows, lanes] = grad_stepped * dt + hp_ref[head, 2:3] * grad
            ghead_ref[head, 2:3] += jnp.sum(
                jnp.sum(grad * values, axis=0, keepdims=True), axis=1, keepdims=True
            )
            gye_ref[rows, :] = entered.astype(bf16)
            w_ref[rows, :] = (stepped * to).astype(bf16)
        low_match = jnp.where(allowed, grad_match, 0.0)
        gbc_ref[:DS, lanes] = exact(c_side, low_match, 1, 1) + dot(low_grad, w_ref[...], 0, 0)
        gbc_ref[DS:, lanes] = exact(b_side, low_match, 1, 0) + dot(states_ref[k], gye_ref[...], 0, 0)
        if k:
            added = dot(gye_ref[...], low(c_flat), 1, 0)
            for h in range(heads):
                rows = slice(h * HEAD_SIZE, (h + 1) * HEAD_SIZE)
                grad_ref[rows, :] = over[h : h + 1, :] * grad_ref[rows, :] + added[rows, :]
        grad_log = running_sum(cumg_ref[...] - jnp.transpose(col_ref[...])[:16, :], reverse=True)
        dt = dt_ref[:, lanes]
        rate_sum = rate_sum + grad_log * dt
        grad_step = (dtg_ref[...] + grad_log * rate) * sigmoid(lin_ref[step_at : step_at + 16, HALO:][:, lanes] + hp_ref[:, 0:1])
        gstep_ref[:, lanes] = grad_step
        bias_sum = bias_sum + grad_step
    ghead_ref[:, 0:1] = jnp.sum(bias_sum, axis=1, keepdims=True)
    ghead_ref[:, 1:2] = jnp.sum(rate_sum, axis=1, keepdims=True) * rate
    side = jnp.transpose(jnp.concatenate([ghead_ref[...], jnp.zeros((112, 128), f32)], axis=0))
    lane = lax.broadcasted_iota(jnp.int32, (8, 128), 1)
    row = jnp.zeros((8, 128), f32)
    for j in range(3):
        own = jnp.where(lane < heads, jnp.broadcast_to(side[j : j + 1, :], (8, 128)), 0.0)
        row = row + pltpu.roll(own, heads + 3 + 2 * KC + j * heads, 1)
    grow_ref[...] = row


def mix_back(heads, step_at, gy, xs, b, c, bt, ct, dt, cum, cumt, lin, hp, places, states, packs):
    length = places.shape[1]
    width = heads * HEAD_SIZE
    return call(
        functools.partial(mix_back_body, heads, len(packs), step_at),
        [
            ((width, length), f32),
            ((2 * DS, length), f32),
            ((16, length), f32),
            ((8, 128), f32),
        ],
        [
            ((16, 128), f32),
            ((width, DS), f32),
            ((width, CHUNK), f32),
            ((width, CHUNK), f32),
            ((width, CHUNK), bf16),
            ((width, CHUNK), bf16),
            ((CHUNK, 128), f32),
            ((16, CHUNK), f32),
            ((16, CHUNK), f32),
        ],
        gy, xs, b, c, bt, ct, dt, cum, cumt, lin, hp, places, states, *packs,
    )


def conv_back_body(heads, bc_at, u_ref, lin_ref, gxs_ref, gbc_ref, inner_ref, basis_ref, place_ref, g_ref, halo_ref, ginner_ref, gbasis_ref):
    places = place_ref[0:1, :]
    length = places.shape[1]
    width = u_ref.shape[0]

    def one(block, grads, taps, first, sums_ref, at):
        pre = conv_pre(block, taps, places)
        sig = sigmoid(pre)
        grad_pre = grads * sig * (1.0 + pre * (1.0 - sig))
        total = None
        for lag in range(KC):
            back = KC - 1 - lag
            counted = jnp.where(places >= back, grad_pre, 0.0) if back else grad_pre
            moved = pltpu.roll(block, back, 1) if back else block
            sums_ref[at, first + lag : first + lag + 1] = jnp.sum(counted * moved[:, HALO:], axis=1, keepdims=True)
            wide = jnp.concatenate([jnp.zeros((counted.shape[0], HALO), f32), counted * taps[:, lag : lag + 1]], axis=1)
            wide = pltpu.roll(wide, length + HALO - back, 1) if back else wide
            total = wide if total is None else total + wide
        return total[:, HALO:], jnp.transpose(total[:, :HALO])[HALO - 8 :, :]

    ginner_ref[...] = jnp.zeros_like(ginner_ref)
    gbasis_ref[...] = jnp.zeros_like(gbasis_ref)

    def inner(i, _):
        start = pl.multiple_of(i * 128, 128)
        rows = pl.ds(start, 128)
        taps = inner_ref[rows, :][:, heads + 3 : heads + 3 + KC]
        own, halo = one(u_ref[rows, :], gxs_ref[rows, :], taps, heads + 3, ginner_ref, rows)
        g_ref[rows, :] = own
        halo_ref[:, pl.ds(start, 128)] = halo
        return 0

    lax.fori_loop(0, width // 128, inner, 0)
    for i in range(0, 2 * DS, 128):
        rows = slice(i, i + 128)
        first = heads + 3 + KC
        block = lin_ref[bc_at + i : bc_at + i + 128, :]
        own, halo = one(block, gbc_ref[rows, :], basis_ref[rows, first : first + KC], first, gbasis_ref, rows)
        g_ref[width + i : width + i + 128, :] = own
        halo_ref[:, width + i : width + i + 128] = halo


def conv_back(heads, bc_at, u, lin, gxs, gbc, inner, basis, places):
    length = places.shape[1]
    width = u.shape[0]
    return call(
        functools.partial(conv_back_body, heads, bc_at),
        [((width + 2 * DS, length), f32), ((8, width + 2 * DS), f32), ((width, 128), f32), ((2 * DS, 128), f32)],
        [],
        u, lin, gxs, gbc, inner, basis, places,
    )


def early_body(pieces, n1_ref, gq_ref, gz_ref, cos_ref, sin_ref, first_ref, z_ref, *refs):
    kv_refs = refs[:pieces]
    gw_ref, gn_ref = refs[pieces:]
    n1 = n1_ref[:, HALO:]
    gkv = kv_refs[0][...].astype(f32)
    for ref in kv_refs[1:]:
        gkv = gkv + ref[...].astype(f32)
    gkv = jnp.concatenate([rotated(gkv[:HEAD_SIZE], cos_ref[...], -sin_ref[...]), gkv[HEAD_SIZE:]], axis=0).astype(bf16)
    at = 0
    total = None
    for grad, weights in ((gz_ref[...], z_ref[...]), (gq_ref[...], first_ref), (gkv, first_ref)):
        rows = grad.shape[0]
        gw_ref[:, at : at + rows] = dot(n1, grad, 1, 1).astype(bf16)
        if weights is first_ref:
            first = at - gz_ref.shape[0]
            weights = first_ref[:, first : first + rows]
        term = dot(weights, grad, 1, 0)
        total = term if total is None else total + term
        at += rows
    gn_ref[...] = total.astype(bf16)


def rows_call(body, outs, cuts, *args):
    blocks = 4

    def spec(shape, cut=0):
        if cut is None:
            return pl.BlockSpec(shape, lambda i: (0,) * len(shape))
        if cut == 1:
            return pl.BlockSpec((shape[0], shape[1] // blocks), lambda i: (0, i))
        return pl.BlockSpec((shape[0] // blocks, cut or shape[1]), lambda i: (i, 0))

    return pl.pallas_call(
        body,
        grid=(blocks,),
        out_shape=[jax.ShapeDtypeStruct(s, d) for s, d in outs],
        in_specs=[spec(a.shape, cut) for a, cut in zip(args, cuts, strict=True)],
        out_specs=[spec(s) for s, _ in outs],
        compiler_params=pltpu.CompilerParams(vmem_limit_bytes=VMEM_LIMIT),
        cost_estimate=pl.CostEstimate(flops=4 * 5 * 10**8, bytes_accessed=1000, transcendentals=0),
    )(*args)


def early_products(n1, gq, gz, cosine, sine, first_w, last_w, gkv):
    features, length = n1.shape[0], gq.shape[1]
    columns = gq.shape[0] + gkv[0].shape[0] + gz.shape[0]
    return rows_call(
        functools.partial(early_body, len(gkv)),
        [((features, columns), bf16), ((features, length), bf16)],
        (0, None, None, None, None, 0, gz.shape[0]) + (None,) * len(gkv),
        n1, gq, gz, cosine, sine, first_w, last_w, *gkv,
    )


def join_body(width, heads, g_ref, behind_ref, step_ref, low_ref):
    length = g_ref.shape[1]
    if length > 128:
        low_ref[: g_ref.shape[0], : length - 128] = g_ref[:, : length - 128].astype(bf16)
    behind = jnp.concatenate([jnp.zeros((120, behind_ref.shape[1]), f32), behind_ref[...]], axis=0)
    low_ref[: g_ref.shape[0], length - 128 :] = (g_ref[:, length - 128 :] + jnp.transpose(behind)).astype(bf16)
    row = lax.broadcasted_iota(jnp.int32, (16, length), 0)
    step = jnp.where(row < heads, step_ref[...], 0.0)
    low_ref[g_ref.shape[0] :, :] = jnp.concatenate([step, jnp.zeros((112, length), f32)], axis=0).astype(bf16)


def joined(heads, grads, behind, step):
    rows, length = grads.shape
    return call(functools.partial(join_body, rows, heads), [((rows + 128, length), bf16)], [], grads, behind, step)[0]


def late_body(shape, width, rest_at, n1_ref, xt_ref, scale_ref, g_ref, first_ref, u_ref, gn_ref, two_ref, inner_a_ref, inner_b_ref, basis_ref, head_ref, loss_ref, gw_ref, low_ref, tail_ref):
    rows, inner_rows, bc_rows, heads = shape
    grad = g_ref[...]
    columns = grad.shape[0]
    made = dot(n1_ref[:, HALO:], grad, 1, 1)
    gw_ref[:, : columns - 128] = made[:, : columns - 128].astype(bf16)
    total = gn_ref[...].astype(f32) + dot(u_ref[:, width:], grad[:width], 1, 0) + dot(first_ref[:, rest_at:], grad[width:], 1, 0)
    low_ref[...] = total.astype(bf16)
    scaled = xt_ref[:, HALO:].astype(f32) * scale_ref[0:1, HALO:]
    column = lax.broadcasted_iota(jnp.int32, tail_ref.shape, 1)
    one = jnp.sum(total * scaled, axis=1, keepdims=True)
    two = jnp.concatenate([two_ref[...], jnp.zeros((120, two_ref.shape[1]), f32)], axis=0)
    two = jnp.transpose(two)[:, 0:1]
    tail_ref[...] = made[:, columns - 128 :] + jnp.where(column == heads, one, jnp.where(column == heads + 1, two, 0.0))
    for s in range(tail_ref.shape[0] // rows):
        inner = slice(s * inner_rows, (s + 1) * inner_rows)
        tail_ref[s * rows : s * rows + inner_rows, :] += inner_a_ref[inner, :] + inner_b_ref[inner, :]
        tail_ref[s * rows : s * rows + bc_rows, :] += basis_ref[s * bc_rows : (s + 1) * bc_rows, :]
        tail_ref[s * rows : s * rows + 1, :] += head_ref[0:1, :] + loss_ref[0:1, :]
    value = tail_ref[...]
    high = value.astype(bf16).astype(f32)
    rest = pltpu.roll(value - high, 64, 1)
    gw_ref[:, columns - 128 :] = jnp.where(column < 64, high, jnp.where(column < 64 + heads, 0.0, rest)).astype(bf16)


def late_products(shape, width, rest_at, n1, xt, scale, grads, first_w, u_w, gn, two, inner_a, inner_b, basis, head, loss):
    features, length = gn.shape
    return rows_call(
        functools.partial(late_body, shape, width, rest_at),
        [((features, grads.shape[0]), bf16), ((features, length), bf16), ((features, 128), f32)],
        (0, 0, None, None, 0, 0, 0, 1, 0, 0, 0, None, None),
        n1, xt, scale, grads, first_w, u_w, gn, two, inner_a, inner_b, basis, head, loss,
    )[:2]


def finish_body(shape, total_ref, other_ref, count_ref, bc_ref, norm_ref, step_ref, ssm_ref, two_ref, inner_ref, basis_ref, head_ref, loss_ref):
    rows, inner_rows, bc_rows, heads, bc_at = shape
    bc_width = bc_ref.shape[1]
    bc_ref[...] = total_ref[:, bc_at : bc_at + bc_width] + other_ref[:, :bc_width]
    tail = total_ref[:, bc_at + bc_width :]
    own = jnp.where(lax.broadcasted_iota(jnp.int32, tail.shape, 1) < heads, tail, tail + pltpu.roll(tail, 64, 1))
    step_ref[...] = own[:, :heads]
    other = other_ref[:, bc_width:]
    both = own + other + pltpu.roll(other, 64, 1)
    own = jnp.concatenate([own, jnp.zeros((128 - rows, 128), f32)], axis=0) if rows < 128 else own
    both = jnp.concatenate([both, jnp.zeros((128 - rows, 128), f32)], axis=0) if rows < 128 else both
    side, side_both = jnp.transpose(own), jnp.transpose(both)
    norm_ref[...] = side_both[heads : heads + 1, :rows]
    two_ref[...] = side[heads + 1 : heads + 2, :rows]
    ssm_ref[...] = side[heads + 2 : heads + 3, :inner_rows]
    inner_ref[...] = side[heads + 3 : heads + 3 + KC, :inner_rows]
    basis_ref[...] = side_both[heads + 3 + KC : heads + 3 + 2 * KC, :bc_rows]
    at = heads + 3 + 2 * KC
    for j in range(3):
        head_ref[j : j + 1, :] = own[0:1, at + j * heads : at + (j + 1) * heads]
    loss_ref[...] = own[0:1, at + 3 * heads : at + 3 * heads + 1] / (count_ref[0:1, 0:1] * MODEL_WIDTH)


def finished(shape, total, other, count):
    rows, inner_rows, bc_rows, heads, _ = shape
    return call(
        functools.partial(finish_body, shape),
        [
            ((rows, 2 * DS), f32),
            ((1, rows), f32),
            ((rows, heads), f32),
            ((1, inner_rows), f32),
            ((1, rows), f32),
            ((KC, inner_rows), f32),
            ((KC, bc_rows), f32),
            ((3, heads), f32),
            ((1, 1), f32),
        ],
        [],
        total, other, count,
    )


def input_body(own_ref, low_ref, x_ref, res_ref, gain_ref, out_ref):
    length = x_ref.shape[0]
    for at in range(0, length, HALO):
        rows = slice(at, at + HALO)
        grad = jnp.transpose(own_ref[:, rows].astype(f32) + low_ref[:, rows].astype(f32)) * gain_ref[0:1, :]
        x = x_ref[rows, :].astype(f32)
        scale = lax.rsqrt(jnp.mean(x * x, axis=1, keepdims=True) + eps)
        inner = jnp.mean(grad * x, axis=1, keepdims=True)
        out_ref[rows, :] = res_ref[rows, :] + scale * grad - scale * scale * scale * x * inner


def input_grad(own, low, x, res, gain):
    return call(input_body, [(x.shape, f32)], [], own, low, x, res, gain)[0]


def mlp_grads_body(n2_ref, e_ref, ggu_ref, m_ref, out_ref):
    both = ggu_ref.shape[1]
    out_ref[:, :both] = dot(n2_ref[...], ggu_ref[...], 0, 0).astype(bf16)
    out_ref[:, both:] = dot(e_ref[...], m_ref[...], 0, 0).astype(bf16)


def mlp_weight_grads(n2, e, ggu, m):
    length, features = n2.shape
    blocks = 4
    columns = ggu.shape[1] + m.shape[1]
    cut = pl.BlockSpec((length, features // blocks), lambda i: (0, i))
    return pl.pallas_call(
        mlp_grads_body,
        grid=(blocks,),
        out_shape=jax.ShapeDtypeStruct((features, columns), bf16),
        in_specs=[cut, cut, pl.BlockSpec(ggu.shape, lambda i: (0, 0)), pl.BlockSpec(m.shape, lambda i: (0, 0))],
        out_specs=pl.BlockSpec((features // blocks, columns), lambda i: (i, 0)),
        compiler_params=pltpu.CompilerParams(vmem_limit_bytes=VMEM_LIMIT),
        cost_estimate=pl.CostEstimate(flops=4 * 5 * 10**8, bytes_accessed=1000, transcendentals=0),
    )(n2, e, ggu, m)


def residual_body(own_ref, low_ref, res_ref, gf_ref, gain_ref, out_ref, ea_ref, ggain_ref):
    total = jnp.zeros((1, res_ref.shape[1]), f32)
    for at in range(0, res_ref.shape[0], HALO):
        rows = slice(at, at + HALO)
        grad = own_ref[rows, :] + low_ref[rows, :].astype(f32)
        res = res_ref[rows, :]
        scale = lax.rsqrt(jnp.mean(res * res, axis=1, keepdims=True) + eps)
        total = total + jnp.sum(grad * (res * scale), axis=0, keepdims=True)
        grad = grad * gain_ref[0:1, :]
        inner = jnp.mean(grad * res, axis=1, keepdims=True)
        grad = gf_ref[rows, :].astype(f32) + scale * grad - scale * scale * scale * res * inner
        out_ref[rows, :] = grad
        ea_ref[rows, :] = grad.astype(bf16)
    ggain_ref[...] = jnp.broadcast_to(total, ggain_ref.shape)


def residual_back(own, low, res, gf, gain):
    return call(
        residual_body, [(res.shape, f32), (res.shape, bf16), ((8, res.shape[1]), f32)], [], own, low, res, gf, gain
    )


def rms_scale(values):
    return lax.rsqrt(jnp.mean(values * values, axis=-1, keepdims=True) + eps)


def norm_back(inputs, inv_rms, grad_normed):
    inner_mean = jnp.mean(grad_normed * inputs, axis=-1, keepdims=True)
    return inv_rms * grad_normed - inv_rms * inv_rms * inv_rms * inputs * inner_mean


def padded_rows(block, rows):
    return jnp.pad(block, ((0, rows - block.shape[0]), (0, 0)))


def shards(
    hidden,
    teacher,
    positions,
    valid_mask,
    norm_gain,
    w_query,
    key_value_weight,
    w_gatein,
    w_bc,
    w_step,
    ssm_gain,
    mlp_gain,
    w_gateup,
    w_out_attn,
    w_out_ssm,
    w_down,
    conv_inner,
    conv_bc,
    head_params,
):
    ways = lax.axis_size(("fsdp", "ctx"))
    blocks = lax.axis_size("ctx")
    rows = norm_gain.shape[0]
    length = hidden.shape[1]
    heads = w_step.shape[1]
    width = heads * HEAD_SIZE
    attn_width = w_query.shape[1]
    kv_width = key_value_weight.shape[2]
    ff_local = w_down.shape[0]
    inner_rows = ssm_gain.shape[0]
    bc_rows = conv_bc.shape[1]
    qkv_width = attn_width + 2 * kv_width
    step_at = qkv_width + 2 * DS

    live_rows = valid_mask.reshape(length, 1).astype(f32)
    count_at = heads + 3 + 2 * KC
    first_shard = packed(
        w_query,
        key_value_weight.reshape(rows, 2 * kv_width),
        w_bc,
        w_step,
        jnp.stack([norm_gain, mlp_gain]),
        ssm_gain[None],
        conv_inner,
        conv_bc,
        valid_mask,
    )
    mlp_shard = jnp.concatenate([w_gateup.reshape(rows, 2 * ff_local), w_down.T], axis=1)
    mixer_shard = w_gatein.reshape(rows, 2 * width)
    out_shard = jnp.concatenate([w_out_attn, w_out_ssm], axis=0).T

    flat_in = hidden.reshape(length, MODEL_WIDTH)
    first_line = gathered_line(first_shard, False)
    before = passed_along(flat_in[length - 16 :], "ctx", 1)
    mixer_shard, first_line = tied(mixer_shard, first_line)
    mixer_line = gathered_line(mixer_shard)
    first_w = gathered_plane(first_line)
    mlp_w = lax.all_gather(mlp_shard, ("fsdp", "ctx"), axis=0, tiled=True)

    places = positions.reshape(1, length)
    place_rows = jnp.broadcast_to(places, (8, length))
    low_rows = jnp.broadcast_to(jnp.arange(length, dtype=jnp.int32)[None] - places, (8, length))
    half = HEAD_SIZE // 2
    frequency = rope_base ** (-2.0 * jnp.arange(half, dtype=f32) / HEAD_SIZE)
    angle = frequency[:, None] * places.astype(f32)
    cosine, sine = jnp.cos(angle), jnp.sin(angle)
    hp = jnp.pad(head_params.T, ((0, 16 - heads), (0, 125)))
    xt, scale_one = prepared(flat_in, before)
    xt, scale_one, cosine, sine, hp, first_w = lax.optimization_barrier((xt, scale_one, cosine, sine, hp, first_w))

    shape = (ways, rows, inner_rows, bc_rows, heads, step_at)
    par_inner, par_basis, param_rows, n1 = unpacked(shape, first_w, xt, scale_one)
    total_count = jnp.sum(param_rows[count_at]) * 16.0 + jnp.sum(param_rows[count_at + 1])
    gain_ssm = par_inner[:, heads + 2 : heads + 3]
    gain_two = param_rows[heads + 1 : heads + 2]
    gain_two_rows = jnp.broadcast_to(gain_two, (8, MODEL_WIDTH))

    first_lin = dot(first_w, n1, 0, 0)
    query, kv_own = roped(attn_width, first_lin, cosine, sine)
    mixer_line, kv_own = tied(mixer_line, kv_own)
    kv = [kv_own] + [passed_along(kv_own, "ctx", s) for s in range(1, blocks)]
    one, two = plane_first(mixer_line)
    one, two, out_shard, *kv = tied(one, two, out_shard, *kv)
    mixer_w = plane_second(one, two)
    out_line = gathered_line(out_shard)
    attn, log_total = attend(query, low_rows, kv)
    mixer_w, attn, out_line = tied(mixer_w, attn, out_line)
    out_halves = plane_first(out_line)
    mixer_lin = dot(mixer_w, n1, 0, 0)
    gate_z, u_in = mixer_lin[:width, HALO:], mixer_lin[width:]

    xs, b_flat, c_flat, b_side, c_side, dt, cum, cumt, pack = conv_forward(
        heads, qkv_width, u_in, first_lin, par_inner, par_basis, hp, place_rows
    )
    packs = [passed_along(pack, "ctx", s) for s in range(1, blocks)]
    xs, *out_halves = tied(xs, *out_halves)
    out_w = plane_second(*out_halves)
    gateup_w, down_w = mlp_w[:, : 2 * ff_local], mlp_w[:, 2 * ff_local :]
    ssm, states, squares = mix_forward(heads, xs, b_flat, c_side, dt, cum, cumt, hp, place_rows, gate_z, packs)
    inv_ssm = lax.rsqrt((squares + swapped(squares)) / (HS * HEAD_SIZE) + eps)
    gated = ssm * jax.nn.silu(gate_z)
    branches = jnp.concatenate([attn, (gated * gain_ssm * inv_ssm[0:1]).astype(bf16)], axis=0)
    part = dot(branches, out_w, 0, 1)
    residual = flat_in.astype(f32) + (part + swapped(part.astype(bf16)).astype(f32))

    scale_two = rms_scale(residual)
    normed_two = (residual * scale_two * gain_two).astype(bf16)
    gateup = dot(normed_two, gateup_w, 1, 0)
    hidden_mlp = (jax.nn.silu(gateup[:, :ff_local]) * gateup[:, ff_local:]).astype(bf16)
    gateup, hidden_mlp = tied(gateup.astype(bf16), hidden_mlp)
    gate_part, up_part = gateup[:, :ff_local].astype(f32), gateup[:, ff_local:].astype(f32)
    part = dot(hidden_mlp, down_w, 1, 1)
    final_rows = residual + (part + swapped(part.astype(bf16)).astype(f32))
    difference = (final_rows - teacher.reshape(length, MODEL_WIDTH).astype(f32)) * live_rows
    local_sq = jnp.sum(difference * difference)

    all_tokens = length * ways
    grad_final = difference * (all_tokens / total_count)
    grad_low = grad_final.astype(bf16)
    grad_hidden_mlp = dot(grad_low, down_w, 1, 0)
    sigma = jax.nn.sigmoid(gate_part)
    grad_gate = grad_hidden_mlp * up_part * sigma * (1.0 + gate_part * (1.0 - sigma))
    grad_up = grad_hidden_mlp * gate_part * sigma
    grad_gateup = jnp.concatenate([grad_gate, grad_up], axis=-1).astype(bf16)
    part = dot(grad_gateup, gateup_w, 1, 1)
    low_part, grad_gateup = tied(part.astype(bf16), grad_gateup)
    loss_lane = heads + 3 + 2 * KC + 3 * heads
    loss_row = jnp.where(lax.broadcasted_iota(jnp.int32, (8, 128), 1) == loss_lane, local_sq, 0.0)
    mlp_grads = mlp_weight_grads(normed_two, grad_low, grad_gateup, hidden_mlp)
    mlp_out = lax.psum_scatter(mlp_grads, "fsdp", scatter_dimension=0, tiled=True)
    grad_residual, grad_out, grad_gain_two = residual_back(part, swapped(low_part), residual, grad_low, gain_two_rows)

    grad_branches = dot(out_w, grad_out, 0, 1)
    grad_attn = grad_branches[:attn_width].astype(bf16)
    inner = jnp.sum(grad_branches[attn_width:] * gated * gain_ssm, axis=0, keepdims=True)
    inner = jnp.broadcast_to(inner, (8, length))
    inner = inner + swapped(inner)
    gy, grad_z, grad_gain_ssm, back_pack = gate_back(
        heads, grad_branches, ssm, gate_z, par_inner, inv_ssm, inner, c_flat, cum, place_rows
    )
    out_partial = dot(grad_out, branches, 0, 1).astype(bf16)
    grad_attn, out_partial, back_pack = tied(grad_attn, out_partial, back_pack)
    back_packs = [passed_along(back_pack, "ctx", -s) for s in range(1, blocks)]
    out_parts = scatter_first(out_partial)
    grad_query, *grad_kv = attend_back(query, low_rows, attn, log_total, grad_attn, cosine, sine, kv)
    back_packs, out_parts, grad_kv = lax.optimization_barrier((back_packs, out_parts, grad_kv))
    returned = [passed_along(grad_kv[s], "ctx", -s) for s in range(1, blocks)]
    out_parts = scatter_second(out_parts)
    grad_xs, grad_basis, grad_step, grad_head = mix_back(
        heads, step_at, gy, xs, b_flat, c_flat, b_side, c_side, dt, cum, cumt, first_lin, hp, place_rows, states, back_packs
    )
    *grad_kv, grad_xs = tied(grad_kv[0], *returned, grad_xs)
    early_w, grad_first = early_products(n1, grad_query, grad_z, cosine, sine, first_w, mixer_w, grad_kv)
    grad_xs, early_w = tied(grad_xs, early_w)
    early_parts = scatter_first(early_w)
    grad_conv, halo, grad_inner, grad_bc_taps = conv_back(
        heads, qkv_width, u_in, first_lin, grad_xs, grad_basis, par_inner, par_basis, place_rows
    )
    halo, mlp_out = tied(halo, mlp_out)
    mlp_out = lax.psum_scatter(mlp_out, "ctx", scatter_dimension=0, tiled=True)
    behind = passed_along(halo, "ctx", -1)
    behind, early_parts, out_parts = tied(behind, early_parts, out_parts)
    early_parts = scatter_second(early_parts)
    grad_late = joined(heads, grad_conv, behind, grad_step)
    late_w, low_normed = late_products(
        shape[1:-1], width, qkv_width, n1, xt, scale_one, grad_late, first_w, mixer_w, grad_first,
        grad_gain_two, grad_gain_ssm, grad_inner, grad_bc_taps, grad_head, loss_row,
    )
    gain_one = jnp.broadcast_to(param_rows[heads : heads + 1], (8, MODEL_WIDTH))
    late_w, low_normed, early_parts, out_parts = tied(late_w, low_normed, early_parts, out_parts)
    late_parts = scatter_first(late_w, heads)
    inner_kept, inner_other = halved([*early_parts, *out_parts])
    grad_input = input_grad(low_normed, swapped(low_normed), flat_in, grad_residual, gain_one)
    gateup_out = mlp_out[:, : 2 * ff_local].astype(f32).reshape(rows, 2, ff_local)
    down_out = mlp_out[:, 2 * ff_local :].astype(f32).T
    late_parts = scatter_second(late_parts, heads)
    late_parts, inner_other, grad_input, gateup_out, down_out = tied(late_parts, inner_other, grad_input, gateup_out, down_out)
    inner_parts = halved_on(inner_kept, inner_other)
    out_at = width + attn_width + 2 * kv_width
    query_out = inner_parts[:, width : width + attn_width]
    kv_out = inner_parts[:, width + attn_width : out_at].reshape(rows, 2, kv_width)
    attn_out = inner_parts[:, out_at : out_at + attn_width].T
    ssm_out = inner_parts[:, out_at + attn_width :].T
    late_out = scatter_third(late_parts)
    count_row = jnp.full((8, 128), total_count, f32)
    bc_out, norm_out, step_out, ssm_gain_out, mlp_gain_out, inner_out, basis_out, head_out, loss_value = finished(
        (rows, inner_rows, bc_rows, heads, width), late_out, swapped(late_out[:, width:]), count_row
    )
    return (
        final_rows.astype(bf16).reshape(1, length, MODEL_WIDTH),
        loss_value.reshape(()),
        grad_input.reshape(1, length, MODEL_WIDTH),
        norm_out.reshape(rows),
        query_out,
        kv_out,
        jnp.stack([inner_parts[:, :width], late_out[:, :width]], axis=1),
        bc_out,
        step_out,
        ssm_gain_out.reshape(inner_rows),
        mlp_gain_out.reshape(rows),
        gateup_out,
        attn_out,
        ssm_out,
        down_out,
        inner_out,
        basis_out,
        head_out,
    )


def solution(mesh):
    placed = (
        P("fsdp", "ctx", None),
        P("fsdp", "ctx", None),
        P("fsdp", "ctx"),
        P("fsdp", "ctx"),
        P(("fsdp", "ctx")),
        P(("fsdp", "ctx"), "tp"),
        P(("fsdp", "ctx"), None, "tp"),
        P(("fsdp", "ctx"), None, "tp"),
        P(("fsdp", "ctx"), None),
        P(("fsdp", "ctx"), "tp"),
        P(("tp", "fsdp", "ctx")),
        P(("fsdp", "ctx")),
        P(("fsdp", "ctx"), None, "tp"),
        P("tp", ("fsdp", "ctx")),
        P("tp", ("fsdp", "ctx")),
        P("tp", ("fsdp", "ctx")),
        P(None, ("tp", "fsdp", "ctx")),
        P(None, ("fsdp", "ctx")),
        P(None, "tp"),
    )
    return jax.shard_map(
        shards,
        mesh=mesh,
        in_specs=placed,
        out_specs=(
            P("fsdp", "ctx", None),
            P(),
            P("fsdp", "ctx", None),
            P(("fsdp", "ctx")),
            P(("fsdp", "ctx"), "tp"),
            P(("fsdp", "ctx"), None, "tp"),
            P(("fsdp", "ctx"), None, "tp"),
            P(("fsdp", "ctx"), None),
            P(("fsdp", "ctx"), "tp"),
            P(("tp", "fsdp", "ctx")),
            P(("fsdp", "ctx")),
            P(("fsdp", "ctx"), None, "tp"),
            P("tp", ("fsdp", "ctx")),
            P("tp", ("fsdp", "ctx")),
            P("tp", ("fsdp", "ctx")),
            P(None, ("tp", "fsdp", "ctx")),
            P(None, ("fsdp", "ctx")),
            P(None, "tp"),
        ),
        check_vma=False,
    )
```
